128 devices in a mesh: gx: 2 (over core), gy: 64 (over z, y, x).
Axes of the slice: x: 4, y: 4, z: 4, core: 2. Of those that a mesh axis runs over, the one named last changes fastest.
Arguments:
- embeddings: bfloat16 [24576, 1024], P(('gx', 'gy'))
- cluster: int32 [24576], P(('gx', 'gy')), may hold values from 0 to 1, as said below
Outputs:
- best_similarity: float32 [24576], P(('gx', 'gy'))
The draws below stay inside these ranges and needn't reach their ends.
Inputs may be any that keep to these rules, and one draw needn't show every extreme that they name: cluster modulo 2 is the owning index of gx; among the 192 documents of one device (aligned blocks) at most 144 have clusters with one owning index, and exactly 144 have one such owner in every block.
All inputs are finite; a program needn't handle non-finite values.
Results may differ from the reference program's by a relative error of at most 0.00048.
Values may be sent and summed in bfloat16 or wider, within the bound.
A program may use at most 128 MiB of HBM per device.

```python
import jax
import jax.numpy as jnp
from jax import lax

D = 1024
ROWS_DEV = 192
CL_OWN = 1
NDOC = 24576
NCLUST = 2
SLOT = 144
N_GX = 2
N_GY = 64


def cluster_law(key):
    subkeys = jax.random.split(jax.random.fold_in(key, 11), 3)
    blocks = NDOC // ROWS_DEV
    slot_rows = 3 * ROWS_DEV // (2 * N_GX)
    hottest = jax.random.randint(subkeys[0], (N_GY,), 0, N_GX)
    block_hot = jnp.tile(hottest, blocks // N_GY)
    within = jnp.arange(ROWS_DEV)
    others = (within - slot_rows) % (N_GX - 1) + 1
    offsets = jnp.where(within < slot_rows, 0, others)
    owners = (block_hot[:, None] + offsets[None, :]) % N_GX
    shuffles = jax.vmap(lambda sub: jax.random.permutation(sub, ROWS_DEV))(jax.random.split(subkeys[1], blocks))
    owners = jnp.take_along_axis(owners, shuffles, axis=1)
    inner = jax.random.randint(subkeys[2], (blocks, ROWS_DEV), 0, CL_OWN)
    return (owners + N_GX * inner).reshape(NDOC).astype(jnp.int32)


def draw_cluster(key, part):
    return cluster_law(key)


def draw_embeddings(key, part):
    labels = cluster_law(key)
    key = jax.random.fold_in(key, 5)
    subkeys = jax.random.split(key, 3)
    centers = jax.random.normal(subkeys[0], (NCLUST, D), jnp.float32)
    tightness = jax.random.uniform(subkeys[1], (NCLUST,), jnp.float32, 0.3, 1.2)
    noise = jax.random.normal(subkeys[2], (NDOC, D), jnp.float32)
    values = centers[labels] * tightness[labels][:, None] + noise
    return values.astype(jnp.bfloat16)


def setup_inputs(seed: int = 0) -> dict:
    seeds = jax.random.split(jax.random.key(seed), 3)
    return {
        "embeddings": draw_embeddings(jax.random.fold_in(seeds[2], 71), 0),
        "cluster": draw_cluster(jax.random.fold_in(seeds[2], 71), 0),
    }


eps = 1e-06

def reference(embeddings, cluster):
    values = embeddings.astype(jnp.float32)
    normed = (values * lax.rsqrt(lax.optimization_barrier(jnp.sum(values * values, axis=1, keepdims=True)) + eps)).astype(jnp.bfloat16)
    owners = (cluster % N_GX).astype(jnp.int32)
    block_rows = SLOT * N_GX
    capacity = block_rows * N_GY
    order = jnp.argsort(owners, stable=True).astype(jnp.int32)
    counts = lax.optimization_barrier(jnp.sum((owners[:, None] == jnp.arange(N_GX, dtype=jnp.int32)[None, :]).astype(jnp.int32), axis=0)).astype(jnp.int32)
    starts = (jnp.cumsum(counts) - counts).astype(jnp.int32)
    padded = jnp.concatenate([order, jnp.full((capacity,), NDOC, jnp.int32)])

    def owner_block(group):
        members = lax.dynamic_slice_in_dim(padded, starts[group].astype(jnp.int32), capacity)
        filled = jnp.arange(capacity, dtype=jnp.int32) < counts[group]
        members = jnp.where(filled, members, NDOC).astype(jnp.int32)
        clamped = jnp.minimum(members, NDOC - 1)
        member_rows = normed[clamped]
        member_ids = jnp.where(filled, cluster[clamped], -1).astype(jnp.int32)

        def row_block(index):
            begin = (index * block_rows).astype(jnp.int32)
            left_rows = lax.dynamic_slice_in_dim(member_rows, begin, block_rows)
            left_ids = lax.dynamic_slice_in_dim(member_ids, begin, block_rows)
            left_members = lax.dynamic_slice_in_dim(members, begin, block_rows)
            products = jnp.dot(left_rows, member_rows.T, preferred_element_type=jnp.float32)
            matched = (left_ids[:, None] == member_ids[None, :]) & (member_ids[None, :] >= 0) & (left_members[:, None] != members[None, :])
            return lax.optimization_barrier(jnp.max(jnp.where(matched, products, jnp.float32(-1.0)), axis=1))
        best = lax.map(row_block, jnp.arange(N_GY, dtype=jnp.int32)).reshape(capacity)
        return (best, members)
    best, members = lax.map(owner_block, jnp.arange(N_GX, dtype=jnp.int32))
    result = jnp.full((NDOC,), -1.0, jnp.float32)
    return result.at[members.reshape(-1)].set(best.reshape(-1), mode='drop')
```

```python
import functools

import jax
import jax.numpy as jnp
from jax import lax
from jax.experimental import pallas as pl
from jax.experimental.pallas import tpu as pltpu
from jax.sharding import PartitionSpec as P

EPS = 1e-06
SLOTS = (
    (0, 0, 0),
    (0, 1, 0),
    (0, 0, 3),
    (0, 0, 1),
    (3, 0, 0),
    (1, 1, 0),
    (0, 3, 1),
    (0, 0, 2),
    (2, 0, 0),
    (1, 2, 0),
    (0, 3, 2),
    (2, 2, 0),
)
STEPS = ((1, 0, 0), (3, 0, 0), (0, 1, 0), (0, 3, 0), (0, 0, 1), (0, 0, 3))
PARTS = ((0, 64), (64, 64), (128, 64))
TREES = (
    {1: (0, 2), 2: (0, 5), 3: (0, 4), 4: (0, 1), 5: (1, 0), 6: (3, 3), 7: (3, 4), 8: (4, 1), 9: (5, 2), 10: (7, 3), 11: (9, 0)},
    {1: (0, 2), 2: (0, 5), 3: (0, 4), 4: (0, 1), 5: (1, 0), 6: (3, 3), 7: (3, 4), 8: (4, 1), 9: (5, 2), 10: (7, 3), 11: (9, 0)},
    {1: (0, 2), 2: (0, 5), 3: (0, 4), 4: (0, 1), 5: (1, 0), 6: (3, 3), 7: (2, 5), 8: (4, 1), 9: (5, 2), 10: (6, 4), 11: (9, 0)},
)
CHILDREN = (
    {0: (1, 3, 4, 2), 1: (5,), 3: (7, 6), 4: (8,), 5: (9,), 7: (10,), 9: (11,)},
    {0: (1, 3, 4, 2), 1: (5,), 3: (7, 6), 4: (8,), 5: (9,), 7: (10,), 9: (11,)},
    {0: (1, 3, 2, 4), 1: (5,), 2: (7,), 3: (6,), 4: (8,), 5: (9,), 6: (10,), 9: (11,)},
)
ROOT_ORDER = ((0, 1), (0, 3), (0, 4), (2, 2), (0, 2), (1, 1), (1, 3), (1, 4), (1, 2), (2, 1), (2, 3), (2, 4))
PAIRED = frozenset((0, 1, 2, 3, 4, 5, 6, 7, 8))
SEGMENTS = (
    (
        (('i', 0), ('d', 0)),
        ((0, 0),),
    ),
    (
        (('n', 0), ('f', 1, 0), ('f', 2, 2), ('f', 3, 0), ('f', 4, 0), ('f', 1, 1), ('f', 2, 0), ('f', 3, 1), ('f', 4, 1), ('f', 5, 0), ('f', 6, 0), ('f', 1, 2), ('f', 2, 1), ('f', 3, 2), ('f', 4, 2), ('i', 1)),
        ((1, 0),),
    ),
    (
        (('n', 1), ('f', 5, 1), ('f', 6, 1), ('i', 2)),
        ((2, 0),),
    ),
    (
        (('d', 1),),
        ((2, 1),),
    ),
    (
        (('n', 2), ('i', 3)),
        ((3, 1),),
    ),
    (
        (('d', 2),),
        ((3, 2),),
    ),
    (
        (('n', 3), ('f', 7, 0), ('f', 7, 2), ('f', 8, 0), ('f', 9, 0), ('i', 4)),
        ((4, 0),),
    ),
    (
        (('f', 5, 2), ('f', 6, 2)),
        ((4, 1), (4, 2)),
    ),
    (
        (('d', 3),),
        ((4, 3),),
    ),
    (
        (('n', 4), ('i', 5)),
        ((5, 2), (5, 3)),
    ),
    (
        (('f', 7, 1), ('f', 8, 1), ('f', 9, 1), ('d', 4)),
        ((5, 4),),
    ),
    (
        (('n', 5), ('f', 10, 0), ('f', 11, 0), ('i', 6)),
        ((6, 1), (6, 2), (6, 4)),
    ),
    (
        (('d', 5),),
        ((6, 5),),
    ),
    (
        (('n', 6), ('i', 7)),
        ((7, 4),),
    ),
    (
        (('f', 8, 2), ('f', 9, 2), ('f', 10, 2)),
        ((7, 5),),
    ),
    (
        (('n', 7), ('f', 10, 1), ('f', 11, 1), ('i', 8)),
        ((8, 0), (8, 2), (8, 5)),
    ),
    (
        (('d', 6),),
        ((8, 6),),
    ),
    (
        (('d', 7),),
        ((8, 7),),
    ),
    (
        (('n', 8), ('i', 9)),
        ((9, 0), (9, 2)),
    ),
    (
        (('f', 11, 2),),
        ((9, 4), (9, 6), (9, 7)),
    ),
    (
        (('n', 9), ('i', 10)),
        ((10, 1), (10, 4)),
    ),
    (
        (('d', 8),),
        ((10, 8),),
    ),
    (
        (('n', 10), ('i', 11)),
        ((11, 2), (11, 6), (11, 7), (11, 8)),
    ),
    (
        (('n', 11),),
        (),
    ),
)

MESH = pl.DeviceIdType.MESH
NSLOT = len(SLOTS)
NPART = len(PARTS)
NSEG = len(SEGMENTS)
NITEM = sum(len(items) for _, items in SEGMENTS)


LEFTS = [p for _, items in SEGMENTS for p, _ in items]
RIGHTS = [q for _, items in SEGMENTS for _, q in items]


def packed(digits, index):
    word = jnp.int32(0)
    for k in range(0, len(digits), 8):
        value = sum(d << (4 * j) for j, d in enumerate(digits[k : k + 8]))
        word = jnp.where(index // 8 == k // 8, jnp.int32(value - (1 << 32) if value >> 31 else value), word)
    return lax.shift_right_logical(word, 4 * (index % 8)) & 15


def start_of(seg):
    first = jnp.int32(0)
    for k, (_, items) in enumerate(SEGMENTS):
        first = first + jnp.where(seg > k, len(items), 0)
    return first


def shifted(place, offset, sign):
    z, y, x = place // 16, (place // 4) % 4, place % 4
    dz, dy, dx = [(4 + sign * v) % 4 for v in offset]
    return ((z + dz) % 4) * 16 + ((y + dy) % 4) * 4 + (x + dx) % 4


def kernel(
    x_ref, c_ref, o_ref, rows, ids, ids_out, id_row, id_col, left_best, best, back, back_out,
    row_send, row_recv, pair_send, pair_recv, id_send, id_recv, back_send, back_recv,
):
    core = lax.axis_index("gx")
    place = lax.axis_index("gy")
    half = x_ref.shape[0]
    whole = 2 * half
    mine = pl.ds(pl.multiple_of(core * half, half), half)

    def device(c, chip):
        return (c, chip)

    greet = set()
    for slot in range(1, NSLOT):
        for sign in (1, -1):
            greet.add(tuple((sign * v) % 4 for v in SLOTS[slot]))
    for axis in range(3):
        for step in (1, 3):
            greet.add(tuple(step if k == axis else 0 for k in range(3)))
    greet = sorted(greet)
    barrier = pltpu.get_barrier_semaphore()
    for offset in greet:
        chip = shifted(place, offset, 1)
        for c in range(2):
            pl.semaphore_signal(barrier, inc=1, device_id=device(c, chip), device_id_type=MESH)
    pl.semaphore_signal(barrier, inc=1, device_id=device(1 - core, place), device_id_type=MESH)

    for begin, size in PARTS:
        values = x_ref[begin : begin + size, :].astype(jnp.float32)
        total = jnp.sum(values * values, axis=1, keepdims=True)
        rows[0, core, begin : begin + size, :] = (values * lax.rsqrt(total + EPS)).astype(jnp.bfloat16)
    lane = lax.broadcasted_iota(jnp.int32, (1, whole), 1)
    cluster = c_ref[...].astype(jnp.float32)
    twice = jnp.concatenate([cluster, cluster], axis=1)
    own_ids = jnp.where((lane >= half) == (core == 1), twice, -1.0)
    ids_out[...] = own_ids
    ids[0, core] = own_ids
    best[...] = jnp.full(best.shape, -1.0, jnp.float32)

    pl.semaphore_wait(barrier, 2 * len(greet) + 1)

    def id_copy(slot, c, sender):
        return pltpu.make_async_remote_copy(
            src_ref=ids_out,
            dst_ref=ids.at[slot, sender],
            send_sem=id_send.at[slot, c],
            recv_sem=id_recv.at[slot, sender],
            device_id=device(c, shifted(place, SLOTS[slot], -1)),
            device_id_type=MESH,
        )

    def row_copy(part, parent, slot, axis_step):
        begin, size = PARTS[part]
        return pltpu.make_async_remote_copy(
            src_ref=rows.at[parent, core, pl.ds(begin, size)],
            dst_ref=rows.at[slot, core, pl.ds(begin, size)],
            send_sem=row_send.at[slot, part],
            recv_sem=row_recv.at[slot, part],
            device_id=device(core, shifted(place, STEPS[axis_step], -1)),
            device_id_type=MESH,
        )

    def pair_copy(slot, part, sender):
        begin, size = PARTS[part]
        return pltpu.make_async_remote_copy(
            src_ref=rows.at[slot, sender, pl.ds(begin, size)],
            dst_ref=rows.at[slot, sender, pl.ds(begin, size)],
            send_sem=pair_send.at[slot, part],
            recv_sem=pair_recv.at[slot, part],
            device_id=device(1 - core, place),
            device_id_type=MESH,
        )

    def row_copy_to(part, slot):
        parent, axis_step = TREES[part][slot]
        return row_copy(part, parent, slot, axis_step)

    for part, slot in ROOT_ORDER:
        row_copy_to(part, slot).start()
    sibling_ids = pltpu.make_async_remote_copy(
        src_ref=ids_out,
        dst_ref=ids.at[0, core],
        send_sem=id_send.at[0, 0],
        recv_sem=id_recv.at[0, 0],
        device_id=device(1 - core, place),
        device_id_type=MESH,
    )
    sibling_ids.start()
    for part in range(NPART):
        pair_copy(0, part, core).start()
    for slot in range(1, NSLOT):
        for c in range(2):
            id_copy(slot, c, core).start()

    def forward(slot, part):
        row_copy_to(part, slot).wait_recv()
        for child in CHILDREN[part].get(slot, ()):
            row_copy_to(part, child).start()
        if slot in PAIRED:
            pair_copy(slot, part, core).start()

    def take_pair(slot):
        for part in range(NPART):
            pair_copy(slot, part, 1 - core).wait_recv()

    def take_ids(slot):
        if slot == 0:
            sibling_ids.wait_recv()
        else:
            for c in range(2):
                id_copy(slot, c, c).wait_recv()
        id_row[slot] = jnp.maximum(ids[slot, 0], ids[slot, 1])

    def begin_left(slot):
        take_ids(slot)
        id_col[...] = jnp.broadcast_to(id_row[slot], (128, whole)).T
        left_best[...] = jnp.full(left_best.shape, -1.0, jnp.float32)

    def end_left(slot):
        turned = left_best[...].T.reshape(128 // 8, 8, whole)
        best[slot] = jnp.maximum(best[slot], jnp.max(turned, axis=0))

    def multiply(index, carry):
        p, q = packed(LEFTS, index), packed(RIGHTS, index)
        right = rows[q].reshape(whole, rows.shape[-1])
        products = lax.dot_general(
            rows[p, core], right, (((1,), (1,)), ((), ())), preferred_element_type=jnp.float32
        )
        left_id = id_col[mine, :]
        row = lax.broadcasted_iota(jnp.int32, (half, 128), 0) + core * half
        column = lax.broadcasted_iota(jnp.int32, (half, 128), 1) + jnp.where(p == q, 0, 2 * whole)
        row_best = left_best[mine, :]
        for k in range(whole // 128):
            lanes = slice(128 * k, 128 * k + 128)
            allowed = (left_id == id_row[q, :, lanes]) & (row != column + 128 * k)
            masked = jnp.where(allowed, products[:, lanes], -1.0)
            row_best = jnp.maximum(row_best, masked)
            best[q, :, lanes] = jnp.maximum(
                best[q, :, lanes], jnp.max(masked.reshape(half // 8, 8, 128), axis=0)
            )
        left_best[mine, :] = row_best
        return carry

    actions = {"f": forward, "d": take_pair, "i": begin_left, "n": end_left}

    def segment(seg, carry):
        for k, (events, _) in enumerate(SEGMENTS):
            if events:

                @pl.when(seg == k)
                def _():
                    for name, *where in events:
                        actions[name](*where)

        return lax.fori_loop(start_of(seg), start_of(seg + 1), multiply, carry)

    lax.fori_loop(0, NSEG, segment, 0)

    def back_copy(slot, c, sender):
        return pltpu.make_async_remote_copy(
            src_ref=back_out.at[slot],
            dst_ref=back.at[slot, sender],
            send_sem=back_send.at[slot, c],
            recv_sem=back_recv.at[slot, sender],
            device_id=device(c, shifted(place, SLOTS[slot], 1)),
            device_id_type=MESH,
        )

    sibling_back = pltpu.make_async_remote_copy(
        src_ref=back_out.at[0],
        dst_ref=back.at[0, core],
        send_sem=back_send.at[0, 0],
        recv_sem=back_recv.at[0, 0],
        device_id=device(1 - core, place),
        device_id_type=MESH,
    )
    for slot in range(NSLOT):
        back_out[slot] = jnp.max(best[slot], axis=0, keepdims=True)
        if slot == 0:
            sibling_back.start()
        else:
            for c in range(2):
                back_copy(slot, c, core).start()
    back[0, core] = back_out[0]
    sibling_back.wait_recv()
    for slot in range(1, NSLOT):
        for c in range(2):
            back_copy(slot, c, c).wait_recv()
    result = jnp.max(back[...].reshape(2 * NSLOT, 1, whole), axis=0)
    o_ref[...] = jnp.where(core == 0, result[:, :half], result[:, half:])

    for part in range(NPART):
        for slot in range(1, NSLOT):
            row_copy_to(part, slot).wait_send()
        for slot in sorted(PAIRED):
            pair_copy(slot, part, core).wait_send()
    sibling_ids.wait_send()
    sibling_back.wait_send()
    for slot in range(1, NSLOT):
        for c in range(2):
            id_copy(slot, c, core).wait_send()
            back_copy(slot, c, core).wait_send()


def local(embeddings, cluster):
    half, width = embeddings.shape
    whole = 2 * half
    best = pl.pallas_call(
        kernel,
        out_shape=jax.ShapeDtypeStruct((1, half), jnp.float32),
        in_specs=[pl.BlockSpec(memory_space=pltpu.VMEM)] * 2,
        out_specs=pl.BlockSpec(memory_space=pltpu.VMEM),
        scratch_shapes=[
            pltpu.VMEM((NSLOT, 2, half, width), jnp.bfloat16),
            pltpu.VMEM((NSLOT, 2, 1, whole), jnp.float32),
            pltpu.VMEM((1, whole), jnp.float32),
            pltpu.VMEM((NSLOT, 1, whole), jnp.float32),
            pltpu.VMEM((whole, 128), jnp.float32),
            pltpu.VMEM((whole, 128), jnp.float32),
            pltpu.VMEM((NSLOT, 8, whole), jnp.float32),
            pltpu.VMEM((NSLOT, 2, 1, whole), jnp.float32),
            pltpu.VMEM((NSLOT, 1, whole), jnp.float32),
            pltpu.SemaphoreType.DMA((NSLOT, NPART)),
            pltpu.SemaphoreType.DMA((NSLOT, NPART)),
            pltpu.SemaphoreType.DMA((NSLOT, NPART)),
            pltpu.SemaphoreType.DMA((NSLOT, NPART)),
            pltpu.SemaphoreType.DMA((NSLOT, 2)),
            pltpu.SemaphoreType.DMA((NSLOT, 2)),
            pltpu.SemaphoreType.DMA((NSLOT, 2)),
            pltpu.SemaphoreType.DMA((NSLOT, 2)),
        ],
        compiler_params=pltpu.CompilerParams(
            collective_id=0, has_side_effects=True, vmem_limit_bytes=40 * 1024 * 1024
        ),
        cost_estimate=pl.CostEstimate(
            flops=2 * NITEM * half * whole * width, bytes_accessed=2 * half * width, transcendentals=half
        ),
    )(embeddings, cluster.reshape(1, half))
    return best.reshape(half)


def solution(mesh):
    return jax.shard_map(
        local,
        mesh=mesh,
        in_specs=(P(("gx", "gy"), None), P(("gx", "gy"))),
        out_specs=P(("gx", "gy")),
        check_vma=False,
    )
```

```python
import functools

import jax
import jax.numpy as jnp
from jax import lax
from jax.experimental import pallas as pl
from jax.experimental.pallas import tpu as pltpu
from jax.sharding import PartitionSpec as P

EPS = 1e-06
SLOTS = (
    (0, 0, 0),
    (0, 1, 0),
    (0, 0, 3),
    (0, 0, 1),
    (3, 0, 0),
    (1, 1, 0),
    (0, 3, 1),
    (0, 0, 2),
    (2, 0, 0),
    (1, 2, 0),
    (0, 3, 2),
    (2, 2, 0),
)
STEPS = ((1, 0, 0), (3, 0, 0), (0, 1, 0), (0, 3, 0), (0, 0, 1), (0, 0, 3))
PARTS = ((0, 64), (64, 64), (128, 64))
TREES = (
    {1: (0, 2), 2: (0, 5), 3: (0, 4), 4: (0, 1), 5: (1, 0), 6: (3, 3), 7: (3, 4), 8: (4, 1), 9: (5, 2), 10: (7, 3), 11: (9, 0)},
    {1: (0, 2), 2: (0, 5), 3: (0, 4), 4: (0, 1), 5: (1, 0), 6: (3, 3), 7: (3, 4), 8: (4, 1), 9: (5, 2), 10: (7, 3), 11: (9, 0)},
    {1: (0, 2), 2: (0, 5), 3: (0, 4), 4: (0, 1), 5: (1, 0), 6: (3, 3), 7: (2, 5), 8: (4, 1), 9: (5, 2), 10: (6, 4), 11: (9, 0)},
)
CHILDREN = (
    {0: (1, 3, 4, 2), 1: (5,), 3: (7, 6), 4: (8,), 5: (9,), 7: (10,), 9: (11,)},
    {0: (1, 3, 4, 2), 1: (5,), 3: (7, 6), 4: (8,), 5: (9,), 7: (10,), 9: (11,)},
    {0: (1, 3, 2, 4), 1: (5,), 2: (7,), 3: (6,), 4: (8,), 5: (9,), 6: (10,), 9: (11,)},
)
ROOT_ORDER = ((0, 1), (0, 3), (0, 4), (2, 2), (0, 2), (1, 1), (1, 3), (1, 4), (1, 2), (2, 1), (2, 3), (2, 4))
PAIRED = frozenset((0, 1, 2, 3, 4, 5, 6, 7, 8))
SEGMENTS = (
    (
        (('i', 0), ('d', 0)),
        ((0, 0),),
    ),
    (
        (('n', 0), ('f', 1, 0), ('f', 2, 2), ('f', 3, 0), ('f', 4, 0), ('f', 1, 1), ('f', 2, 0), ('f', 3, 1), ('f', 4, 1), ('f', 5, 0), ('f', 6, 0), ('f', 1, 2), ('f', 2, 1), ('f', 3, 2), ('f', 4, 2), ('i', 1)),
        ((1, 0),),
    ),
    (
        (('n', 1), ('f', 5, 1), ('f', 6, 1), ('i', 2)),
        ((2, 0),),
    ),
    (
        (('d', 1),),
        ((2, 1),),
    ),
    (
        (('n', 2), ('i', 3)),
        ((3, 1),),
    ),
    (
        (('d', 2),),
        ((3, 2),),
    ),
    (
        (('n', 3), ('f', 7, 0), ('f', 7, 2), ('f', 8, 0), ('f', 9, 0), ('i', 4)),
        ((4, 0),),
    ),
    (
        (('f', 5, 2), ('f', 6, 2)),
        ((4, 1), (4, 2)),
    ),
    (
        (('d', 3),),
        ((4, 3),),
    ),
    (
        (('n', 4), ('i', 5)),
        ((5, 2), (5, 3)),
    ),
    (
        (('f', 7, 1), ('f', 8, 1), ('f', 9, 1), ('d', 4)),
        ((5, 4),),
    ),
    (
        (('n', 5), ('f', 10, 0), ('f', 11, 0), ('i', 6)),
        ((6, 1), (6, 2), (6, 4)),
    ),
    (
        (('d', 5),),
        ((6, 5),),
    ),
    (
        (('n', 6), ('i', 7)),
        ((7, 4),),
    ),
    (
        (('f', 8, 2), ('f', 9, 2), ('f', 10, 2)),
        ((7, 5),),
    ),
    (
        (('n', 7), ('f', 10, 1), ('f', 11, 1), ('i', 8)),
        ((8, 0), (8, 2), (8, 5)),
    ),
    (
        (('d', 6),),
        ((8, 6),),
    ),
    (
        (('d', 7),),
        ((8, 7),),
    ),
    (
        (('n', 8), ('i', 9)),
        ((9, 0), (9, 2)),
    ),
    (
        (('f', 11, 2),),
        ((9, 4), (9, 6), (9, 7)),
    ),
    (
        (('n', 9), ('i', 10)),
        ((10, 1), (10, 4)),
    ),
    (
        (('d', 8),),
        ((10, 8),),
    ),
    (
        (('n', 10), ('i', 11)),
        ((11, 2), (11, 6), (11, 7), (11, 8)),
    ),
    (
        (('n', 11),),
        (),
    ),
)

MESH = pl.DeviceIdType.MESH
NSLOT = len(SLOTS)
NPART = len(PARTS)
NSEG = len(SEGMENTS)
NITEM = sum(len(items) for _, items in SEGMENTS)


LEFTS = [p for _, items in SEGMENTS for p, _ in items]
RIGHTS = [q for _, items in SEGMENTS for _, q in items]


def packed(digits, index):
    word = jnp.int32(0)
    for k in range(0, len(digits), 8):
        value = sum(d << (4 * j) for j, d in enumerate(digits[k : k + 8]))
        word = jnp.where(index // 8 == k // 8, jnp.int32(value - (1 << 32) if value >> 31 else value), word)
    return lax.shift_right_logical(word, 4 * (index % 8)) & 15


def start_of(seg):
    first = jnp.int32(0)
    for k, (_, items) in enumerate(SEGMENTS):
        first = first + jnp.where(seg > k, len(items), 0)
    return first


def shifted(place, offset, sign):
    z, y, x = place // 16, (place // 4) % 4, place % 4
    dz, dy, dx = [(4 + sign * v) % 4 for v in offset]
    return ((z + dz) % 4) * 16 + ((y + dy) % 4) * 4 + (x + dx) % 4


def gather(
    x_ref, c_ref, rows, id_row, ids, ids_out, row_send, row_recv, pair_send, pair_recv, id_send, id_recv
):
    core = lax.axis_index("gx")
    place = lax.axis_index("gy")
    half = x_ref.shape[0]
    whole = 2 * half
    mine = pl.ds(pl.multiple_of(core * half, half), half)

    def device(c, chip):
        return (c, chip)

    greet = set()
    for slot in range(1, NSLOT):
        for sign in (1, -1):
            greet.add(tuple((sign * v) % 4 for v in SLOTS[slot]))
    for axis in range(3):
        for step in (1, 3):
            greet.add(tuple(step if k == axis else 0 for k in range(3)))
    greet = sorted(greet)
    barrier = pltpu.get_barrier_semaphore()
    for offset in greet:
        chip = shifted(place, offset, 1)
        for c in range(2):
            pl.semaphore_signal(barrier, inc=1, device_id=device(c, chip), device_id_type=MESH)
    pl.semaphore_signal(barrier, inc=1, device_id=device(1 - core, place), device_id_type=MESH)

    for begin, size in PARTS:
        values = x_ref[begin : begin + size, :].astype(jnp.float32)
        total = jnp.sum(values * values, axis=1, keepdims=True)
        rows[0, core, begin : begin + size, :] = (values * lax.rsqrt(total + EPS)).astype(jnp.bfloat16)
    lane = lax.broadcasted_iota(jnp.int32, (1, whole), 1)
    cluster = c_ref[...].astype(jnp.float32)
    twice = jnp.concatenate([cluster, cluster], axis=1)
    own_ids = jnp.where((lane >= half) == (core == 1), twice, -1.0)
    ids_out[...] = own_ids
    ids[0, core] = own_ids

    pl.semaphore_wait(barrier, 2 * len(greet) + 1)

    def id_copy(slot, c, sender):
        return pltpu.make_async_remote_copy(
            src_ref=ids_out,
            dst_ref=ids.at[slot, sender],
            send_sem=id_send.at[slot, c],
            recv_sem=id_recv.at[slot, sender],
            device_id=device(c, shifted(place, SLOTS[slot], -1)),
            device_id_type=MESH,
        )

    def row_copy(part, parent, slot, axis_step):
        begin, size = PARTS[part]
        return pltpu.make_async_remote_copy(
            src_ref=rows.at[parent, core, pl.ds(begin, size)],
            dst_ref=rows.at[slot, core, pl.ds(begin, size)],
            send_sem=row_send.at[slot, part],
            recv_sem=row_recv.at[slot, part],
            device_id=device(core, shifted(place, STEPS[axis_step], -1)),
            device_id_type=MESH,
        )

    def pair_copy(slot, part, sender):
        begin, size = PARTS[part]
        return pltpu.make_async_remote_copy(
            src_ref=rows.at[slot, sender, pl.ds(begin, size)],
            dst_ref=rows.at[slot, sender, pl.ds(begin, size)],
            send_sem=pair_send.at[slot, part],
            recv_sem=pair_recv.at[slot, part],
            device_id=device(1 - core, place),
            device_id_type=MESH,
        )

    def row_copy_to(part, slot):
        parent, axis_step = TREES[part][slot]
        return row_copy(part, parent, slot, axis_step)

    for part, slot in ROOT_ORDER:
        row_copy_to(part, slot).start()
    sibling_ids = pltpu.make_async_remote_copy(
        src_ref=ids_out,
        dst_ref=ids.at[0, core],
        send_sem=id_send.at[0, 0],
        recv_sem=id_recv.at[0, 0],
        device_id=device(1 - core, place),
        device_id_type=MESH,
    )
    sibling_ids.start()
    for part in range(NPART):
        pair_copy(0, part, core).start()
    for slot in range(1, NSLOT):
        for c in range(2):
            id_copy(slot, c, core).start()

    def forward(slot, part):
        row_copy_to(part, slot).wait_recv()
        for child in CHILDREN[part].get(slot, ()):
            row_copy_to(part, child).start()
        if slot in PAIRED:
            pair_copy(slot, part, core).start()

    def take_pair(slot):
        for part in range(NPART):
            pair_copy(slot, part, 1 - core).wait_recv()

    def take_ids(slot):
        if slot == 0:
            sibling_ids.wait_recv()
        else:
            for c in range(2):
                id_copy(slot, c, c).wait_recv()
        id_row[slot] = jnp.maximum(ids[slot, 0], ids[slot, 1])

    for events, _ in SEGMENTS:
        for name, *where in events:
            if name == "f":
                forward(*where)
    for slot in range(NSLOT):
        take_ids(slot)
        if slot in PAIRED:
            take_pair(slot)
    for part in range(NPART):
        for slot in range(1, NSLOT):
            row_copy_to(part, slot).wait_send()
        for slot in sorted(PAIRED):
            pair_copy(slot, part, core).wait_send()
    sibling_ids.wait_send()
    for slot in range(1, NSLOT):
        for c in range(2):
            id_copy(slot, c, core).wait_send()


def product(rows, id_row, best, id_col, left_best):
    core = lax.axis_index("gx")
    half = rows.shape[2]
    whole = 2 * half
    mine = pl.ds(pl.multiple_of(core * half, half), half)
    best[...] = jnp.full(best.shape, -1.0, jnp.float32)

    def begin_left(slot):
        id_col[...] = jnp.broadcast_to(id_row[slot], (128, whole)).T
        left_best[...] = jnp.full(left_best.shape, -1.0, jnp.float32)

    def end_left(slot):
        turned = left_best[...].T.reshape(128 // 8, 8, whole)
        best[slot] = jnp.maximum(best[slot], jnp.max(turned, axis=0))

    def multiply(index, carry):
        p, q = packed(LEFTS, index), packed(RIGHTS, index)
        right = rows[q].reshape(whole, rows.shape[-1])
        products = lax.dot_general(
            rows[p, core], right, (((1,), (1,)), ((), ())), preferred_element_type=jnp.float32
        )
        left_id = id_col[mine, :]
        row = lax.broadcasted_iota(jnp.int32, (half, 128), 0) + core * half
        column = lax.broadcasted_iota(jnp.int32, (half, 128), 1) + jnp.where(p == q, 0, 2 * whole)
        row_best = left_best[mine, :]
        for k in range(whole // 128):
            lanes = slice(128 * k, 128 * k + 128)
            allowed = (left_id == id_row[q, :, lanes]) & (row != column + 128 * k)
            masked = jnp.where(allowed, products[:, lanes], -1.0)
            row_best = jnp.maximum(row_best, masked)
            best[q, :, lanes] = jnp.maximum(
                best[q, :, lanes], jnp.max(masked.reshape(half // 8, 8, 128), axis=0)
            )
        left_best[mine, :] = row_best
        return carry

    actions = {"i": begin_left, "n": end_left}

    def segment(seg, carry):
        for k, (events, _) in enumerate(SEGMENTS):
            if any(name in actions for name, *_ in events):

                @pl.when(seg == k)
                def _():
                    for name, *where in events:
                        if name in actions:
                            actions[name](*where)

        return lax.fori_loop(start_of(seg), start_of(seg + 1), multiply, carry)

    lax.fori_loop(0, NSEG, segment, 0)


def give_back(best, o_ref, back, back_out, back_send, back_recv):
    core = lax.axis_index("gx")
    place = lax.axis_index("gy")
    half = o_ref.shape[1]
    whole = 2 * half

    def device(c, chip):
        return (c, chip)

    barrier = pltpu.get_barrier_semaphore()
    for slot in range(1, NSLOT):
        chip = shifted(place, SLOTS[slot], -1)
        for c in range(2):
            pl.semaphore_signal(barrier, inc=1, device_id=device(c, chip), device_id_type=MESH)
    pl.semaphore_signal(barrier, inc=1, device_id=device(1 - core, place), device_id_type=MESH)
    pl.semaphore_wait(barrier, 2 * NSLOT - 1)
    def back_copy(slot, c, sender):
        return pltpu.make_async_remote_copy(
            src_ref=back_out.at[slot],
            dst_ref=back.at[slot, sender],
            send_sem=back_send.at[slot, c],
            recv_sem=back_recv.at[slot, sender],
            device_id=device(c, shifted(place, SLOTS[slot], 1)),
            device_id_type=MESH,
        )

    sibling_back = pltpu.make_async_remote_copy(
        src_ref=back_out.at[0],
        dst_ref=back.at[0, core],
        send_sem=back_send.at[0, 0],
        recv_sem=back_recv.at[0, 0],
        device_id=device(1 - core, place),
        device_id_type=MESH,
    )
    for slot in range(NSLOT):
        back_out[slot] = jnp.max(best[slot], axis=0, keepdims=True)
        if slot == 0:
            sibling_back.start()
        else:
            for c in range(2):
                back_copy(slot, c, core).start()
    back[0, core] = back_out[0]
    sibling_back.wait_recv()
    for slot in range(1, NSLOT):
        for c in range(2):
            back_copy(slot, c, c).wait_recv()
    result = jnp.max(back[...].reshape(2 * NSLOT, 1, whole), axis=0)
    o_ref[...] = jnp.where(core == 0, result[:, :half], result[:, half:])

    sibling_back.wait_send()
    for slot in range(1, NSLOT):
        for c in range(2):
            back_copy(slot, c, core).wait_send()


def local(embeddings, cluster):
    half, width = embeddings.shape
    whole = 2 * half
    vmem = pl.BlockSpec(memory_space=pltpu.VMEM)
    rows, id_row = pl.pallas_call(
        gather,
        out_shape=(
            jax.ShapeDtypeStruct((NSLOT, 2, half, width), jnp.bfloat16),
            jax.ShapeDtypeStruct((NSLOT, 1, whole), jnp.float32),
        ),
        in_specs=[vmem] * 2,
        out_specs=(vmem, vmem),
        scratch_shapes=[
            pltpu.VMEM((NSLOT, 2, 1, whole), jnp.float32),
            pltpu.VMEM((1, whole), jnp.float32),
        ]
        + [pltpu.SemaphoreType.DMA((NSLOT, NPART))] * 4
        + [pltpu.SemaphoreType.DMA((NSLOT, 2))] * 2,
        compiler_params=pltpu.CompilerParams(
            collective_id=0, has_side_effects=True, vmem_limit_bytes=24 * 1024 * 1024
        ),
    )(embeddings, cluster.reshape(1, half))
    best = pl.pallas_call(
        product,
        out_shape=jax.ShapeDtypeStruct((NSLOT, 8, whole), jnp.float32),
        in_specs=[vmem] * 2,
        out_specs=vmem,
        scratch_shapes=[pltpu.VMEM((whole, 128), jnp.float32), pltpu.VMEM((whole, 128), jnp.float32)],
        compiler_params=pltpu.CompilerParams(vmem_limit_bytes=24 * 1024 * 1024),
    )(rows, id_row)
    result = pl.pallas_call(
        give_back,
        out_shape=jax.ShapeDtypeStruct((1, half), jnp.float32),
        in_specs=[vmem],
        out_specs=vmem,
        scratch_shapes=[
            pltpu.VMEM((NSLOT, 2, 1, whole), jnp.float32),
            pltpu.VMEM((NSLOT, 1, whole), jnp.float32),
        ]
        + [pltpu.SemaphoreType.DMA((NSLOT, 2))] * 2,
        compiler_params=pltpu.CompilerParams(
            collective_id=1, has_side_effects=True, vmem_limit_bytes=24 * 1024 * 1024
        ),
    )(best)
    return result.reshape(half)


def solution(mesh):
    return jax.shard_map(
        local,
        mesh=mesh,
        in_specs=(P(("gx", "gy"), None), P(("gx", "gy"))),
        out_specs=P(("gx", "gy")),
        check_vma=False,
    )
```

```python
import jax
import jax.numpy as jnp
from jax import lax
from jax.experimental import pallas as pl
from jax.experimental.pallas import tpu as pltpu
from jax.sharding import PartitionSpec as P

EPS = 1e-06
TURNS = (
    (0, 1, 2, 3, 4, 5),
    (0, 1, 2, 3, 5, 4),
    (0, 1, 3, 2, 4, 5),
    (0, 1, 3, 2, 5, 4),
    (1, 0, 2, 3, 4, 5),
    (1, 0, 2, 3, 5, 4),
    (1, 0, 3, 2, 4, 5),
    (1, 0, 3, 2, 5, 4),
)
TURN_OF = [0, 4, 4, 0, 2, 6, 6, 2, 2, 6, 6, 2, 0, 4, 4, 0, 1, 5, 5, 1, 3, 7, 7, 3, 3, 7, 7, 3, 1, 5, 5, 1, 1, 5, 5, 1, 3, 7, 7, 3, 3, 7, 7, 3, 1, 5, 5, 1, 0, 4, 4, 0, 2, 6, 6, 2, 2, 6, 6, 2, 0, 4, 4, 0]
HOLDERS = (0, 8, 1, 4, 3, 40, 17, 2, 44, 7, 49, 60)
SOURCES = (0, 4, 2, 8, 3, 20, 34, 1, 28, 11, 50, 60)
GREETED = (1, 2, 3, 4, 7, 8, 11, 16, 17, 20, 28, 32, 34, 40, 44, 49, 50, 60)
PARTS = ((0, 64), (64, 64), (128, 64))
TREES = (
    {1: (0, 3), 2: (0, 0), 3: (0, 2), 4: (2, 0), 5: (1, 5), 6: (2, 4), 7: (0, 1), 8: (5, 3), 9: (4, 2), 10: (6, 4), 11: (8, 5)},
    {1: (0, 3), 2: (0, 0), 3: (0, 2), 4: (7, 1), 5: (1, 5), 6: (2, 4), 7: (0, 1), 8: (5, 3), 9: (4, 2), 10: (6, 4), 11: (8, 5)},
    {1: (0, 3), 2: (0, 0), 3: (0, 2), 4: (7, 1), 5: (1, 5), 6: (2, 4), 7: (0, 1), 8: (5, 3), 9: (4, 2), 10: (6, 4), 11: (8, 5)},
)
CHILDREN = (
    {0: (1, 2, 7, 3), 1: (5,), 2: (4, 6), 4: (9,), 5: (8,), 6: (10,), 8: (11,)},
    {0: (1, 2, 7, 3), 1: (5,), 2: (6,), 4: (9,), 5: (8,), 6: (10,), 7: (4,), 8: (11,)},
    {0: (1, 2, 7, 3), 1: (5,), 2: (6,), 4: (9,), 5: (8,), 6: (10,), 7: (4,), 8: (11,)},
)
ROOT_ORDER = ((0, 1), (0, 2), (0, 3), (1, 7), (1, 1), (1, 2), (1, 3), (2, 7), (2, 1), (2, 2), (2, 3), (0, 7))
PAIRED = frozenset((0, 1, 2, 3, 4, 5, 6, 7, 8, 9, 10))
SEGMENTS = (
    (
        (('i', 0), ('d', 0), ('s',), ('f', 1, 0), ('f', 2, 0), ('f', 3, 0), ('f', 7, 1), ('f', 1, 1), ('f', 2, 1), ('f', 3, 1), ('f', 7, 2), ('f', 5, 0), ('f', 6, 0), ('f', 1, 2), ('f', 2, 2), ('f', 3, 2), ('f', 4, 1), ('i', 1)),
        ((1, 0),),
    ),
    (
        (('i', 2),),
        ((2, 0),),
    ),
    (
        (('f', 5, 1), ('f', 6, 1), ('d', 1)),
        ((2, 1),),
    ),
    (
        (('i', 3), ('d', 2)),
        ((3, 2), (3, 1)),
    ),
    (
        (('f', 4, 0), ('f', 4, 2), ('f', 8, 0), ('i', 4)),
        ((4, 1), (4, 0)),
    ),
    (
        (('f', 5, 2), ('f', 6, 2), ('f', 9, 1), ('i', 5)),
        ((5, 1), (5, 2), (5, 0)),
    ),
    (
        (('d', 3),),
        ((5, 3),),
    ),
    (
        (('d', 4),),
        ((5, 4),),
    ),
    (
        (('f', 7, 0), ('f', 8, 1), ('i', 6), ('d', 5)),
        ((6, 5),),
    ),
    (
        (('f', 9, 0), ('f', 10, 0), ('f', 11, 0)),
        ((6, 0), (6, 3), (6, 4)),
    ),
    (
        (('i', 7),),
        ((7, 5),),
    ),
    (
        (('d', 6),),
        ((7, 6),),
    ),
    (
        (('f', 8, 2), ('i', 8)),
        ((8, 2), (8, 3)),
    ),
    (
        (('f', 9, 2), ('f', 10, 1), ('f', 11, 1)),
        ((8, 4), (8, 6)),
    ),
    (
        (('d', 7),),
        ((8, 7),),
    ),
    (
        (('i', 9),),
        ((9, 6),),
    ),
    (
        (('d', 8),),
        ((9, 8), (9, 1)),
    ),
    (
        (('b', 5), ('b', 6), ('b', 8), ('f', 10, 2), ('f', 11, 2), ('i', 10)),
        ((10, 2), (10, 3), (10, 7), (10, 0)),
    ),
    (
        (('i', 11),),
        ((11, 0), (11, 1), (11, 4)),
    ),
    (
        (('d', 9),),
        ((11, 9),),
    ),
    (
        (('d', 10),),
        ((11, 10),),
    ),
    (
        (('b', 0), ('b', 1), ('b', 2), ('b', 3), ('b', 4), ('b', 7), ('b', 9), ('b', 10), ('b', 11)),
        (),
    ),
)

MESH = pl.DeviceIdType.MESH
NSLOT = len(SOURCES)
NPART = len(PARTS)
NSEG = len(SEGMENTS)
LEFTS = [p for _, items in SEGMENTS for p, _ in items]
RIGHTS = [q for _, items in SEGMENTS for _, q in items]
PAD = 256


def packed(digits, index):
    word = jnp.int32(0)
    for k in range(0, len(digits), 8):
        value = sum(d << (4 * j) for j, d in enumerate(digits[k : k + 8]))
        value = value - (1 << 32) if value >> 31 else value
        word = jnp.where(index // 8 == k // 8, jnp.int32(value), word)
    return lax.shift_right_logical(word, 4 * (index % 8)) & 15


def start_of(seg):
    first = jnp.int32(0)
    for k, (_, items) in enumerate(SEGMENTS):
        if items:
            first = first + jnp.where(seg > k, len(items), 0)
    return first


def gray(code):
    return code ^ ((code >> 1) & 21)


def turned(turn, word):
    return sum(1 << TURNS[turn][k] for k in range(6) if word >> k & 1)


def kernel(
    x_hbm, c_hbm, o_ref, x_ref, c_ref, own, other, ids, ids_out, id_col, side, best, back, back_out,
    load_sem, row_send, row_recv, pair_send, pair_recv, id_send, id_recv, back_send, back_recv,
):
    core = lax.axis_index("gx")
    place = lax.axis_index("gy")
    half = x_ref.shape[0]

    loads = [
        pltpu.make_async_copy(
            x_hbm.at[pl.ds(begin, size)], x_ref.at[pl.ds(begin, size)], load_sem.at[part]
        )
        for part, (begin, size) in enumerate(PARTS)
    ]
    loads.append(pltpu.make_async_copy(c_hbm, c_ref, load_sem.at[NPART]))
    for load in loads:
        load.start()

    corner = gray(place)
    turn = packed(TURN_OF, corner)

    def chip(word):
        values = [turned(t, word) for t in range(len(TURNS))]
        there = jnp.int32(values[0])
        for value in sorted(set(values) - {values[0]}):
            hits = turn < 0
            for t, v in enumerate(values):
                if v == value:
                    hits = hits | (turn == t)
            there = jnp.where(hits, value, there)
        return gray(corner ^ there)

    source = [chip(w) for w in SOURCES]
    holder = [chip(w) for w in HOLDERS]
    step_to = [chip(1 << k) for k in range(6)]

    barrier = pltpu.get_barrier_semaphore()

    def greet(c, where):
        pl.semaphore_signal(barrier, inc=1, device_id=(c, where), device_id_type=MESH)

    greeted = []
    for word in GREETED:
        greeted.append(chip(word))
    for where in greeted:
        greet(core, where)
        greet(1 - core, where)
    greet(1 - core, place)

    lane = lax.broadcasted_iota(jnp.int32, (1, PAD), 1)
    for part, (begin, size) in enumerate(PARTS):
        loads[part].wait()
        values = x_ref[begin : begin + size, :].astype(jnp.float32)
        total = jnp.sum(values * values, axis=1, keepdims=True)
        own[0, begin : begin + size, :] = (values * lax.rsqrt(total + EPS)).astype(jnp.bfloat16)
    loads[NPART].wait()
    cluster = c_ref[...].astype(jnp.float32)
    ids_out[...] = jnp.concatenate([cluster, jnp.full((1, PAD - half), -2.0, jnp.float32)], axis=1)
    ids[0, 0] = ids_out[...]

    pl.semaphore_wait(barrier, 2 * len(GREETED) + 1)

    def id_copy(slot, which):
        return pltpu.make_async_remote_copy(
            src_ref=ids_out,
            dst_ref=ids.at[slot, which],
            send_sem=id_send.at[slot, which],
            recv_sem=id_recv.at[slot, which],
            device_id=(1 - core if which else core, holder[slot]),
            device_id_type=MESH,
        )

    def back_copy(slot, which):
        return pltpu.make_async_remote_copy(
            src_ref=back_out.at[slot, which],
            dst_ref=back.at[slot, which],
            send_sem=back_send.at[slot, which],
            recv_sem=back_recv.at[slot, which],
            device_id=(1 - core if which else core, source[slot]),
            device_id_type=MESH,
        )

    def row_copy(part, slot):
        begin, size = PARTS[part]
        parent, step = TREES[part][slot]
        return pltpu.make_async_remote_copy(
            src_ref=own.at[parent, pl.ds(begin, size)],
            dst_ref=own.at[slot, pl.ds(begin, size)],
            send_sem=row_send.at[slot, part],
            recv_sem=row_recv.at[slot, part],
            device_id=(core, step_to[step]),
            device_id_type=MESH,
        )

    def pair_copy(slot, part):
        begin, size = PARTS[part]
        return pltpu.make_async_remote_copy(
            src_ref=own.at[slot, pl.ds(begin, size)],
            dst_ref=other.at[slot, pl.ds(begin, size)],
            send_sem=pair_send.at[slot, part],
            recv_sem=pair_recv.at[slot, part],
            device_id=(1 - core, place),
            device_id_type=MESH,
        )

    for part, slot in ROOT_ORDER:
        row_copy(part, slot).start()
    id_copy(0, 1).start()
    for part in range(NPART):
        pair_copy(0, part).start()
    for slot in range(1, NSLOT):
        id_copy(slot, 0).start()
        if slot in PAIRED:
            id_copy(slot, 1).start()

    best[...] = jnp.full(best.shape, -1.0, jnp.float32)
    side[...] = jnp.full(side.shape, -1.0, jnp.float32)
    for slot in range(NSLOT):
        own[slot, half:PAD, :] = jnp.zeros((PAD - half, own.shape[2]), own.dtype)

    def forward(slot, part):
        row_copy(part, slot).wait_recv()
        for child in CHILDREN[part].get(slot, ()):
            row_copy(part, child).start()
        if slot in PAIRED:
            pair_copy(slot, part).start()

    def take_pair(slot):
        for part in range(NPART):
            pair_copy(slot, part).wait_recv()

    def take_ids(slot):
        if slot > 0:
            id_copy(slot, 0).wait_recv()
        if slot in PAIRED:
            id_copy(slot, 1).wait_recv()
            for which in range(2):
                column = jnp.broadcast_to(ids[slot, which], (128, PAD)).T
                id_col[slot, which * half : (which + 1) * half, :] = column[:half]

    def give_back(slot):
        if slot in PAIRED:
            turned_side = jnp.max(side[slot].T.reshape(128 // 8, 8, 2 * PAD), axis=0)
            back_out[slot, 0] = jnp.max(
                jnp.maximum(best[slot], turned_side[:, :PAD]), axis=0, keepdims=True
            )
            back_out[slot, 1] = jnp.max(turned_side[:, PAD:], axis=0, keepdims=True)
            if slot > 0:
                back_copy(slot, 0).start()
            back_copy(slot, 1).start()
        else:
            back_out[slot, 0] = jnp.max(best[slot], axis=0, keepdims=True)
            back_copy(slot, 0).start()

    def multiply(p, q, same):
        left = jnp.concatenate([own[q, :half, :], other[q]], axis=0)
        products = lax.dot_general(
            left, own[p], (((1,), (1,)), ((), ())), preferred_element_type=jnp.float32
        )
        left_id = id_col[q]
        row_best = None
        for k in range(PAD // 128):
            lanes = slice(128 * k, 128 * k + 128)
            allowed = left_id == ids[p, 0, :, lanes]
            if same:
                row = lax.broadcasted_iota(jnp.int32, (2 * half, 128), 0)
                column = lax.broadcasted_iota(jnp.int32, (2 * half, 128), 1) + 128 * k
                allowed = allowed & (row != column)
            masked = jnp.where(allowed, products[:, lanes], -1.0)
            row_best = masked if row_best is None else jnp.maximum(row_best, masked)
            best[p, :, lanes] = jnp.maximum(
                best[p, :, lanes], jnp.max(masked.reshape(half // 4, 8, 128), axis=0)
            )
        side[q, :half, :] = jnp.maximum(side[q, :half, :], row_best[:half])
        side[q, PAD : PAD + half, :] = jnp.maximum(side[q, PAD : PAD + half, :], row_best[half:])

    def step(index, carry):
        multiply(packed(LEFTS, index), packed(RIGHTS, index), False)
        return carry

    actions = {
        "f": forward,
        "d": take_pair,
        "i": take_ids,
        "b": give_back,
        "s": lambda: multiply(0, 0, True),
    }

    def segment(seg, carry):
        for k, (events, _) in enumerate(SEGMENTS):
            if events:

                @pl.when(seg == k)
                def _():
                    for name, *where in events:
                        actions[name](*where)

        return lax.fori_loop(start_of(seg), start_of(seg + 1), step, carry)

    lax.fori_loop(0, NSEG, segment, 0)

    result = back_out[0, 0]
    for slot in range(NSLOT):
        for which in range(2):
            if (slot > 0 or which) and (slot in PAIRED or not which):
                back_copy(slot, which).wait_recv()
                result = jnp.maximum(result, back[slot, which])
    o_ref[...] = result[:, :half]

    for part in range(NPART):
        for slot in range(1, NSLOT):
            row_copy(part, slot).wait_send()
        for slot in sorted(PAIRED):
            pair_copy(slot, part).wait_send()
    for slot in range(NSLOT):
        for which in range(2):
            if (slot > 0 or which) and (slot in PAIRED or not which):
                id_copy(slot, which).wait_send()
                back_copy(slot, which).wait_send()


def local(embeddings, cluster):
    half, width = embeddings.shape
    best = pl.pallas_call(
        kernel,
        out_shape=jax.ShapeDtypeStruct((1, half), jnp.float32),
        in_specs=[pl.BlockSpec(memory_space=pl.ANY)] * 2,
        out_specs=pl.BlockSpec(memory_space=pltpu.VMEM),
        scratch_shapes=[
            pltpu.VMEM((half, width), jnp.bfloat16),
            pltpu.VMEM((1, half), jnp.int32),
            pltpu.VMEM((NSLOT, PAD, width), jnp.bfloat16),
            pltpu.VMEM((NSLOT, half, width), jnp.bfloat16),
            pltpu.VMEM((NSLOT, 2, 1, PAD), jnp.float32),
            pltpu.VMEM((1, PAD), jnp.float32),
            pltpu.VMEM((NSLOT, 2 * half, 128), jnp.float32),
            pltpu.VMEM((NSLOT, 2 * PAD, 128), jnp.float32),
            pltpu.VMEM((NSLOT, 8, PAD), jnp.float32),
            pltpu.VMEM((NSLOT, 2, 1, PAD), jnp.float32),
            pltpu.VMEM((NSLOT, 2, 1, PAD), jnp.float32),
            pltpu.SemaphoreType.DMA((NPART + 1,)),
            pltpu.SemaphoreType.DMA((NSLOT, NPART)),
            pltpu.SemaphoreType.DMA((NSLOT, NPART)),
            pltpu.SemaphoreType.DMA((NSLOT, NPART)),
            pltpu.SemaphoreType.DMA((NSLOT, NPART)),
            pltpu.SemaphoreType.DMA((NSLOT, 2)),
            pltpu.SemaphoreType.DMA((NSLOT, 2)),
            pltpu.SemaphoreType.DMA((NSLOT, 2)),
            pltpu.SemaphoreType.DMA((NSLOT, 2)),
        ],
        compiler_params=pltpu.CompilerParams(
            collective_id=0, has_side_effects=True, vmem_limit_bytes=56 * 1024 * 1024
        ),
        cost_estimate=pl.CostEstimate(
            flops=4 * len(LEFTS) * half * half * width, bytes_accessed=2 * half * width, transcendentals=half
        ),
    )(embeddings, cluster.reshape(1, half))
    return best.reshape(half)


def solution(mesh):
    return jax.shard_map(
        local,
        mesh=mesh,
        in_specs=(P(("gx", "gy"), None), P(("gx", "gy"))),
        out_specs=P(("gx", "gy")),
        check_vma=False,
    )
```

```python
import jax
import jax.numpy as jnp
from jax import lax
from jax.experimental import pallas as pl
from jax.experimental.pallas import tpu as pltpu
from jax.sharding import PartitionSpec as P

EPS = 1e-06
TURNS = (
    (0, 1, 2, 3, 4, 5),
    (0, 1, 2, 3, 5, 4),
    (0, 1, 3, 2, 4, 5),
    (0, 1, 3, 2, 5, 4),
    (1, 0, 2, 3, 4, 5),
    (1, 0, 2, 3, 5, 4),
    (1, 0, 3, 2, 4, 5),
    (1, 0, 3, 2, 5, 4),
)
TURN_OF = [0, 4, 4, 0, 2, 6, 6, 2, 2, 6, 6, 2, 0, 4, 4, 0, 1, 5, 5, 1, 3, 7, 7, 3, 3, 7, 7, 3, 1, 5, 5, 1, 1, 5, 5, 1, 3, 7, 7, 3, 3, 7, 7, 3, 1, 5, 5, 1, 0, 4, 4, 0, 2, 6, 6, 2, 2, 6, 6, 2, 0, 4, 4, 0]
HOLDERS = (0, 2, 1, 16, 32, 10, 20, 17, 42, 22, 49, 14)
SOURCES = (0, 1, 2, 32, 16, 5, 40, 34, 21, 41, 50, 13)
GREETED = (1, 2, 4, 5, 8, 10, 13, 14, 16, 17, 20, 21, 22, 32, 34, 40, 41, 42, 49, 50)
PARTS = ((0, 64), (64, 64), (128, 64))
TREES = (
    {1: (0, 1), 2: (0, 0), 3: (0, 4), 4: (0, 5), 5: (1, 3), 6: (3, 2), 7: (2, 4), 8: (5, 5), 9: (6, 1), 10: (7, 4), 11: (5, 3)},
    {1: (0, 1), 2: (0, 0), 3: (0, 4), 4: (0, 5), 5: (1, 3), 6: (3, 2), 7: (3, 0), 8: (5, 5), 9: (6, 1), 10: (7, 4), 11: (5, 3)},
    {1: (0, 1), 2: (0, 0), 3: (0, 4), 4: (0, 5), 5: (1, 3), 6: (3, 2), 7: (3, 0), 8: (5, 5), 9: (6, 1), 10: (7, 4), 11: (5, 3)},
)
CHILDREN = (
    {0: (1, 2, 3, 4), 1: (5,), 2: (7,), 3: (6,), 5: (8, 11), 6: (9,), 7: (10,)},
    {0: (1, 3, 2, 4), 1: (5,), 3: (7, 6), 5: (8, 11), 6: (9,), 7: (10,)},
    {0: (1, 3, 2, 4), 1: (5,), 3: (7, 6), 5: (8, 11), 6: (9,), 7: (10,)},
)
ROOT_ORDER = ((0, 1), (0, 2), (0, 3), (0, 4), (1, 1), (1, 2), (1, 3), (1, 4), (2, 1), (2, 2), (2, 3), (2, 4))
PAIRED = frozenset((0, 1, 2, 3, 4, 5, 6, 7, 8, 10))
SEGMENTS = (
    (
        (('i', 0), ('d', 0), ('t', 0), ('s',), ('f', 1, 0), ('f', 2, 0), ('f', 3, 0), ('f', 4, 0), ('f', 1, 1), ('f', 2, 1), ('f', 3, 1), ('f', 4, 1), ('f', 5, 0), ('f', 6, 0), ('f', 1, 2), ('f', 2, 2), ('f', 3, 2), ('f', 4, 2), ('i', 1), ('t', 1)),
        ((1, 0),),
    ),
    (
        (('f', 5, 1), ('f', 6, 1), ('i', 3), ('t', 3)),
        ((3, 0),),
    ),
    (
        (('i', 2), ('d', 2)),
        ((3, 2),),
    ),
    (
        (('d', 1),),
        ((3, 1),),
    ),
    (
        (('t', 2),),
        ((2, 1),),
    ),
    (
        (('f', 7, 0), ('f', 7, 1), ('f', 8, 0), ('f', 9, 0), ('i', 4), ('t', 4), ('d', 3)),
        ((4, 3),),
    ),
    (
        (('f', 5, 2), ('f', 6, 2), ('i', 5), ('t', 5)),
        ((5, 3), (5, 0), (5, 2)),
    ),
    (
        (('f', 7, 2), ('f', 8, 1), ('f', 9, 1)),
        ((5, 1),),
    ),
    (
        (('d', 4),),
        ((5, 4),),
    ),
    (
        (('f', 10, 0), ('f', 11, 0), ('i', 6), ('t', 6)),
        ((6, 0), (6, 2)),
    ),
    (
        (('d', 5),),
        ((6, 5), (6, 4)),
    ),
    (
        (('f', 8, 2), ('f', 9, 2), ('i', 7), ('t', 7)),
        ((7, 5),),
    ),
    (
        (('f', 10, 1), ('f', 11, 1)),
        ((7, 1), (7, 4)),
    ),
    (
        (('d', 6),),
        ((7, 6),),
    ),
    (
        (('i', 8), ('t', 8)),
        ((8, 3), (8, 6)),
    ),
    (
        (('d', 7),),
        ((8, 7),),
    ),
    (
        (('i', 9), ('t', 9)),
        ((9, 5),),
    ),
    (
        (('f', 10, 2), ('f', 11, 2)),
        ((9, 4),),
    ),
    (
        (('d', 8),),
        ((9, 8),),
    ),
    (
        (('i', 10), ('t', 10)),
        ((10, 6), (10, 1), (10, 8)),
    ),
    (
        (('i', 11), ('t', 11)),
        ((11, 0), (11, 1), (11, 2), (11, 4), (11, 7), (11, 8)),
    ),
    (
        (('d', 10),),
        ((11, 10),),
    ),
    (
        (('b', 0), ('b', 1), ('b', 2), ('b', 3), ('b', 4), ('b', 5), ('b', 6), ('b', 7), ('b', 8), ('b', 9), ('b', 10), ('b', 11)),
        (),
    ),
)

MESH = pl.DeviceIdType.MESH
NSLOT = len(SOURCES)
NPART = len(PARTS)
NSEG = len(SEGMENTS)
LEFTS = [p for _, items in SEGMENTS for p, _ in items]
RIGHTS = [q for _, items in SEGMENTS for _, q in items]
PAD = 256


def packed(digits, index):
    word = jnp.int32(0)
    for k in range(0, len(digits), 8):
        value = sum(d << (4 * j) for j, d in enumerate(digits[k : k + 8]))
        value = value - (1 << 32) if value >> 31 else value
        word = jnp.where(index // 8 == k // 8, jnp.int32(value), word)
    return lax.shift_right_logical(word, 4 * (index % 8)) & 15


def start_of(seg):
    first = jnp.int32(0)
    for k, (_, items) in enumerate(SEGMENTS):
        if items:
            first = first + jnp.where(seg > k, len(items), 0)
    return first


def gray(code):
    return code ^ ((code >> 1) & 21)


def turned(turn, word):
    return sum(1 << TURNS[turn][k] for k in range(6) if word >> k & 1)


def kernel(
    x_hbm, c_hbm, o_ref, x_ref, c_ref, own, other, across, ids, ids_out, id_col, side, best, back, back_out,
    load_sem, row_send, row_recv, pair_send, pair_recv, id_send, id_recv, back_send, back_recv,
):
    core = lax.axis_index("gx")
    place = lax.axis_index("gy")
    half = x_ref.shape[0]

    loads = [
        pltpu.make_async_copy(
            x_hbm.at[pl.ds(begin, size)], x_ref.at[pl.ds(begin, size)], load_sem.at[part]
        )
        for part, (begin, size) in enumerate(PARTS)
    ]
    loads.append(pltpu.make_async_copy(c_hbm, c_ref, load_sem.at[NPART]))
    for load in loads:
        load.start()

    corner = gray(place)
    turn = packed(TURN_OF, corner)

    def chip(word):
        values = [turned(t, word) for t in range(len(TURNS))]
        there = jnp.int32(values[0])
        for value in sorted(set(values) - {values[0]}):
            hits = turn < 0
            for t, v in enumerate(values):
                if v == value:
                    hits = hits | (turn == t)
            there = jnp.where(hits, value, there)
        return gray(corner ^ there)

    source = [chip(w) for w in SOURCES]
    holder = [chip(w) for w in HOLDERS]
    step_to = [chip(1 << k) for k in range(6)]

    barrier = pltpu.get_barrier_semaphore()

    def greet(c, where):
        pl.semaphore_signal(barrier, inc=1, device_id=(c, where), device_id_type=MESH)

    greeted = []
    for word in GREETED:
        greeted.append(chip(word))
    for where in greeted:
        greet(core, where)
        greet(1 - core, where)
    greet(1 - core, place)

    lane = lax.broadcasted_iota(jnp.int32, (1, PAD), 1)
    for part, (begin, size) in enumerate(PARTS):
        loads[part].wait()
        values = x_ref[begin : begin + size, :].astype(jnp.float32)
        total = jnp.sum(values * values, axis=1, keepdims=True)
        own[0, begin : begin + size, :] = (values * lax.rsqrt(total + EPS)).astype(jnp.bfloat16)
    loads[NPART].wait()
    cluster = c_ref[...].astype(jnp.float32)
    ids_out[...] = jnp.concatenate([cluster, jnp.full((1, PAD - half), -2.0, jnp.float32)], axis=1)
    ids[0, 0] = ids_out[...]

    pl.semaphore_wait(barrier, 2 * len(GREETED) + 1)

    def id_copy(slot, which):
        return pltpu.make_async_remote_copy(
            src_ref=ids_out,
            dst_ref=ids.at[slot, which],
            send_sem=id_send.at[slot, which],
            recv_sem=id_recv.at[slot, which],
            device_id=(1 - core if which else core, holder[slot]),
            device_id_type=MESH,
        )

    def back_copy(slot, which):
        return pltpu.make_async_remote_copy(
            src_ref=back_out.at[slot, which],
            dst_ref=back.at[slot, which],
            send_sem=back_send.at[slot, which],
            recv_sem=back_recv.at[slot, which],
            device_id=(1 - core if which else core, source[slot]),
            device_id_type=MESH,
        )

    def row_copy(part, slot):
        begin, size = PARTS[part]
        parent, step = TREES[part][slot]
        return pltpu.make_async_remote_copy(
            src_ref=own.at[parent, pl.ds(begin, size)],
            dst_ref=own.at[slot, pl.ds(begin, size)],
            send_sem=row_send.at[slot, part],
            recv_sem=row_recv.at[slot, part],
            device_id=(core, step_to[step]),
            device_id_type=MESH,
        )

    def pair_copy(slot, part):
        begin, size = PARTS[part]
        return pltpu.make_async_remote_copy(
            src_ref=own.at[slot, pl.ds(begin, size)],
            dst_ref=other.at[slot, pl.ds(begin, size)],
            send_sem=pair_send.at[slot, part],
            recv_sem=pair_recv.at[slot, part],
            device_id=(1 - core, place),
            device_id_type=MESH,
        )

    for part, slot in ROOT_ORDER:
        row_copy(part, slot).start()
    id_copy(0, 1).start()
    for part in range(NPART):
        pair_copy(0, part).start()
    for slot in range(1, NSLOT):
        id_copy(slot, 0).start()
        if slot in PAIRED:
            id_copy(slot, 1).start()

    best[...] = jnp.full(best.shape, -1.0, jnp.float32)
    side[...] = jnp.full(side.shape, -1.0, jnp.float32)
    for slot in range(NSLOT):
        own[slot, half:PAD, :] = jnp.zeros((PAD - half, own.shape[2]), own.dtype)

    def forward(slot, part):
        row_copy(part, slot).wait_recv()
        for child in CHILDREN[part].get(slot, ()):
            row_copy(part, child).start()
        if slot in PAIRED:
            pair_copy(slot, part).start()

    def take_pair(slot):
        for part in range(NPART):
            pair_copy(slot, part).wait_recv()

    def take_ids(slot):
        if slot > 0:
            id_copy(slot, 0).wait_recv()
        if slot in PAIRED:
            id_copy(slot, 1).wait_recv()
            for which in range(2):
                column = jnp.broadcast_to(ids[slot, which], (128, PAD)).T
                id_col[slot, which * half : (which + 1) * half, :] = column[:half]

    def take_across(slot):
        across[slot] = own[slot].T

    def give_back(slot):
        if slot in PAIRED:
            turned_side = jnp.max(side[slot].T.reshape(128 // 8, 8, 2 * PAD), axis=0)
            back_out[slot, 0] = jnp.max(
                jnp.maximum(best[slot], turned_side[:, :PAD]), axis=0, keepdims=True
            )
            back_out[slot, 1] = jnp.max(turned_side[:, PAD:], axis=0, keepdims=True)
            if slot > 0:
                back_copy(slot, 0).start()
            back_copy(slot, 1).start()
        else:
            back_out[slot, 0] = jnp.max(best[slot], axis=0, keepdims=True)
            back_copy(slot, 0).start()

    def multiply(p, q, same):
        left = jnp.concatenate([own[q, :half, :], other[q]], axis=0)
        products = jnp.dot(left, across[p], preferred_element_type=jnp.float32)
        left_id = id_col[q]
        row_best = None
        for k in range(PAD // 128):
            lanes = slice(128 * k, 128 * k + 128)
            allowed = left_id == ids[p, 0, :, lanes]
            if same:
                row = lax.broadcasted_iota(jnp.int32, (2 * half, 128), 0)
                column = lax.broadcasted_iota(jnp.int32, (2 * half, 128), 1) + 128 * k
                allowed = allowed & (row != column)
            masked = jnp.where(allowed, products[:, lanes], -1.0)
            row_best = masked if row_best is None else jnp.maximum(row_best, masked)
            best[p, :, lanes] = jnp.maximum(
                best[p, :, lanes], jnp.max(masked.reshape(half // 4, 8, 128), axis=0)
            )
        side[q, :half, :] = jnp.maximum(side[q, :half, :], row_best[:half])
        side[q, PAD : PAD + half, :] = jnp.maximum(side[q, PAD : PAD + half, :], row_best[half:])

    def step(index, carry):
        multiply(packed(LEFTS, index), packed(RIGHTS, index), False)
        return carry

    actions = {
        "f": forward,
        "d": take_pair,
        "i": take_ids,
        "t": take_across,
        "b": give_back,
        "s": lambda: multiply(0, 0, True),
    }

    def segment(seg, carry):
        for k, (events, _) in enumerate(SEGMENTS):
            if events:

                @pl.when(seg == k)
                def _():
                    for name, *where in events:
                        actions[name](*where)

        return lax.fori_loop(start_of(seg), start_of(seg + 1), step, carry)

    lax.fori_loop(0, NSEG, segment, 0)

    result = back_out[0, 0]
    for slot in range(NSLOT):
        for which in range(2):
            if (slot > 0 or which) and (slot in PAIRED or not which):
                back_copy(slot, which).wait_recv()
                result = jnp.maximum(result, back[slot, which])
    o_ref[...] = result[:, :half]

    for part in range(NPART):
        for slot in range(1, NSLOT):
            row_copy(part, slot).wait_send()
        for slot in sorted(PAIRED):
            pair_copy(slot, part).wait_send()
    for slot in range(NSLOT):
        for which in range(2):
            if (slot > 0 or which) and (slot in PAIRED or not which):
                id_copy(slot, which).wait_send()
                back_copy(slot, which).wait_send()


def local(embeddings, cluster):
    half, width = embeddings.shape
    best = pl.pallas_call(
        kernel,
        out_shape=jax.ShapeDtypeStruct((1, half), jnp.float32),
        in_specs=[pl.BlockSpec(memory_space=pl.ANY)] * 2,
        out_specs=pl.BlockSpec(memory_space=pltpu.VMEM),
        scratch_shapes=[
            pltpu.VMEM((half, width), jnp.bfloat16),
            pltpu.VMEM((1, half), jnp.int32),
            pltpu.VMEM((NSLOT, PAD, width), jnp.bfloat16),
            pltpu.VMEM((NSLOT, half, width), jnp.bfloat16),
            pltpu.VMEM((NSLOT, width, PAD), jnp.bfloat16),
            pltpu.VMEM((NSLOT, 2, 1, PAD), jnp.float32),
            pltpu.VMEM((1, PAD), jnp.float32),
            pltpu.VMEM((NSLOT, 2 * half, 128), jnp.float32),
            pltpu.VMEM((NSLOT, 2 * PAD, 128), jnp.float32),
            pltpu.VMEM((NSLOT, 8, PAD), jnp.float32),
            pltpu.VMEM((NSLOT, 2, 1, PAD), jnp.float32),
            pltpu.VMEM((NSLOT, 2, 1, PAD), jnp.float32),
            pltpu.SemaphoreType.DMA((NPART + 1,)),
            pltpu.SemaphoreType.DMA((NSLOT, NPART)),
            pltpu.SemaphoreType.DMA((NSLOT, NPART)),
            pltpu.SemaphoreType.DMA((NSLOT, NPART)),
            pltpu.SemaphoreType.DMA((NSLOT, NPART)),
            pltpu.SemaphoreType.DMA((NSLOT, 2)),
            pltpu.SemaphoreType.DMA((NSLOT, 2)),
            pltpu.SemaphoreType.DMA((NSLOT, 2)),
            pltpu.SemaphoreType.DMA((NSLOT, 2)),
        ],
        compiler_params=pltpu.CompilerParams(
            collective_id=0, has_side_effects=True, vmem_limit_bytes=56 * 1024 * 1024
        ),
        cost_estimate=pl.CostEstimate(
            flops=4 * len(LEFTS) * half * half * width, bytes_accessed=2 * half * width, transcendentals=half
        ),
    )(embeddings, cluster.reshape(1, half))
    return best.reshape(half)


def solution(mesh):
    return jax.shard_map(
        local,
        mesh=mesh,
        in_specs=(P(("gx", "gy"), None), P(("gx", "gy"))),
        out_specs=P(("gx", "gy")),
        check_vma=False,
    )
```

```python
import jax
import jax.numpy as jnp
from jax import lax
from jax.experimental import pallas as pl
from jax.experimental.pallas import tpu as pltpu
from jax.sharding import PartitionSpec as P

EPS = 1e-06
TURNS = (
    (0, 1, 2, 3, 4, 5),
    (0, 1, 2, 3, 5, 4),
    (0, 1, 3, 2, 4, 5),
    (0, 1, 3, 2, 5, 4),
    (1, 0, 2, 3, 4, 5),
    (1, 0, 2, 3, 5, 4),
    (1, 0, 3, 2, 4, 5),
    (1, 0, 3, 2, 5, 4),
)
TURN_OF = [0, 4, 4, 0, 2, 6, 6, 2, 2, 6, 6, 2, 0, 4, 4, 0, 1, 5, 5, 1, 3, 7, 7, 3, 3, 7, 7, 3, 1, 5, 5, 1, 1, 5, 5, 1, 3, 7, 7, 3, 3, 7, 7, 3, 1, 5, 5, 1, 0, 4, 4, 0, 2, 6, 6, 2, 2, 6, 6, 2, 0, 4, 4, 0]
HOLDERS = (0, 2, 1, 16, 32, 10, 20, 17, 42, 22, 49, 14)
SOURCES = (0, 1, 2, 32, 16, 5, 40, 34, 21, 41, 50, 13)
GREETED = (1, 2, 4, 5, 8, 10, 13, 14, 16, 17, 20, 21, 22, 32, 34, 40, 41, 42, 49, 50)
PARTS = ((0, 64), (64, 64), (128, 64))
TREES = (
    {1: (0, 1), 2: (0, 0), 3: (0, 4), 4: (0, 5), 5: (1, 3), 6: (3, 2), 7: (2, 4), 8: (5, 5), 9: (6, 1), 10: (7, 4), 11: (5, 3)},
    {1: (0, 1), 2: (0, 0), 3: (0, 4), 4: (0, 5), 5: (1, 3), 6: (3, 2), 7: (3, 0), 8: (5, 5), 9: (6, 1), 10: (7, 4), 11: (5, 3)},
    {1: (0, 1), 2: (0, 0), 3: (0, 4), 4: (0, 5), 5: (1, 3), 6: (3, 2), 7: (3, 0), 8: (5, 5), 9: (6, 1), 10: (7, 4), 11: (5, 3)},
)
CHILDREN = (
    {0: (1, 2, 3, 4), 1: (5,), 2: (7,), 3: (6,), 5: (8, 11), 6: (9,), 7: (10,)},
    {0: (1, 3, 2, 4), 1: (5,), 3: (7, 6), 5: (8, 11), 6: (9,), 7: (10,)},
    {0: (1, 3, 2, 4), 1: (5,), 3: (7, 6), 5: (8, 11), 6: (9,), 7: (10,)},
)
ROOT_FIRST = 4
ROOT_ORDER = ((0, 1), (0, 2), (0, 3), (0, 4), (1, 1), (1, 2), (1, 3), (1, 4), (2, 1), (2, 2), (2, 3), (2, 4))
PAIRED = frozenset((0, 1, 2, 3, 4, 5, 6, 7, 8, 10))
SEGMENTS = (
    (
        (('i',), ('f', 1, 0, 0), ('f', 2, 0, 0), ('f', 3, 0, 0), ('f', 4, 0, 0), ('j',), ('d', 0)),
        ((0, 0),),
        (),
    ),
    (
        (('f', 1, 1, 0), ('f', 2, 1, 0), ('f', 3, 1, 0), ('f', 4, 1, 0), ('f', 5, 0, 0), ('f', 6, 0, 0), ('f', 1, 2, 1), ('f', 2, 2, 1), ('f', 3, 2, 1), ('f', 4, 2, 1)),
        ((1, 0),),
        (),
    ),
    (
        (('f', 5, 1, 0), ('f', 6, 1, 0)),
        ((3, 0),),
        (),
    ),
    (
        (('d', 2),),
        ((3, 2),),
        (),
    ),
    (
        (('d', 1),),
        ((3, 1), (2, 1)),
        (),
    ),
    (
        (('f', 7, 0, 0), ('f', 7, 1, 0), ('f', 8, 0, 0), ('f', 9, 0, 0), ('d', 3)),
        ((4, 3),),
        (),
    ),
    (
        (('f', 5, 2, 1), ('f', 6, 2, 1)),
        ((5, 3), (5, 0), (5, 2)),
        (),
    ),
    (
        (('f', 7, 2, 1), ('f', 8, 1, 0), ('f', 9, 1, 0)),
        ((5, 1),),
        (),
    ),
    (
        (('d', 4),),
        ((5, 4),),
        (),
    ),
    (
        (('f', 10, 0, 0), ('f', 11, 0, 0)),
        ((6, 0), (6, 2)),
        (),
    ),
    (
        (('d', 5),),
        ((6, 5),),
        (),
    ),
    (
        (('f', 8, 2, 1), ('f', 9, 2, 1)),
        ((6, 4), (7, 5)),
        (),
    ),
    (
        (('f', 10, 1, 0), ('f', 11, 1, 0)),
        ((7, 1), (7, 4)),
        (),
    ),
    (
        (('d', 6),),
        ((7, 6), (8, 3), (8, 6)),
        (),
    ),
    (
        (('f', 10, 2, 1), ('f', 11, 2, 1), ('d', 7)),
        ((8, 7), (9, 5), (9, 4)),
        (),
    ),
    (
        (('d', 8),),
        ((9, 8), (10, 6), (10, 1), (10, 8), (11, 0), (11, 1), (11, 2), (11, 4), (11, 7), (11, 8)),
        (),
    ),
    (
        (('d', 10),),
        ((11, 10),),
        (0, 1, 2, 3, 4, 5, 6, 7, 8, 9, 10, 11),
    ),
)

MESH = pl.DeviceIdType.MESH
NSLOT = len(SOURCES)
NPART = len(PARTS)
NSEG = len(SEGMENTS)
LEFTS = [p for _, items, _ in SEGMENTS for p, _ in items]
RIGHTS = [q for _, items, _ in SEGMENTS for _, q in items]
BACKS = [slot for _, _, slots in SEGMENTS for slot in slots]
PAD = 256


def packed(digits, index):
    word = jnp.int32(0)
    for k in range(0, len(digits), 8):
        value = sum(d << (4 * j) for j, d in enumerate(digits[k : k + 8]))
        value = value - (1 << 32) if value >> 31 else value
        word = jnp.where(index // 8 == k // 8, jnp.int32(value), word)
    return lax.shift_right_logical(word, 4 * (index % 8)) & 15


def start_of(seg, column):
    first = jnp.int32(0)
    for k, segment in enumerate(SEGMENTS):
        if segment[column]:
            first = first + jnp.where(seg > k, len(segment[column]), 0)
    return first


def gray(code):
    return code ^ ((code >> 1) & 21)


def turned(turn, word):
    return sum(1 << TURNS[turn][k] for k in range(6) if word >> k & 1)


def kernel(
    x_hbm, c_hbm, o_ref, x_ref, c_ref, own, other, ids, ids_out, id_col, side, best, back, back_out, swap_out,
    swap, load_sem, row_send, row_recv, pair_send, pair_recv, id_send, id_recv, back_send, back_recv, swap_sem,
):
    core = lax.axis_index("gx")
    place = lax.axis_index("gy")
    half = x_ref.shape[0]

    loads = [
        pltpu.make_async_copy(
            x_hbm.at[pl.ds(begin, size)], x_ref.at[pl.ds(begin, size)], load_sem.at[part]
        )
        for part, (begin, size) in enumerate(PARTS)
    ]
    loads.append(pltpu.make_async_copy(c_hbm, c_ref, load_sem.at[NPART]))
    for load in loads:
        load.start()

    corner = gray(place)
    turn = packed(TURN_OF, corner)

    def chip(word):
        values = [turned(t, word) for t in range(len(TURNS))]
        there = jnp.int32(values[0])
        for value in sorted(set(values) - {values[0]}):
            hits = turn < 0
            for t, v in enumerate(values):
                if v == value:
                    hits = hits | (turn == t)
            there = jnp.where(hits, value, there)
        return gray(corner ^ there)

    chips = {word: chip(word) for word in GREETED}
    source = [chips.get(w) for w in SOURCES]
    holder = [chips.get(w) for w in HOLDERS]
    step_to = [chips[1 << k] for k in range(6)]

    barrier = pltpu.get_barrier_semaphore()
    for word in GREETED:
        pl.semaphore_signal(barrier, inc=1, device_id=(core, chips[word]), device_id_type=MESH)
    pl.semaphore_signal(barrier, inc=1, device_id=(1 - core, place), device_id_type=MESH)

    for part, (begin, size) in enumerate(PARTS):
        loads[part].wait()
        values = x_ref[begin : begin + size, :].astype(jnp.float32)
        total = jnp.sum(values * values, axis=1, keepdims=True)
        own[0, begin : begin + size, :] = (values * lax.rsqrt(total + EPS)).astype(jnp.bfloat16)
    loads[NPART].wait()
    cluster = c_ref[...].astype(jnp.float32)
    ids_out[...] = jnp.concatenate([cluster, jnp.full((1, PAD - half), -2.0, jnp.float32)], axis=1)
    ids[0, 0] = ids_out[...]

    pl.semaphore_wait(barrier, len(GREETED) + 1)

    def id_copy(slot):
        return pltpu.make_async_remote_copy(
            src_ref=ids_out,
            dst_ref=ids.at[0, slot],
            send_sem=id_send.at[slot],
            recv_sem=id_recv.at[slot],
            device_id=(core, holder[slot]),
            device_id_type=MESH,
        )

    def id_pair_copy():
        return pltpu.make_async_remote_copy(
            src_ref=ids.at[0],
            dst_ref=ids.at[1],
            send_sem=id_send.at[0],
            recv_sem=id_recv.at[0],
            device_id=(1 - core, place),
            device_id_type=MESH,
        )

    def back_copy(slot, where):
        return pltpu.make_async_remote_copy(
            src_ref=back_out.at[slot],
            dst_ref=back.at[slot],
            send_sem=back_send.at[slot],
            recv_sem=back_recv.at[slot],
            device_id=(core, where),
            device_id_type=MESH,
        )

    def row_copy(part, slot):
        begin, size = PARTS[part]
        parent, step = TREES[part][slot]
        return pltpu.make_async_remote_copy(
            src_ref=own.at[parent, pl.ds(begin, size)],
            dst_ref=own.at[slot, pl.ds(begin, size)],
            send_sem=row_send.at[slot, part],
            recv_sem=row_recv.at[slot, part],
            device_id=(core, step_to[step]),
            device_id_type=MESH,
        )

    def pair_copy(slot):
        return pltpu.make_async_remote_copy(
            src_ref=own.at[slot, pl.ds(0, half)],
            dst_ref=other.at[slot],
            send_sem=pair_send.at[slot],
            recv_sem=pair_recv.at[slot],
            device_id=(1 - core, place),
            device_id_type=MESH,
        )

    for part, slot in ROOT_ORDER[:ROOT_FIRST]:
        row_copy(part, slot).start()
    for slot in range(1, NSLOT):
        id_copy(slot).start()
    for part, slot in ROOT_ORDER[ROOT_FIRST:]:
        row_copy(part, slot).start()
    pair_copy(0).start()

    best[...] = jnp.full(best.shape, -1.0, jnp.float32)
    side[...] = jnp.full(side.shape, -1.0, jnp.float32)
    for slot in range(NSLOT):
        own[slot, half:PAD, :] = jnp.zeros((PAD - half, own.shape[2]), own.dtype)

    def forward(slot, part, last):
        row_copy(part, slot).wait_recv()
        for child in CHILDREN[part].get(slot, ()):
            row_copy(part, child).start()
        if last and slot in PAIRED:
            pair_copy(slot).start()

    def send_ids():
        for slot in range(1, NSLOT):
            id_copy(slot).wait_recv()
        id_pair_copy().start()

    def take_ids():
        id_pair_copy().wait_recv()

        def turn_ids(slot, carry):
            for which in range(2):
                column = jnp.broadcast_to(ids[which, slot], (128, PAD)).T
                id_col[slot, which * half : (which + 1) * half, :] = column[:half]
            return carry

        lax.fori_loop(0, NSLOT, turn_ids, 0)

    def give_back(index, carry):
        slot = packed(BACKS, index)
        turned_side = jnp.max(side[slot].T.reshape(128 // 8, 8, 2 * PAD), axis=0)
        back_out[slot, 0] = jnp.max(jnp.maximum(best[slot], turned_side[:, :PAD]), axis=0, keepdims=True)
        back_out[slot, 1] = jnp.max(turned_side[:, PAD:], axis=0, keepdims=True)
        where = source[1]
        for k in range(2, NSLOT):
            where = jnp.where(slot == k, source[k], where)

        @pl.when(slot > 0)
        def _():
            back_copy(slot, where).start()

        return carry

    def multiply(index, carry):
        p, q = packed(LEFTS, index), packed(RIGHTS, index)
        left = jnp.concatenate([own[q, :half, :], other[q]], axis=0)
        products = lax.dot_general(
            left, own[p], (((1,), (1,)), ((), ())), preferred_element_type=jnp.float32
        )
        left_id = id_col[q]
        row = lax.broadcasted_iota(jnp.int32, (2 * half, 128), 0) + jnp.where(p == q, 0, 4 * PAD)
        column = lax.broadcasted_iota(jnp.int32, (2 * half, 128), 1)
        row_best = None
        for k in range(PAD // 128):
            lanes = slice(128 * k, 128 * k + 128)
            allowed = (left_id == ids[0, p, :, lanes]) & (row != column + 128 * k)
            masked = jnp.where(allowed, products[:, lanes], -1.0)
            row_best = masked if row_best is None else jnp.maximum(row_best, masked)
            best[p, :, lanes] = jnp.maximum(
                best[p, :, lanes], jnp.max(masked.reshape(half // 4, 8, 128), axis=0)
            )
        side[q, :half, :] = jnp.maximum(side[q, :half, :], row_best[:half])
        side[q, PAD : PAD + half, :] = jnp.maximum(side[q, PAD : PAD + half, :], row_best[half:])
        return carry

    actions = {
        "f": forward,
        "d": lambda slot: pair_copy(slot).wait_recv(),
        "i": send_ids,
        "j": take_ids,
    }

    def segment(seg, carry):
        for k, (events, _, _) in enumerate(SEGMENTS):
            if events:

                @pl.when(seg == k)
                def _():
                    for name, *where in events:
                        actions[name](*where)

        lax.fori_loop(start_of(seg, 1), start_of(seg + 1, 1), multiply, carry)
        return lax.fori_loop(start_of(seg, 2), start_of(seg + 1, 2), give_back, carry)

    lax.fori_loop(0, NSEG, segment, 0)

    result = back_out[0]
    for slot in range(1, NSLOT):
        back_copy(slot, source[slot]).wait_recv()
        result = jnp.maximum(result, back[slot])
    swap_out[...] = result[1]
    swapping = pltpu.make_async_remote_copy(
        src_ref=swap_out,
        dst_ref=swap,
        send_sem=swap_sem.at[0],
        recv_sem=swap_sem.at[1],
        device_id=(1 - core, place),
        device_id_type=MESH,
    )
    swapping.start()

    for part in range(NPART):
        for slot in range(1, NSLOT):
            row_copy(part, slot).wait_send()
    for slot in sorted(PAIRED):
        pair_copy(slot).wait_send()
    id_pair_copy().wait_send()
    for slot in range(1, NSLOT):
        id_copy(slot).wait_send()
        back_copy(slot, source[slot]).wait_send()
    swapping.wait()
    o_ref[...] = jnp.maximum(result[0], swap[...])[:, :half]


def local(embeddings, cluster):
    half, width = embeddings.shape
    best = pl.pallas_call(
        kernel,
        out_shape=jax.ShapeDtypeStruct((1, half), jnp.float32),
        in_specs=[pl.BlockSpec(memory_space=pl.ANY)] * 2,
        out_specs=pl.BlockSpec(memory_space=pltpu.VMEM),
        scratch_shapes=[
            pltpu.VMEM((half, width), jnp.bfloat16),
            pltpu.VMEM((1, half), jnp.int32),
            pltpu.VMEM((NSLOT, PAD, width), jnp.bfloat16),
            pltpu.VMEM((NSLOT, half, width), jnp.bfloat16),
            pltpu.VMEM((2, NSLOT, 1, PAD), jnp.float32),
            pltpu.VMEM((1, PAD), jnp.float32),
            pltpu.VMEM((NSLOT, 2 * half, 128), jnp.float32),
            pltpu.VMEM((NSLOT, 2 * PAD, 128), jnp.float32),
            pltpu.VMEM((NSLOT, 8, PAD), jnp.float32),
            pltpu.VMEM((NSLOT, 2, 1, PAD), jnp.float32),
            pltpu.VMEM((NSLOT, 2, 1, PAD), jnp.float32),
            pltpu.VMEM((1, PAD), jnp.float32),
            pltpu.VMEM((1, PAD), jnp.float32),
            pltpu.SemaphoreType.DMA((NPART + 1,)),
            pltpu.SemaphoreType.DMA((NSLOT, NPART)),
            pltpu.SemaphoreType.DMA((NSLOT, NPART)),
            pltpu.SemaphoreType.DMA((NSLOT,)),
            pltpu.SemaphoreType.DMA((NSLOT,)),
            pltpu.SemaphoreType.DMA((NSLOT,)),
            pltpu.SemaphoreType.DMA((NSLOT,)),
            pltpu.SemaphoreType.DMA((NSLOT,)),
            pltpu.SemaphoreType.DMA((NSLOT,)),
            pltpu.SemaphoreType.DMA((2,)),
        ],
        compiler_params=pltpu.CompilerParams(
            collective_id=0, has_side_effects=True, vmem_limit_bytes=56 * 1024 * 1024
        ),
        cost_estimate=pl.CostEstimate(
            flops=4 * len(LEFTS) * half * half * width, bytes_accessed=2 * half * width, transcendentals=half
        ),
    )(embeddings, cluster.reshape(1, half))
    return best.reshape(half)


def solution(mesh):
    return jax.shard_map(
        local,
        mesh=mesh,
        in_specs=(P(("gx", "gy"), None), P(("gx", "gy"))),
        out_specs=P(("gx", "gy")),
        check_vma=False,
    )
```

```python
import jax
import jax.numpy as jnp
from jax import lax
from jax.experimental import pallas as pl
from jax.experimental.pallas import tpu as pltpu
from jax.sharding import PartitionSpec as P

EPS = 1e-06
TURNS = (
    (0, 1, 2, 3, 4, 5),
    (0, 1, 2, 3, 5, 4),
    (0, 1, 3, 2, 4, 5),
    (0, 1, 3, 2, 5, 4),
    (1, 0, 2, 3, 4, 5),
    (1, 0, 2, 3, 5, 4),
    (1, 0, 3, 2, 4, 5),
    (1, 0, 3, 2, 5, 4),
)
TURN_OF = [0, 4, 4, 0, 2, 6, 6, 2, 2, 6, 6, 2, 0, 4, 4, 0, 1, 5, 5, 1, 3, 7, 7, 3, 3, 7, 7, 3, 1, 5, 5, 1, 1, 5, 5, 1, 3, 7, 7, 3, 3, 7, 7, 3, 1, 5, 5, 1, 0, 4, 4, 0, 2, 6, 6, 2, 2, 6, 6, 2, 0, 4, 4, 0]
HOLDERS = (0, 32, 8, 5, 24, 34, 1, 4, 50, 38, 7, 56)
SOURCES = (0, 16, 4, 10, 36, 17, 2, 8, 49, 25, 11, 52)
GREETED = (1, 2, 4, 5, 7, 8, 10, 11, 16, 17, 24, 25, 32, 34, 36, 38, 49, 50, 52, 56)
PARTS = ((0, 64), (64, 64), (128, 64))
TREES = (
    {1: (0, 5), 2: (0, 3), 3: (7, 0), 4: (2, 4), 5: (1, 1), 6: (3, 3), 7: (0, 2), 8: (5, 5), 9: (5, 2), 10: (3, 0), 11: (4, 4)},
    {1: (0, 5), 2: (0, 3), 3: (7, 0), 4: (2, 4), 5: (1, 1), 6: (3, 3), 7: (0, 2), 8: (5, 5), 9: (5, 2), 10: (3, 0), 11: (4, 4)},
    {1: (0, 5), 2: (0, 3), 3: (6, 2), 4: (2, 4), 5: (1, 1), 6: (0, 0), 7: (3, 1), 8: (5, 5), 9: (5, 2), 10: (3, 0), 11: (4, 4)},
)
CHILDREN = (
    {0: (1, 7, 2), 1: (5,), 2: (4,), 3: (10, 6), 4: (11,), 5: (8, 9), 7: (3,)},
    {0: (1, 7, 2), 1: (5,), 2: (4,), 3: (10, 6), 4: (11,), 5: (8, 9), 7: (3,)},
    {0: (1, 2, 6), 1: (5,), 2: (4,), 3: (7, 10), 4: (11,), 5: (8, 9), 6: (3,)},
)
GROUP = 2
ROOT_FIRST = 3
ROOT_ORDER = ((0, 1), (0, 2), (0, 7), (2, 6), (1, 1), (1, 2), (1, 7), (2, 1), (2, 2))
PAIRED = frozenset((0, 1, 2, 3, 4, 5, 6, 7, 9, 10))
SEGMENTS = (
    (
        (('i',), ('f', 1, 0, 0), ('f', 2, 0, 0), ('f', 6, 2, 0), ('f', 7, 0, 0), ('j',), ('d', 0)),
        ((0, 0), (0, 0)),
        (),
    ),
    (
        (('f', 1, 1, 0), ('f', 2, 1, 0), ('f', 7, 1, 0), ('f', 3, 0, 0), ('f', 4, 0, 0), ('f', 5, 0, 0), ('f', 1, 2, 1), ('f', 2, 2, 1), ('f', 3, 2, 0)),
        ((1, 0), (2, 0)),
        (),
    ),
    (
        (('f', 3, 1, 1), ('f', 4, 1, 0), ('f', 5, 1, 0)),
        ((3, 0), (3, 0)),
        (),
    ),
    (
        (('d', 1), ('d', 2)),
        ((3, 1), (3, 2), (2, 1), (2, 1)),
        (),
    ),
    (
        (('f', 6, 0, 0), ('f', 8, 0, 0), ('f', 9, 0, 0), ('f', 4, 2, 1), ('f', 5, 2, 1), ('f', 10, 0, 0), ('d', 3)),
        ((4, 1), (4, 3), (5, 1), (5, 3), (5, 0), (5, 2)),
        (),
    ),
    (
        (('f', 6, 1, 1), ('f', 8, 1, 0), ('f', 9, 1, 0), ('d', 4), ('d', 5)),
        ((5, 4), (6, 5)),
        (),
    ),
    (
        (('f', 7, 2, 1), ('f', 10, 1, 0), ('f', 11, 0, 0)),
        ((6, 4), (7, 1)),
        (),
    ),
    (
        (('d', 6),),
        ((7, 6), (7, 2), (7, 4), (7, 4)),
        (),
    ),
    (
        (('f', 8, 2, 1), ('f', 9, 2, 1)),
        ((8, 3), (8, 0), (8, 6), (8, 4)),
        (),
    ),
    (
        (('f', 10, 2, 1), ('f', 11, 1, 0), ('d', 7)),
        ((8, 7), (9, 6), (9, 4), (9, 2), (10, 0), (10, 4)),
        (),
    ),
    (
        (('d', 9),),
        ((10, 9), (10, 2)),
        (),
    ),
    (
        (('f', 11, 2, 1),),
        ((10, 7), (11, 2)),
        (),
    ),
    (
        (('d', 10),),
        ((11, 7), (11, 10)),
        (0, 1, 2, 3, 4, 5, 6, 7, 8, 9, 10, 11),
    ),
)

MESH = pl.DeviceIdType.MESH
NSLOT = len(SOURCES)
NPART = len(PARTS)
NSEG = len(SEGMENTS)
LEFTS = [p for _, items, _ in SEGMENTS for p, _ in items]
RIGHTS = [q for _, items, _ in SEGMENTS for _, q in items]
BACKS = [slot for _, _, slots in SEGMENTS for slot in slots]
PAD = 256


def packed(digits, index):
    word = jnp.int32(0)
    for k in range(0, len(digits), 8):
        value = sum(d << (4 * j) for j, d in enumerate(digits[k : k + 8]))
        value = value - (1 << 32) if value >> 31 else value
        word = jnp.where(index // 8 == k // 8, jnp.int32(value), word)
    return lax.shift_right_logical(word, 4 * (index % 8)) & 15


def start_of(seg, column):
    first = jnp.int32(0)
    for k, segment in enumerate(SEGMENTS):
        if segment[column]:
            first = first + jnp.where(seg > k, len(segment[column]), 0)
    return first


def gray(code):
    return code ^ ((code >> 1) & 21)


def turned(turn, word):
    return sum(1 << TURNS[turn][k] for k in range(6) if word >> k & 1)


def kernel(
    x_hbm, c_hbm, o_ref, x_ref, c_ref, own, other, ids, ids_out, id_col, side, best, back, back_out, swap_out,
    swap, load_sem, row_send, row_recv, pair_send, pair_recv, id_send, id_recv, back_send, back_recv, swap_sem,
):
    core = lax.axis_index("gx")
    place = lax.axis_index("gy")
    half = x_ref.shape[0]

    loads = [
        pltpu.make_async_copy(
            x_hbm.at[pl.ds(begin, size)], x_ref.at[pl.ds(begin, size)], load_sem.at[part]
        )
        for part, (begin, size) in enumerate(PARTS)
    ]
    loads.append(pltpu.make_async_copy(c_hbm, c_ref, load_sem.at[NPART]))
    for load in loads:
        load.start()

    corner = gray(place)
    turn = packed(TURN_OF, corner)

    def chip(word):
        values = [turned(t, word) for t in range(len(TURNS))]
        there = jnp.int32(values[0])
        for value in sorted(set(values) - {values[0]}):
            hits = turn < 0
            for t, v in enumerate(values):
                if v == value:
                    hits = hits | (turn == t)
            there = jnp.where(hits, value, there)
        return gray(corner ^ there)

    chips = {word: chip(word) for word in GREETED}
    source = [chips.get(w) for w in SOURCES]
    holder = [chips.get(w) for w in HOLDERS]
    step_to = [chips[1 << k] for k in range(6)]

    barrier = pltpu.get_barrier_semaphore()
    for word in GREETED:
        pl.semaphore_signal(barrier, inc=1, device_id=(core, chips[word]), device_id_type=MESH)
    pl.semaphore_signal(barrier, inc=1, device_id=(1 - core, place), device_id_type=MESH)

    for part, (begin, size) in enumerate(PARTS):
        loads[part].wait()
        values = x_ref[begin : begin + size, :].astype(jnp.float32)
        total = jnp.sum(values * values, axis=1, keepdims=True)
        own[0, begin : begin + size, :] = (values * lax.rsqrt(total + EPS)).astype(jnp.bfloat16)
    loads[NPART].wait()
    cluster = c_ref[...].astype(jnp.float32)
    ids_out[...] = jnp.concatenate([cluster, jnp.full((1, PAD - half), -2.0, jnp.float32)], axis=1)
    ids[0, 0] = ids_out[...]

    pl.semaphore_wait(barrier, len(GREETED) + 1)

    def id_copy(slot):
        return pltpu.make_async_remote_copy(
            src_ref=ids_out,
            dst_ref=ids.at[0, slot],
            send_sem=id_send.at[slot],
            recv_sem=id_recv.at[slot],
            device_id=(core, holder[slot]),
            device_id_type=MESH,
        )

    def id_pair_copy():
        return pltpu.make_async_remote_copy(
            src_ref=ids.at[0],
            dst_ref=ids.at[1],
            send_sem=id_send.at[0],
            recv_sem=id_recv.at[0],
            device_id=(1 - core, place),
            device_id_type=MESH,
        )

    def back_copy(slot, where):
        return pltpu.make_async_remote_copy(
            src_ref=back_out.at[slot],
            dst_ref=back.at[slot],
            send_sem=back_send.at[slot],
            recv_sem=back_recv.at[slot],
            device_id=(core, where),
            device_id_type=MESH,
        )

    def row_copy(part, slot):
        begin, size = PARTS[part]
        parent, step = TREES[part][slot]
        return pltpu.make_async_remote_copy(
            src_ref=own.at[parent, pl.ds(begin, size)],
            dst_ref=own.at[slot, pl.ds(begin, size)],
            send_sem=row_send.at[slot, part],
            recv_sem=row_recv.at[slot, part],
            device_id=(core, step_to[step]),
            device_id_type=MESH,
        )

    def pair_copy(slot):
        return pltpu.make_async_remote_copy(
            src_ref=own.at[slot, pl.ds(0, half)],
            dst_ref=other.at[slot],
            send_sem=pair_send.at[slot],
            recv_sem=pair_recv.at[slot],
            device_id=(1 - core, place),
            device_id_type=MESH,
        )

    for part, slot in ROOT_ORDER[:ROOT_FIRST]:
        row_copy(part, slot).start()
    for slot in range(1, NSLOT):
        id_copy(slot).start()
    for part, slot in ROOT_ORDER[ROOT_FIRST:]:
        row_copy(part, slot).start()
    pair_copy(0).start()

    best[...] = jnp.full(best.shape, -1.0, jnp.float32)
    side[...] = jnp.full(side.shape, -1.0, jnp.float32)
    for slot in range(NSLOT):
        own[slot, half:PAD, :] = jnp.zeros((PAD - half, own.shape[2]), own.dtype)

    def forward(slot, part, last):
        row_copy(part, slot).wait_recv()
        for child in CHILDREN[part].get(slot, ()):
            row_copy(part, child).start()
        if last and slot in PAIRED:
            pair_copy(slot).start()

    def send_ids():
        for slot in range(1, NSLOT):
            id_copy(slot).wait_recv()
        id_pair_copy().start()

    def take_ids():
        id_pair_copy().wait_recv()

        def turn_ids(slot, carry):
            for which in range(2):
                column = jnp.broadcast_to(ids[which, slot], (128, PAD)).T
                id_col[slot, which * half : (which + 1) * half, :] = column[:half]
            return carry

        lax.fori_loop(0, NSLOT, turn_ids, 0)

    def give_back(index, carry):
        slot = packed(BACKS, index)
        turned_side = jnp.max(side[slot].T.reshape(128 // 8, 8, 2 * PAD), axis=0)
        back_out[slot, 0] = jnp.max(jnp.maximum(best[slot], turned_side[:, :PAD]), axis=0, keepdims=True)
        back_out[slot, 1] = jnp.max(turned_side[:, PAD:], axis=0, keepdims=True)
        where = source[1]
        for k in range(2, NSLOT):
            where = jnp.where(slot == k, source[k], where)

        @pl.when(slot > 0)
        def _():
            back_copy(slot, where).start()

        return carry

    def multiply(index, carry):
        pairs = [
            (packed(LEFTS, GROUP * index + u), packed(RIGHTS, GROUP * index + u)) for u in range(GROUP)
        ]
        products = [
            lax.dot_general(
                jnp.concatenate([own[q, :half, :], other[q]], axis=0),
                own[p],
                (((1,), (1,)), ((), ())),
                preferred_element_type=jnp.float32,
            )
            for p, q in pairs
        ]
        for (p, q), product in zip(pairs, products):
            left_id = id_col[q]
            row = lax.broadcasted_iota(jnp.int32, (2 * half, 128), 0) + jnp.where(p == q, 0, 4 * PAD)
            column = lax.broadcasted_iota(jnp.int32, (2 * half, 128), 1)
            row_best = None
            for k in range(PAD // 128):
                lanes = slice(128 * k, 128 * k + 128)
                allowed = (left_id == ids[0, p, :, lanes]) & (row != column + 128 * k)
                masked = jnp.where(allowed, product[:, lanes], -1.0)
                row_best = masked if row_best is None else jnp.maximum(row_best, masked)
                best[p, :, lanes] = jnp.maximum(
                    best[p, :, lanes], jnp.max(masked.reshape(half // 4, 8, 128), axis=0)
                )
            side[q, :half, :] = jnp.maximum(side[q, :half, :], row_best[:half])
            side[q, PAD : PAD + half, :] = jnp.maximum(side[q, PAD : PAD + half, :], row_best[half:])
        return carry

    actions = {
        "f": forward,
        "d": lambda slot: pair_copy(slot).wait_recv(),
        "i": send_ids,
        "j": take_ids,
    }

    def segment(seg, carry):
        for k, (events, _, _) in enumerate(SEGMENTS):
            if events:

                @pl.when(seg == k)
                def _():
                    for name, *where in events:
                        actions[name](*where)

        lax.fori_loop(start_of(seg, 1) // GROUP, start_of(seg + 1, 1) // GROUP, multiply, carry)
        return lax.fori_loop(start_of(seg, 2), start_of(seg + 1, 2), give_back, carry)

    lax.fori_loop(0, NSEG, segment, 0)

    result = back_out[0]
    for slot in range(1, NSLOT):
        back_copy(slot, source[slot]).wait_recv()
        result = jnp.maximum(result, back[slot])
    swap_out[...] = result[1]
    swapping = pltpu.make_async_remote_copy(
        src_ref=swap_out,
        dst_ref=swap,
        send_sem=swap_sem.at[0],
        recv_sem=swap_sem.at[1],
        device_id=(1 - core, place),
        device_id_type=MESH,
    )
    swapping.start()

    for part in range(NPART):
        for slot in range(1, NSLOT):
            row_copy(part, slot).wait_send()
    for slot in sorted(PAIRED):
        pair_copy(slot).wait_send()
    id_pair_copy().wait_send()
    for slot in range(1, NSLOT):
        id_copy(slot).wait_send()
        back_copy(slot, source[slot]).wait_send()
    swapping.wait()
    o_ref[...] = jnp.maximum(result[0], swap[...])[:, :half]


def local(embeddings, cluster):
    half, width = embeddings.shape
    best = pl.pallas_call(
        kernel,
        out_shape=jax.ShapeDtypeStruct((1, half), jnp.float32),
        in_specs=[pl.BlockSpec(memory_space=pl.ANY)] * 2,
        out_specs=pl.BlockSpec(memory_space=pltpu.VMEM),
        scratch_shapes=[
            pltpu.VMEM((half, width), jnp.bfloat16),
            pltpu.VMEM((1, half), jnp.int32),
            pltpu.VMEM((NSLOT, PAD, width), jnp.bfloat16),
            pltpu.VMEM((NSLOT, half, width), jnp.bfloat16),
            pltpu.VMEM((2, NSLOT, 1, PAD), jnp.float32),
            pltpu.VMEM((1, PAD), jnp.float32),
            pltpu.VMEM((NSLOT, 2 * half, 128), jnp.float32),
            pltpu.VMEM((NSLOT, 2 * PAD, 128), jnp.float32),
            pltpu.VMEM((NSLOT, 8, PAD), jnp.float32),
            pltpu.VMEM((NSLOT, 2, 1, PAD), jnp.float32),
            pltpu.VMEM((NSLOT, 2, 1, PAD), jnp.float32),
            pltpu.VMEM((1, PAD), jnp.float32),
            pltpu.VMEM((1, PAD), jnp.float32),
            pltpu.SemaphoreType.DMA((NPART + 1,)),
            pltpu.SemaphoreType.DMA((NSLOT, NPART)),
            pltpu.SemaphoreType.DMA((NSLOT, NPART)),
            pltpu.SemaphoreType.DMA((NSLOT,)),
            pltpu.SemaphoreType.DMA((NSLOT,)),
            pltpu.SemaphoreType.DMA((NSLOT,)),
            pltpu.SemaphoreType.DMA((NSLOT,)),
            pltpu.SemaphoreType.DMA((NSLOT,)),
            pltpu.SemaphoreType.DMA((NSLOT,)),
            pltpu.SemaphoreType.DMA((2,)),
        ],
        compiler_params=pltpu.CompilerParams(
            collective_id=0, has_side_effects=True, vmem_limit_bytes=56 * 1024 * 1024
        ),
        cost_estimate=pl.CostEstimate(
            flops=4 * len(LEFTS) * half * half * width, bytes_accessed=2 * half * width, transcendentals=half
        ),
    )(embeddings, cluster.reshape(1, half))
    return best.reshape(half)


def solution(mesh):
    return jax.shard_map(
        local,
        mesh=mesh,
        in_specs=(P(("gx", "gy"), None), P(("gx", "gy"))),
        out_specs=P(("gx", "gy")),
        check_vma=False,
    )
```

```python
import jax
import jax.numpy as jnp
from jax import lax
from jax.experimental import pallas as pl
from jax.experimental.pallas import tpu as pltpu
from jax.sharding import PartitionSpec as P

EPS = 1e-06
TURNS = (
    (0, 1, 2, 3, 4, 5),
    (0, 1, 2, 3, 5, 4),
    (0, 1, 3, 2, 4, 5),
    (0, 1, 3, 2, 5, 4),
    (1, 0, 2, 3, 4, 5),
    (1, 0, 2, 3, 5, 4),
    (1, 0, 3, 2, 4, 5),
    (1, 0, 3, 2, 5, 4),
)
TURN_OF = [0, 4, 4, 0, 2, 6, 6, 2, 2, 6, 6, 2, 0, 4, 4, 0, 1, 5, 5, 1, 3, 7, 7, 3, 3, 7, 7, 3, 1, 5, 5, 1, 1, 5, 5, 1, 3, 7, 7, 3, 3, 7, 7, 3, 1, 5, 5, 1, 0, 4, 4, 0, 2, 6, 6, 2, 2, 6, 6, 2, 0, 4, 4, 0]
HOLDERS = (0, 8, 1, 2, 16, 40, 6, 3, 7, 48, 44, 60)
SOURCES = (0, 4, 2, 1, 32, 20, 9, 3, 11, 48, 28, 60)
GREETED = (1, 2, 3, 4, 6, 7, 8, 9, 11, 16, 20, 28, 32, 40, 44, 48, 60)
PARTS = ((0, 64), (64, 64), (128, 64))
TREES = (
    {1: (0, 3), 2: (0, 0), 3: (0, 1), 4: (0, 4), 5: (1, 5), 6: (3, 2), 7: (3, 1), 8: (7, 2), 9: (4, 4), 10: (5, 3), 11: (10, 5)},
    {1: (0, 3), 2: (0, 0), 3: (0, 1), 4: (0, 4), 5: (1, 5), 6: (3, 2), 7: (2, 0), 8: (6, 1), 9: (4, 4), 10: (5, 3), 11: (10, 5)},
    {1: (0, 3), 2: (0, 0), 3: (0, 1), 4: (0, 4), 5: (1, 5), 6: (3, 2), 7: (2, 0), 8: (6, 1), 9: (4, 4), 10: (5, 3), 11: (10, 5)},
)
CHILDREN = (
    {0: (1, 3, 4, 2), 1: (5,), 3: (7, 6), 4: (9,), 5: (10,), 7: (8,), 10: (11,)},
    {0: (1, 3, 2, 4), 1: (5,), 2: (7,), 3: (6,), 4: (9,), 5: (10,), 6: (8,), 10: (11,)},
    {0: (1, 3, 2, 4), 1: (5,), 2: (7,), 3: (6,), 4: (9,), 5: (10,), 6: (8,), 10: (11,)},
)
GROUP = 2
ROOT_FIRST = 4
ROOT_ORDER = ((0, 1), (0, 3), (0, 4), (1, 2), (1, 1), (1, 3), (1, 4), (2, 2), (0, 2), (2, 1), (2, 3), (2, 4))
PAIRED = frozenset((0, 1, 2, 3, 4, 5, 6, 7, 8, 9))
SEGMENTS = (
    (
        (('i',), ('f', 1, 0, 0), ('f', 2, 1, 0), ('f', 3, 0, 0), ('f', 4, 0, 0), ('j',), ('d', 0), ('s',), ('f', 1, 1, 0), ('f', 2, 2, 0), ('f', 3, 1, 0), ('f', 4, 1, 0), ('f', 5, 0, 0), ('f', 6, 0, 0), ('f', 1, 2, 1), ('f', 2, 0, 1), ('f', 3, 2, 1), ('f', 4, 2, 1)),
        (1,),
        ((1, 0, 0),),
        (),
    ),
    (
        (('f', 5, 1, 0), ('f', 6, 1, 0), ('d', 1)),
        (2,),
        ((2, 0, 1),),
        (),
    ),
    (
        (('d', 2),),
        (3,),
        ((3, 1, 2),),
        (),
    ),
    (
        (('f', 7, 0, 0), ('f', 7, 1, 0), ('f', 9, 0, 0), ('f', 10, 0, 0), ('d', 3)),
        (4,),
        ((4, 3, 0),),
        (),
    ),
    (
        (('f', 5, 2, 1), ('f', 6, 2, 1)),
        (),
        ((4, 1, 2),),
        (),
    ),
    (
        (),
        (5,),
        ((5, 3, 2),),
        (),
    ),
    (
        (('f', 7, 2, 1), ('f', 8, 1, 0), ('f', 9, 1, 0), ('f', 10, 1, 0)),
        (6,),
        ((6, 1, 2),),
        (),
    ),
    (
        (('f', 8, 0, 0), ('f', 11, 0, 0), ('d', 5), ('d', 4)),
        (),
        ((6, 5, 4),),
        (),
    ),
    (
        (),
        (7,),
        ((7, 5, 4),),
        (),
    ),
    (
        (('f', 8, 2, 1), ('f', 9, 2, 1), ('f', 10, 2, 1)),
        (8,),
        ((8, 1, 5),),
        (),
    ),
    (
        (('f', 11, 1, 0), ('d', 8)),
        (9,),
        ((9, 5, 8),),
        (),
    ),
    (
        (('d', 7),),
        (),
        ((9, 0, 7),),
        (),
    ),
    (
        (('d', 6),),
        (),
        ((9, 2, 6),),
        (),
    ),
    (
        (('f', 11, 2, 1),),
        (10,),
        ((10, 0, 2), (10, 6, 4)),
        (),
    ),
    (
        (),
        (11,),
        ((11, 2, 6),),
        (),
    ),
    (
        (('d', 9),),
        (),
        ((11, 7, 9), (5, 4, 4), (8, 4, 4)),
        (1, 2, 3, 4, 5, 6, 7, 8, 0, 9, 10, 11),
    ),
)

MESH = pl.DeviceIdType.MESH
NSLOT = len(SOURCES)
NPART = len(PARTS)
NSEG = len(SEGMENTS)
TURNED = [slot for _, slots, _, _ in SEGMENTS for slot in slots]
LEFTS = [group[0] for _, _, groups, _ in SEGMENTS for group in groups]
RIGHTS = [[group[1 + u] for _, _, groups, _ in SEGMENTS for group in groups] for u in range(GROUP)]
BACKS = [slot for _, _, _, slots in SEGMENTS for slot in slots]
BACK_GROUP = 4
PAD = 256


def packed(digits, index):
    word = jnp.int32(0)
    for k in range(0, len(digits), 8):
        value = sum(d << (4 * j) for j, d in enumerate(digits[k : k + 8]))
        value = value - (1 << 32) if value >> 31 else value
        word = jnp.where(index // 8 == k // 8, jnp.int32(value), word)
    return lax.shift_right_logical(word, 4 * (index % 8)) & 15


def start_of(seg, column):
    first = jnp.int32(0)
    for k, segment in enumerate(SEGMENTS):
        if segment[column]:
            first = first + jnp.where(seg > k, len(segment[column]), 0)
    return first


def gray(code):
    return code ^ ((code >> 1) & 21)


def turned(turn, word):
    return sum(1 << TURNS[turn][k] for k in range(6) if word >> k & 1)


def kernel(
    x_hbm, c_hbm, o_ref, x_ref, c_ref, own, other, across, ids, ids_out, id_col, side, best, back, back_out, swap_out,
    swap, load_sem, row_send, row_recv, pair_send, pair_recv, id_send, id_recv, back_send, back_recv, swap_sem,
):
    core = lax.axis_index("gx")
    place = lax.axis_index("gy")
    half = x_ref.shape[0]

    loads = [
        pltpu.make_async_copy(
            x_hbm.at[pl.ds(begin, size)], x_ref.at[pl.ds(begin, size)], load_sem.at[part]
        )
        for part, (begin, size) in enumerate(PARTS)
    ]
    loads.append(pltpu.make_async_copy(c_hbm, c_ref, load_sem.at[NPART]))
    for load in loads:
        load.start()

    corner = gray(place)
    turn = packed(TURN_OF, corner)

    def chip(word):
        values = [turned(t, word) for t in range(len(TURNS))]
        there = jnp.int32(values[0])
        for value in sorted(set(values) - {values[0]}):
            hits = turn < 0
            for t, v in enumerate(values):
                if v == value:
                    hits = hits | (turn == t)
            there = jnp.where(hits, value, there)
        return gray(corner ^ there)

    chips = {word: chip(word) for word in GREETED}
    source = [chips.get(w) for w in SOURCES]
    holder = [chips.get(w) for w in HOLDERS]
    step_to = [chips[1 << k] for k in range(6)]

    barrier = pltpu.get_barrier_semaphore()
    for word in GREETED:
        pl.semaphore_signal(barrier, inc=1, device_id=(core, chips[word]), device_id_type=MESH)
    pl.semaphore_signal(barrier, inc=1, device_id=(1 - core, place), device_id_type=MESH)

    for slot in range(NSLOT):
        own[slot, half:PAD, :] = jnp.zeros((PAD - half, own.shape[2]), own.dtype)

    for part, (begin, size) in enumerate(PARTS):
        loads[part].wait()
        values = x_ref[begin : begin + size, :].astype(jnp.float32)
        total = jnp.sum(values * values, axis=1, keepdims=True)
        own[0, begin : begin + size, :] = (values * lax.rsqrt(total + EPS)).astype(jnp.bfloat16)
    loads[NPART].wait()
    cluster = c_ref[...].astype(jnp.float32)
    ids_out[...] = jnp.concatenate([cluster, jnp.full((1, PAD - half), -2.0, jnp.float32)], axis=1)
    ids[0, 0] = ids_out[...]
    back_out[...] = jnp.full(back_out.shape, -1.0, jnp.float32)

    pl.semaphore_wait(barrier, len(GREETED) + 1)

    def id_copy(slot):
        return pltpu.make_async_remote_copy(
            src_ref=ids_out,
            dst_ref=ids.at[0, slot],
            send_sem=id_send.at[slot],
            recv_sem=id_recv.at[slot],
            device_id=(core, holder[slot]),
            device_id_type=MESH,
        )

    def id_pair_copy():
        return pltpu.make_async_remote_copy(
            src_ref=ids.at[0],
            dst_ref=ids.at[1],
            send_sem=id_send.at[0],
            recv_sem=id_recv.at[0],
            device_id=(1 - core, place),
            device_id_type=MESH,
        )

    def back_copy(slot, where):
        return pltpu.make_async_remote_copy(
            src_ref=back_out.at[slot],
            dst_ref=back.at[slot],
            send_sem=back_send.at[slot],
            recv_sem=back_recv.at[slot],
            device_id=(core, where),
            device_id_type=MESH,
        )

    def row_copy(part, slot):
        begin, size = PARTS[part]
        parent, step = TREES[part][slot]
        return pltpu.make_async_remote_copy(
            src_ref=own.at[parent, pl.ds(begin, size)],
            dst_ref=own.at[slot, pl.ds(begin, size)],
            send_sem=row_send.at[slot, part],
            recv_sem=row_recv.at[slot, part],
            device_id=(core, step_to[step]),
            device_id_type=MESH,
        )

    def pair_copy(slot):
        return pltpu.make_async_remote_copy(
            src_ref=own.at[slot, pl.ds(0, half)],
            dst_ref=other.at[slot],
            send_sem=pair_send.at[slot],
            recv_sem=pair_recv.at[slot],
            device_id=(1 - core, place),
            device_id_type=MESH,
        )

    for part, slot in ROOT_ORDER[:ROOT_FIRST]:
        row_copy(part, slot).start()
    for slot in range(1, NSLOT):
        id_copy(slot).start()
    for part, slot in ROOT_ORDER[ROOT_FIRST:]:
        row_copy(part, slot).start()
    pair_copy(0).start()

    across[0] = own[0].T
    best[...] = jnp.full(best.shape, -1.0, jnp.float32)
    side[...] = jnp.full(side.shape, -1.0, jnp.float32)

    def forward(slot, part, last):
        row_copy(part, slot).wait_recv()
        for child in CHILDREN[part].get(slot, ()):
            row_copy(part, child).start()
        if last and slot in PAIRED:
            pair_copy(slot).start()

    def send_ids():
        for slot in range(1, NSLOT):
            id_copy(slot).wait_recv()
        id_pair_copy().start()

    def take_ids():
        id_pair_copy().wait_recv()

        def turn_ids(slot, carry):
            for which in range(2):
                column = jnp.broadcast_to(ids[which, slot], (128, PAD)).T
                id_col[slot, which * half : (which + 1) * half, :] = column[:half]
            return carry

        lax.fori_loop(0, NSLOT, turn_ids, 0)

    def give_back(index, carry):
        slots = [packed(BACKS, BACK_GROUP * index + u) for u in range(BACK_GROUP)]
        for slot in slots:
            turned_side = jnp.max(side[slot].T.reshape(128 // 8, 8, 2 * half), axis=0)
            turned_side = jnp.max(turned_side, axis=0, keepdims=True)
            high = jnp.max(best[slot], axis=0, keepdims=True)
            back_out[slot, 0, :, :half] = jnp.maximum(high[:, :half], turned_side[:, :half])
            back_out[slot, 1, :, :half] = turned_side[:, half:]
        for slot in slots:
            where = source[1]
            for k in range(2, NSLOT):
                where = jnp.where(slot == k, source[k], where)

            @pl.when(slot > 0)
            def _():
                back_copy(slot, where).start()

        return carry

    def turn_rows(index, carry):
        slot = packed(TURNED, index)
        across[slot] = own[slot].T
        return carry

    def products_of(p, qs, same):
        left = jnp.concatenate([part for q in qs for part in (own[q, :half, :], other[q])], axis=0)
        products = jnp.dot(left, across[p], preferred_element_type=jnp.float32)
        highest = [best[p, :, 128 * k : 128 * k + 128] for k in range(PAD // 128)]
        for u, q in enumerate(qs):
            left_id = id_col[q]
            row_best = None
            for k in range(PAD // 128):
                lanes = slice(128 * k, 128 * k + 128)
                allowed = left_id == ids[0, p, :, lanes]
                if same:
                    row = lax.broadcasted_iota(jnp.int32, (2 * half, 128), 0)
                    column = lax.broadcasted_iota(jnp.int32, (2 * half, 128), 1) + 128 * k
                    allowed = allowed & (row != column)
                masked = jnp.where(allowed, products[2 * half * u : 2 * half * (u + 1), lanes], -1.0)
                row_best = masked if row_best is None else jnp.maximum(row_best, masked)
                highest[k] = jnp.maximum(
                    highest[k], jnp.max(masked.reshape(half // 4, 8, 128), axis=0)
                )
            side[q] = jnp.maximum(side[q], row_best)
        for k in range(PAD // 128):
            best[p, :, 128 * k : 128 * k + 128] = highest[k]

    def multiply(index, carry):
        products_of(packed(LEFTS, index), [packed(rights, index) for rights in RIGHTS], False)
        return carry

    actions = {
        "f": forward,
        "d": lambda slot: pair_copy(slot).wait_recv(),
        "i": send_ids,
        "j": take_ids,
        "s": lambda: products_of(0, [0], True),
    }

    def segment(seg, carry):
        for k, (events, _, _, _) in enumerate(SEGMENTS):
            if events:

                @pl.when(seg == k)
                def _():
                    for name, *where in events:
                        actions[name](*where)

        lax.fori_loop(start_of(seg, 1), start_of(seg + 1, 1), turn_rows, carry)
        lax.fori_loop(start_of(seg, 2), start_of(seg + 1, 2), multiply, carry)
        first, end = start_of(seg, 3) // BACK_GROUP, start_of(seg + 1, 3) // BACK_GROUP
        return lax.fori_loop(first, end, give_back, carry)

    lax.fori_loop(0, NSEG, segment, 0)

    result = back_out[0]
    for slot in range(1, NSLOT):
        back_copy(slot, source[slot]).wait_recv()
        result = jnp.maximum(result, back[slot])
    swap_out[...] = result[1]
    swapping = pltpu.make_async_remote_copy(
        src_ref=swap_out,
        dst_ref=swap,
        send_sem=swap_sem.at[0],
        recv_sem=swap_sem.at[1],
        device_id=(1 - core, place),
        device_id_type=MESH,
    )
    swapping.start()

    for part in range(NPART):
        for slot in range(1, NSLOT):
            row_copy(part, slot).wait_send()
    for slot in sorted(PAIRED):
        pair_copy(slot).wait_send()
    id_pair_copy().wait_send()
    for slot in range(1, NSLOT):
        id_copy(slot).wait_send()
        back_copy(slot, source[slot]).wait_send()
    swapping.wait()
    o_ref[...] = jnp.maximum(result[0], swap[...])[:, :half]


def local(embeddings, cluster):
    half, width = embeddings.shape
    best = pl.pallas_call(
        kernel,
        out_shape=jax.ShapeDtypeStruct((1, half), jnp.float32),
        in_specs=[pl.BlockSpec(memory_space=pl.ANY)] * 2,
        out_specs=pl.BlockSpec(memory_space=pltpu.VMEM),
        scratch_shapes=[
            pltpu.VMEM((half, width), jnp.bfloat16),
            pltpu.VMEM((1, half), jnp.int32),
            pltpu.VMEM((NSLOT, PAD, width), jnp.bfloat16),
            pltpu.VMEM((NSLOT, half, width), jnp.bfloat16),
            pltpu.VMEM((NSLOT, width, PAD), jnp.bfloat16),
            pltpu.VMEM((2, NSLOT, 1, PAD), jnp.float32),
            pltpu.VMEM((1, PAD), jnp.float32),
            pltpu.VMEM((NSLOT, 2 * half, 128), jnp.float32),
            pltpu.VMEM((NSLOT, 2 * half, 128), jnp.float32),
            pltpu.VMEM((NSLOT, 8, PAD), jnp.float32),
            pltpu.VMEM((NSLOT, 2, 1, PAD), jnp.float32),
            pltpu.VMEM((NSLOT, 2, 1, PAD), jnp.float32),
            pltpu.VMEM((1, PAD), jnp.float32),
            pltpu.VMEM((1, PAD), jnp.float32),
            pltpu.SemaphoreType.DMA((NPART + 1,)),
            pltpu.SemaphoreType.DMA((NSLOT, NPART)),
            pltpu.SemaphoreType.DMA((NSLOT, NPART)),
            pltpu.SemaphoreType.DMA((NSLOT,)),
            pltpu.SemaphoreType.DMA((NSLOT,)),
            pltpu.SemaphoreType.DMA((NSLOT,)),
            pltpu.SemaphoreType.DMA((NSLOT,)),
            pltpu.SemaphoreType.DMA((NSLOT,)),
            pltpu.SemaphoreType.DMA((NSLOT,)),
            pltpu.SemaphoreType.DMA((2,)),
        ],
        compiler_params=pltpu.CompilerParams(
            collective_id=0, has_side_effects=True, vmem_limit_bytes=56 * 1024 * 1024
        ),
        cost_estimate=pl.CostEstimate(
            flops=4 * GROUP * len(LEFTS) * half * half * width, bytes_accessed=2 * half * width, transcendentals=half
        ),
    )(embeddings, cluster.reshape(1, half))
    return best.reshape(half)


def solution(mesh):
    return jax.shard_map(
        local,
        mesh=mesh,
        in_specs=(P(("gx", "gy"), None), P(("gx", "gy"))),
        out_specs=P(("gx", "gy")),
        check_vma=False,
    )
```

```python
import jax
import jax.numpy as jnp
from jax import lax
from jax.experimental import pallas as pl
from jax.experimental.pallas import tpu as pltpu
from jax.sharding import PartitionSpec as P

EPS = 1e-06
TURNS = (
    (0, 1, 2, 3, 4, 5),
    (0, 1, 2, 3, 5, 4),
    (0, 1, 3, 2, 4, 5),
    (0, 1, 3, 2, 5, 4),
    (1, 0, 2, 3, 4, 5),
    (1, 0, 2, 3, 5, 4),
    (1, 0, 3, 2, 4, 5),
    (1, 0, 3, 2, 5, 4),
)
TURN_OF = [0, 4, 4, 0, 2, 6, 6, 2, 2, 6, 6, 2, 0, 4, 4, 0, 1, 5, 5, 1, 3, 7, 7, 3, 3, 7, 7, 3, 1, 5, 5, 1, 1, 5, 5, 1, 3, 7, 7, 3, 3, 7, 7, 3, 1, 5, 5, 1, 0, 4, 4, 0, 2, 6, 6, 2, 2, 6, 6, 2, 0, 4, 4, 0]
HOLDERS = (0, 8, 1, 2, 16, 40, 6, 3, 7, 48, 44, 60)
SOURCES = (0, 4, 2, 1, 32, 20, 9, 3, 11, 48, 28, 60)
GREETED = (1, 2, 3, 4, 6, 7, 8, 9, 11, 16, 20, 28, 32, 40, 44, 48, 60)
PARTS = ((0, 64), (64, 64), (128, 64))
TREES = (
    {1: (0, 3), 2: (0, 0), 3: (0, 1), 4: (0, 4), 5: (1, 5), 6: (3, 2), 7: (3, 1), 8: (7, 2), 9: (4, 4), 10: (5, 3), 11: (10, 5)},
    {1: (0, 3), 2: (0, 0), 3: (0, 1), 4: (0, 4), 5: (1, 5), 6: (3, 2), 7: (2, 0), 8: (6, 1), 9: (4, 4), 10: (5, 3), 11: (10, 5)},
    {1: (0, 3), 2: (0, 0), 3: (0, 1), 4: (0, 4), 5: (1, 5), 6: (3, 2), 7: (2, 0), 8: (6, 1), 9: (4, 4), 10: (5, 3), 11: (10, 5)},
)
CHILDREN = (
    {0: (1, 3, 4, 2), 1: (5,), 3: (7, 6), 4: (9,), 5: (10,), 7: (8,), 10: (11,)},
    {0: (1, 3, 2, 4), 1: (5,), 2: (7,), 3: (6,), 4: (9,), 5: (10,), 6: (8,), 10: (11,)},
    {0: (1, 3, 2, 4), 1: (5,), 2: (7,), 3: (6,), 4: (9,), 5: (10,), 6: (8,), 10: (11,)},
)
GROUP = 2
ROOT_FIRST = 4
ROOT_ORDER = ((0, 1), (0, 3), (0, 4), (1, 2), (1, 1), (1, 3), (1, 4), (2, 2), (0, 2), (2, 1), (2, 3), (2, 4))
PAIRED = frozenset((0, 1, 2, 3, 4, 5, 6, 7, 8, 9))
SEGMENTS = (
    (
        (('i',), ('j',), ('f', 1, 0, 0), ('f', 2, 1, 0), ('f', 3, 0, 0), ('f', 4, 0, 0), ('d', 0), ('s',), ('f', 1, 1, 0), ('f', 2, 2, 0), ('f', 3, 1, 0), ('f', 4, 1, 0), ('f', 5, 0, 0), ('f', 6, 0, 0), ('f', 1, 2, 1), ('f', 2, 0, 1), ('f', 3, 2, 1), ('f', 4, 2, 1)),
        ((1, 0, 0),),
        (),
    ),
    (
        (('f', 5, 1, 0), ('f', 6, 1, 0), ('d', 1)),
        ((2, 0, 1),),
        (),
    ),
    (
        (('d', 2),),
        ((3, 1, 2),),
        (),
    ),
    (
        (('d', 3),),
        ((4, 3, 0),),
        (),
    ),
    (
        (('f', 7, 0, 0), ('f', 7, 1, 0), ('f', 9, 0, 0), ('f', 10, 0, 0)),
        ((4, 1, 2),),
        (),
    ),
    (
        (('f', 5, 2, 1), ('f', 6, 2, 1)),
        ((5, 3, 2), (6, 1, 2)),
        (),
    ),
    (
        (('d', 5), ('d', 4)),
        ((6, 5, 4),),
        (),
    ),
    (
        (('f', 7, 2, 1), ('f', 8, 1, 0), ('f', 9, 1, 0), ('f', 10, 1, 0)),
        ((7, 5, 4),),
        (),
    ),
    (
        (('f', 8, 0, 0), ('f', 11, 0, 0)),
        ((5, 4, 4),),
        (),
    ),
    (
        (('f', 8, 2, 1), ('f', 9, 2, 1), ('f', 10, 2, 1)),
        ((8, 1, 4), (9, 0, 5)),
        (),
    ),
    (
        (('f', 11, 1, 0), ('d', 8), ('d', 7)),
        ((9, 8, 7),),
        (),
    ),
    (
        (('d', 6),),
        ((9, 2, 6), (10, 0, 4), (10, 2, 6), (8, 5, 5)),
        (),
    ),
    (
        (('f', 11, 2, 1),),
        ((11, 2, 6),),
        (),
    ),
    (
        (('d', 9),),
        ((11, 7, 9),),
        (1, 2, 3, 4, 5, 6, 7, 8, 0, 9, 10, 11),
    ),
)

MESH = pl.DeviceIdType.MESH
NSLOT = len(SOURCES)
NPART = len(PARTS)
NSEG = len(SEGMENTS)
LEFTS = [group[0] for _, groups, _ in SEGMENTS for group in groups]
RIGHTS = [[group[1 + u] for _, groups, _ in SEGMENTS for group in groups] for u in range(GROUP)]
BACKS = [slot for _, _, slots in SEGMENTS for slot in slots]
BACK_GROUP = 4
PAD = 256


def packed(digits, index):
    word = jnp.int32(0)
    for k in range(0, len(digits), 8):
        value = sum(d << (4 * j) for j, d in enumerate(digits[k : k + 8]))
        value = value - (1 << 32) if value >> 31 else value
        word = jnp.where(index // 8 == k // 8, jnp.int32(value), word)
    return lax.shift_right_logical(word, 4 * (index % 8)) & 15


def start_of(seg, column):
    first = jnp.int32(0)
    for k, segment in enumerate(SEGMENTS):
        if segment[column]:
            first = first + jnp.where(seg > k, len(segment[column]), 0)
    return first


def gray(code):
    return code ^ ((code >> 1) & 21)


def turned(turn, word):
    return sum(1 << TURNS[turn][k] for k in range(6) if word >> k & 1)


def kernel(
    x_hbm, c_hbm, o_ref, x_ref, c_ref, own, other, ids, ids_out, id_col, id_row, side, best, back, back_out, swap_out,
    swap, load_sem, row_send, row_recv, pair_send, pair_recv, id_send, id_recv, back_send, back_recv, swap_sem,
):
    core = lax.axis_index("gx")
    place = lax.axis_index("gy")
    half = x_ref.shape[0]

    loads = [
        pltpu.make_async_copy(
            x_hbm.at[pl.ds(begin, size)], x_ref.at[pl.ds(begin, size)], load_sem.at[part]
        )
        for part, (begin, size) in enumerate(PARTS)
    ]
    loads.append(pltpu.make_async_copy(c_hbm, c_ref, load_sem.at[NPART]))
    for load in loads:
        load.start()

    corner = gray(place)
    turn = packed(TURN_OF, corner)

    def chip(word):
        values = [turned(t, word) for t in range(len(TURNS))]
        there = jnp.int32(values[0])
        for value in sorted(set(values) - {values[0]}):
            hits = turn < 0
            for t, v in enumerate(values):
                if v == value:
                    hits = hits | (turn == t)
            there = jnp.where(hits, value, there)
        return gray(corner ^ there)

    chips = {word: chip(word) for word in GREETED}
    source = [chips.get(w) for w in SOURCES]
    holder = [chips.get(w) for w in HOLDERS]
    step_to = [chips[1 << k] for k in range(6)]

    barrier = pltpu.get_barrier_semaphore()
    for word in GREETED:
        pl.semaphore_signal(barrier, inc=1, device_id=(core, chips[word]), device_id_type=MESH)
    pl.semaphore_signal(barrier, inc=1, device_id=(1 - core, place), device_id_type=MESH)

    for part, (begin, size) in enumerate(PARTS):
        loads[part].wait()
        values = x_ref[begin : begin + size, :].astype(jnp.float32)
        total = jnp.sum(values * values, axis=1, keepdims=True)
        own[0, begin : begin + size, :] = (values * lax.rsqrt(total + EPS)).astype(jnp.bfloat16)
    loads[NPART].wait()
    cluster = c_ref[...].astype(jnp.float32)
    ids_out[...] = jnp.concatenate([cluster, jnp.full((1, PAD - half), -2.0, jnp.float32)], axis=1)
    ids[0, 0] = ids_out[...]
    back_out[...] = jnp.full(back_out.shape, -1.0, jnp.float32)

    pl.semaphore_wait(barrier, len(GREETED) + 1)

    def id_copy(slot):
        return pltpu.make_async_remote_copy(
            src_ref=ids_out,
            dst_ref=ids.at[0, slot],
            send_sem=id_send.at[slot],
            recv_sem=id_recv.at[slot],
            device_id=(core, holder[slot]),
            device_id_type=MESH,
        )

    def id_pair_copy():
        return pltpu.make_async_remote_copy(
            src_ref=ids.at[0],
            dst_ref=ids.at[1],
            send_sem=id_send.at[0],
            recv_sem=id_recv.at[0],
            device_id=(1 - core, place),
            device_id_type=MESH,
        )

    def back_copy(slot, where):
        return pltpu.make_async_remote_copy(
            src_ref=back_out.at[slot],
            dst_ref=back.at[slot],
            send_sem=back_send.at[slot],
            recv_sem=back_recv.at[slot],
            device_id=(core, where),
            device_id_type=MESH,
        )

    def row_copy(part, slot):
        begin, size = PARTS[part]
        parent, step = TREES[part][slot]
        return pltpu.make_async_remote_copy(
            src_ref=own.at[parent, pl.ds(begin, size)],
            dst_ref=own.at[slot, pl.ds(begin, size)],
            send_sem=row_send.at[slot, part],
            recv_sem=row_recv.at[slot, part],
            device_id=(core, step_to[step]),
            device_id_type=MESH,
        )

    def pair_copy(slot):
        return pltpu.make_async_remote_copy(
            src_ref=own.at[slot],
            dst_ref=other.at[slot],
            send_sem=pair_send.at[slot],
            recv_sem=pair_recv.at[slot],
            device_id=(1 - core, place),
            device_id_type=MESH,
        )

    for part, slot in ROOT_ORDER[:ROOT_FIRST]:
        row_copy(part, slot).start()
    for slot in range(1, NSLOT):
        id_copy(slot).start()
    for part, slot in ROOT_ORDER[ROOT_FIRST:]:
        row_copy(part, slot).start()
    pair_copy(0).start()

    best[...] = jnp.full(best.shape, -1.0, jnp.float32)
    side[...] = jnp.full(side.shape, -1.0, jnp.float32)

    def forward(slot, part, last):
        row_copy(part, slot).wait_recv()
        for child in CHILDREN[part].get(slot, ()):
            row_copy(part, child).start()
        if last and slot in PAIRED:
            pair_copy(slot).start()

    def send_ids():
        for slot in range(1, NSLOT):
            id_copy(slot).wait_recv()
        id_pair_copy().start()

    def take_ids():
        id_pair_copy().wait_recv()

        def turn_ids(slot, carry):
            id_col[slot] = jnp.broadcast_to(ids[0, slot], (128, PAD)).T[:half]
            id_row[slot] = jnp.concatenate([ids[0, slot, :, :half], ids[1, slot, :, :half]], axis=1)
            return carry

        lax.fori_loop(0, NSLOT, turn_ids, 0)

    def give_back(index, carry):
        slots = [packed(BACKS, BACK_GROUP * index + u) for u in range(BACK_GROUP)]
        for slot in slots:
            padded = jnp.concatenate([side[slot], jnp.full((PAD - half, 128), -1.0, jnp.float32)], axis=0)
            turned_side = jnp.max(padded.T.reshape(128 // 8, 8, PAD), axis=0)
            turned_side = jnp.max(turned_side, axis=0, keepdims=True)
            high = jnp.max(best[slot], axis=0, keepdims=True)
            back_out[slot, 0, :, :half] = jnp.maximum(high[:, :half], turned_side[:, :half])
            back_out[slot, 1, :, :half] = high[:, half:]
        for slot in slots:
            where = source[1]
            for k in range(2, NSLOT):
                where = jnp.where(slot == k, source[k], where)

            @pl.when(slot > 0)
            def _():
                back_copy(slot, where).start()

        return carry

    def products_of(p, qs, same):
        right = jnp.concatenate([part for q in qs for part in (own[q], other[q])], axis=0)
        products = lax.dot_general(
            own[p], right, (((1,), (1,)), ((), ())), preferred_element_type=jnp.float32
        )
        left_id = id_col[p]
        row_best = side[p]
        for u, q in enumerate(qs):
            for k in range(2 * half // 128):
                lanes = slice(128 * k, 128 * k + 128)
                allowed = left_id == id_row[q, :, lanes]
                if same:
                    row = lax.broadcasted_iota(jnp.int32, (half, 128), 0)
                    column = lax.broadcasted_iota(jnp.int32, (half, 128), 1) + 128 * k
                    allowed = allowed & (row != column)
                product = products[:, 2 * half * u + 128 * k : 2 * half * u + 128 * k + 128]
                masked = jnp.where(allowed, product, -1.0)
                row_best = jnp.maximum(row_best, masked)
                best[q, :, lanes] = jnp.maximum(
                    best[q, :, lanes], jnp.max(masked.reshape(half // 8, 8, 128), axis=0)
                )
        side[p] = row_best

    def multiply(index, carry):
        products_of(packed(LEFTS, index), [packed(rights, index) for rights in RIGHTS], False)
        return carry

    actions = {
        "f": forward,
        "d": lambda slot: pair_copy(slot).wait_recv(),
        "i": send_ids,
        "j": take_ids,
        "s": lambda: products_of(0, [0], True),
    }

    def segment(seg, carry):
        for k, (events, _, _) in enumerate(SEGMENTS):
            if events:

                @pl.when(seg == k)
                def _():
                    for name, *where in events:
                        actions[name](*where)

        lax.fori_loop(start_of(seg, 1), start_of(seg + 1, 1), multiply, carry)
        first, end = start_of(seg, 2) // BACK_GROUP, start_of(seg + 1, 2) // BACK_GROUP
        return lax.fori_loop(first, end, give_back, carry)

    lax.fori_loop(0, NSEG, segment, 0)

    result = back_out[0]
    for slot in range(1, NSLOT):
        back_copy(slot, source[slot]).wait_recv()
        result = jnp.maximum(result, back[slot])
    swap_out[...] = result[1]
    swapping = pltpu.make_async_remote_copy(
        src_ref=swap_out,
        dst_ref=swap,
        send_sem=swap_sem.at[0],
        recv_sem=swap_sem.at[1],
        device_id=(1 - core, place),
        device_id_type=MESH,
    )
    swapping.start()

    for part in range(NPART):
        for slot in range(1, NSLOT):
            row_copy(part, slot).wait_send()
    for slot in sorted(PAIRED):
        pair_copy(slot).wait_send()
    id_pair_copy().wait_send()
    for slot in range(1, NSLOT):
        id_copy(slot).wait_send()
        back_copy(slot, source[slot]).wait_send()
    swapping.wait()
    o_ref[...] = jnp.maximum(result[0], swap[...])[:, :half]


def local(embeddings, cluster):
    half, width = embeddings.shape
    best = pl.pallas_call(
        kernel,
        out_shape=jax.ShapeDtypeStruct((1, half), jnp.float32),
        in_specs=[pl.BlockSpec(memory_space=pl.ANY)] * 2,
        out_specs=pl.BlockSpec(memory_space=pltpu.VMEM),
        scratch_shapes=[
            pltpu.VMEM((half, width), jnp.bfloat16),
            pltpu.VMEM((1, half), jnp.int32),
            pltpu.VMEM((NSLOT, half, width), jnp.bfloat16),
            pltpu.VMEM((NSLOT, half, width), jnp.bfloat16),
            pltpu.VMEM((2, NSLOT, 1, PAD), jnp.float32),
            pltpu.VMEM((1, PAD), jnp.float32),
            pltpu.VMEM((NSLOT, half, 128), jnp.float32),
            pltpu.VMEM((NSLOT, 1, 2 * half), jnp.float32),
            pltpu.VMEM((NSLOT, half, 128), jnp.float32),
            pltpu.VMEM((NSLOT, 8, 2 * half), jnp.float32),
            pltpu.VMEM((NSLOT, 2, 1, PAD), jnp.float32),
            pltpu.VMEM((NSLOT, 2, 1, PAD), jnp.float32),
            pltpu.VMEM((1, PAD), jnp.float32),
            pltpu.VMEM((1, PAD), jnp.float32),
            pltpu.SemaphoreType.DMA((NPART + 1,)),
            pltpu.SemaphoreType.DMA((NSLOT, NPART)),
            pltpu.SemaphoreType.DMA((NSLOT, NPART)),
            pltpu.SemaphoreType.DMA((NSLOT,)),
            pltpu.SemaphoreType.DMA((NSLOT,)),
            pltpu.SemaphoreType.DMA((NSLOT,)),
            pltpu.SemaphoreType.DMA((NSLOT,)),
            pltpu.SemaphoreType.DMA((NSLOT,)),
            pltpu.SemaphoreType.DMA((NSLOT,)),
            pltpu.SemaphoreType.DMA((2,)),
        ],
        compiler_params=pltpu.CompilerParams(
            collective_id=0, has_side_effects=True, vmem_limit_bytes=56 * 1024 * 1024
        ),
        cost_estimate=pl.CostEstimate(
            flops=4 * GROUP * len(LEFTS) * half * half * width, bytes_accessed=2 * half * width, transcendentals=half
        ),
    )(embeddings, cluster.reshape(1, half))
    return best.reshape(half)


def solution(mesh):
    return jax.shard_map(
        local,
        mesh=mesh,
        in_specs=(P(("gx", "gy"), None), P(("gx", "gy"))),
        out_specs=P(("gx", "gy")),
        check_vma=False,
    )
```

```python
import jax
import jax.numpy as jnp
from jax import lax
from jax.experimental import pallas as pl
from jax.experimental.pallas import tpu as pltpu
from jax.sharding import PartitionSpec as P

EPS = 1e-06
TURNS = (
    (0, 1, 2, 3, 4, 5),
    (0, 1, 2, 3, 5, 4),
    (0, 1, 3, 2, 4, 5),
    (0, 1, 3, 2, 5, 4),
    (1, 0, 2, 3, 4, 5),
    (1, 0, 2, 3, 5, 4),
    (1, 0, 3, 2, 4, 5),
    (1, 0, 3, 2, 5, 4),
)
TURN_OF = [0, 4, 4, 0, 2, 6, 6, 2, 2, 6, 6, 2, 0, 4, 4, 0, 1, 5, 5, 1, 3, 7, 7, 3, 3, 7, 7, 3, 1, 5, 5, 1, 1, 5, 5, 1, 3, 7, 7, 3, 3, 7, 7, 3, 1, 5, 5, 1, 0, 4, 4, 0, 2, 6, 6, 2, 2, 6, 6, 2, 0, 4, 4, 0]
HOLDERS = (0, 8, 1, 2, 16, 40, 6, 3, 7, 48, 44, 60)
SOURCES = (0, 4, 2, 1, 32, 20, 9, 3, 11, 48, 28, 60)
GREETED = (1, 2, 3, 4, 6, 7, 8, 9, 11, 16, 20, 28, 32, 40, 44, 48, 60)
PARTS = ((0, 64), (64, 64), (128, 64))
TREES = (
    {1: (0, 3), 2: (0, 0), 3: (0, 1), 4: (0, 4), 5: (1, 5), 6: (3, 2), 7: (3, 1), 8: (7, 2), 9: (4, 4), 10: (5, 3), 11: (10, 5)},
    {1: (0, 3), 2: (0, 0), 3: (0, 1), 4: (0, 4), 5: (1, 5), 6: (3, 2), 7: (2, 0), 8: (6, 1), 9: (4, 4), 10: (5, 3), 11: (10, 5)},
    {1: (0, 3), 2: (0, 0), 3: (0, 1), 4: (0, 4), 5: (1, 5), 6: (3, 2), 7: (2, 0), 8: (6, 1), 9: (4, 4), 10: (5, 3), 11: (10, 5)},
)
CHILDREN = (
    {0: (1, 3, 4, 2), 1: (5,), 3: (7, 6), 4: (9,), 5: (10,), 7: (8,), 10: (11,)},
    {0: (1, 3, 2, 4), 1: (5,), 2: (7,), 3: (6,), 4: (9,), 5: (10,), 6: (8,), 10: (11,)},
    {0: (1, 3, 2, 4), 1: (5,), 2: (7,), 3: (6,), 4: (9,), 5: (10,), 6: (8,), 10: (11,)},
)
GROUP = 2
ROOT_FIRST = 4
ROOT_ORDER = ((0, 1), (0, 3), (0, 4), (1, 2), (1, 1), (1, 3), (1, 4), (2, 2), (0, 2), (2, 1), (2, 3), (2, 4))
PAIRED = frozenset((0, 1, 2, 3, 4, 5, 6, 7, 8, 9))
SEGMENTS = (
    (
        (('i',), ('j',), ('f', 1, 0, 0), ('f', 2, 1, 0), ('f', 3, 0, 0), ('f', 4, 0, 0), ('d', 0), ('s',), ('f', 1, 1, 0), ('f', 2, 2, 0), ('f', 3, 1, 0), ('f', 4, 1, 0), ('f', 5, 0, 0), ('f', 6, 0, 0), ('f', 1, 2, 1), ('f', 2, 0, 1), ('f', 3, 2, 1), ('f', 4, 2, 1)),
        ((1, 0, 0),),
        (),
    ),
    (
        (('f', 5, 1, 0), ('f', 6, 1, 0), ('d', 1)),
        ((2, 0, 1),),
        (),
    ),
    (
        (('d', 2),),
        ((3, 1, 2),),
        (),
    ),
    (
        (('d', 3),),
        ((4, 3, 0),),
        (),
    ),
    (
        (('f', 7, 0, 0), ('f', 7, 1, 0), ('f', 9, 0, 0), ('f', 10, 0, 0)),
        ((4, 1, 2),),
        (),
    ),
    (
        (('f', 5, 2, 1), ('f', 6, 2, 1)),
        ((5, 3, 2), (6, 1, 2)),
        (),
    ),
    (
        (('d', 5), ('d', 4)),
        ((6, 5, 4),),
        (),
    ),
    (
        (('f', 7, 2, 1), ('f', 8, 1, 0), ('f', 9, 1, 0), ('f', 10, 1, 0)),
        ((7, 5, 4),),
        (),
    ),
    (
        (('f', 8, 0, 0), ('f', 11, 0, 0)),
        ((5, 4, 4),),
        (),
    ),
    (
        (('f', 8, 2, 1), ('f', 9, 2, 1), ('f', 10, 2, 1)),
        ((8, 1, 4), (9, 0, 5)),
        (),
    ),
    (
        (('f', 11, 1, 0), ('d', 8), ('d', 7)),
        ((9, 8, 7),),
        (),
    ),
    (
        (('d', 6),),
        ((9, 2, 6), (10, 0, 4), (10, 2, 6), (8, 5, 5)),
        (),
    ),
    (
        (('f', 11, 2, 1),),
        ((11, 2, 6),),
        (),
    ),
    (
        (('d', 9),),
        ((11, 7, 9),),
        (1, 2, 3, 4, 5, 6, 7, 8, 0, 9, 10, 11),
    ),
)

MESH = pl.DeviceIdType.MESH
NSLOT = len(SOURCES)
NPART = len(PARTS)
NSEG = len(SEGMENTS)
LEFTS = [group[0] for _, groups, _ in SEGMENTS for group in groups]
RIGHTS = [[group[1 + u] for _, groups, _ in SEGMENTS for group in groups] for u in range(GROUP)]
BACKS = [slot for _, _, slots in SEGMENTS for slot in slots]
BACK_GROUP = 4
PAD = 256


def packed(digits, index):
    word = jnp.int32(0)
    for k in range(0, len(digits), 8):
        value = sum(d << (4 * j) for j, d in enumerate(digits[k : k + 8]))
        value = value - (1 << 32) if value >> 31 else value
        word = jnp.where(index // 8 == k // 8, jnp.int32(value), word)
    return lax.shift_right_logical(word, 4 * (index % 8)) & 15


def start_of(seg, column):
    first = jnp.int32(0)
    for k, segment in enumerate(SEGMENTS):
        if segment[column]:
            first = first + jnp.where(seg > k, len(segment[column]), 0)
    return first


def gray(code):
    return code ^ ((code >> 1) & 21)


def turned(turn, word):
    return sum(1 << TURNS[turn][k] for k in range(6) if word >> k & 1)


def kernel(
    x_hbm, c_hbm, o_ref, x_ref, c_ref, own, other, ids, ids_out, id_col, id_row, side, best, back, back_out, swap_out,
    swap, load_sem, row_send, row_recv, pair_send, pair_recv, id_send, id_recv, back_send, back_recv, swap_sem,
):
    core = lax.axis_index("gx")
    place = lax.axis_index("gy")
    half = x_ref.shape[0]

    loads = [
        pltpu.make_async_copy(
            x_hbm.at[pl.ds(begin, size)], x_ref.at[pl.ds(begin, size)], load_sem.at[part]
        )
        for part, (begin, size) in enumerate(PARTS)
    ]
    loads.append(pltpu.make_async_copy(c_hbm, c_ref, load_sem.at[NPART]))
    for load in loads:
        load.start()

    corner = gray(place)
    turn = packed(TURN_OF, corner)

    def chip(word):
        values = [turned(t, word) for t in range(len(TURNS))]
        there = jnp.int32(values[0])
        for value in sorted(set(values) - {values[0]}):
            hits = turn < 0
            for t, v in enumerate(values):
                if v == value:
                    hits = hits | (turn == t)
            there = jnp.where(hits, value, there)
        return gray(corner ^ there)

    chips = {word: chip(word) for word in GREETED}
    source = [chips.get(w) for w in SOURCES]
    holder = [chips.get(w) for w in HOLDERS]
    step_to = [chips[1 << k] for k in range(6)]

    barrier = pltpu.get_barrier_semaphore()
    for word in GREETED:
        pl.semaphore_signal(barrier, inc=1, device_id=(core, chips[word]), device_id_type=MESH)
    pl.semaphore_signal(barrier, inc=1, device_id=(1 - core, place), device_id_type=MESH)

    for part, (begin, size) in enumerate(PARTS):
        loads[part].wait()
        values = x_ref[begin : begin + size, :].astype(jnp.float32)
        total = jnp.sum(values * values, axis=1, keepdims=True)
        own[0, begin : begin + size, :] = (values * lax.rsqrt(total + EPS)).astype(jnp.bfloat16)
    loads[NPART].wait()
    cluster = c_ref[...].astype(jnp.float32)
    ids_out[...] = jnp.concatenate([cluster, jnp.full((1, PAD - half), -2.0, jnp.float32)], axis=1)
    ids[0, 0] = ids_out[...]
    back_out[...] = jnp.full(back_out.shape, -1.0, jnp.float32)

    pl.semaphore_wait(barrier, len(GREETED) + 1)

    def id_copy(slot):
        return pltpu.make_async_remote_copy(
            src_ref=ids_out,
            dst_ref=ids.at[0, slot],
            send_sem=id_send.at[slot],
            recv_sem=id_recv.at[slot],
            device_id=(core, holder[slot]),
            device_id_type=MESH,
        )

    def id_pair_copy():
        return pltpu.make_async_remote_copy(
            src_ref=ids.at[0],
            dst_ref=ids.at[1],
            send_sem=id_send.at[0],
            recv_sem=id_recv.at[0],
            device_id=(1 - core, place),
            device_id_type=MESH,
        )

    def back_copy(slot, where):
        return pltpu.make_async_remote_copy(
            src_ref=back_out.at[slot],
            dst_ref=back.at[slot],
            send_sem=back_send.at[slot],
            recv_sem=back_recv.at[slot],
            device_id=(core, where),
            device_id_type=MESH,
        )

    def row_copy(part, slot):
        begin, size = PARTS[part]
        parent, step = TREES[part][slot]
        return pltpu.make_async_remote_copy(
            src_ref=own.at[parent, pl.ds(begin, size)],
            dst_ref=own.at[slot, pl.ds(begin, size)],
            send_sem=row_send.at[slot, part],
            recv_sem=row_recv.at[slot, part],
            device_id=(core, step_to[step]),
            device_id_type=MESH,
        )

    def pair_copy(slot):
        return pltpu.make_async_remote_copy(
            src_ref=own.at[slot],
            dst_ref=other.at[slot],
            send_sem=pair_send.at[slot],
            recv_sem=pair_recv.at[slot],
            device_id=(1 - core, place),
            device_id_type=MESH,
        )

    for part, slot in ROOT_ORDER[:ROOT_FIRST]:
        row_copy(part, slot).start()
    for slot in range(1, NSLOT):
        id_copy(slot).start()
    for part, slot in ROOT_ORDER[ROOT_FIRST:]:
        row_copy(part, slot).start()
    pair_copy(0).start()

    best[...] = jnp.full(best.shape, -1.0, jnp.float32)
    side[...] = jnp.full(side.shape, -1.0, jnp.float32)

    def forward(slot, part, last):
        row_copy(part, slot).wait_recv()
        for child in CHILDREN[part].get(slot, ()):
            row_copy(part, child).start()
        if last and slot in PAIRED:
            pair_copy(slot).start()

    def send_ids():
        for slot in range(1, NSLOT):
            id_copy(slot).wait_recv()
        id_pair_copy().start()

    def take_ids():
        id_pair_copy().wait_recv()

        def turn_ids(slot, carry):
            id_col[slot] = jnp.broadcast_to(ids[0, slot], (128, PAD)).T[:half]
            id_row[slot] = jnp.concatenate([ids[0, slot, :, :half], ids[1, slot, :, :half]], axis=1)
            return carry

        lax.fori_loop(0, NSLOT, turn_ids, 0)

    def give_back(index, carry):
        slots = [packed(BACKS, BACK_GROUP * index + u) for u in range(BACK_GROUP)]
        for slot in slots:
            padded = jnp.concatenate([side[slot], jnp.full((PAD - half, 128), -1.0, jnp.float32)], axis=0)
            turned_side = jnp.max(padded.T.reshape(128 // 8, 8, PAD), axis=0)
            turned_side = jnp.max(turned_side, axis=0, keepdims=True)
            high = jnp.max(best[slot], axis=0, keepdims=True)
            back_out[slot, 0, :, :half] = jnp.maximum(high[:, :half], turned_side[:, :half])
            back_out[slot, 1, :, :half] = high[:, half:]
        for slot in slots:
            where = source[1]
            for k in range(2, NSLOT):
                where = jnp.where(slot == k, source[k], where)

            @pl.when(slot > 0)
            def _():
                back_copy(slot, where).start()

        return carry

    def products_of(p, qs, same):
        right = jnp.concatenate([part for q in qs for part in (own[q], other[q])], axis=0)
        left_id = id_col[p]
        row_best = side[p]
        for begin in range(0, 2 * half * len(qs), PAD):
            end = min(begin + PAD, 2 * half * len(qs))
            products = lax.dot_general(
                own[p], right[begin:end], (((1,), (1,)), ((), ())), preferred_element_type=jnp.float32
            )
            for k in range(begin, end, 128):
                q, first = qs[k // (2 * half)], k % (2 * half)
                lanes = slice(first, first + 128)
                allowed = left_id == id_row[q, :, lanes]
                if same:
                    row = lax.broadcasted_iota(jnp.int32, (half, 128), 0)
                    column = lax.broadcasted_iota(jnp.int32, (half, 128), 1) + first
                    allowed = allowed & (row != column)
                masked = jnp.where(allowed, products[:, k - begin : k - begin + 128], -1.0)
                row_best = jnp.maximum(row_best, masked)
                best[q, :, lanes] = jnp.maximum(
                    best[q, :, lanes], jnp.max(masked.reshape(half // 8, 8, 128), axis=0)
                )
        side[p] = row_best

    def multiply(index, carry):
        products_of(packed(LEFTS, index), [packed(rights, index) for rights in RIGHTS], False)
        return carry

    actions = {
        "f": forward,
        "d": lambda slot: pair_copy(slot).wait_recv(),
        "i": send_ids,
        "j": take_ids,
        "s": lambda: products_of(0, [0], True),
    }

    def segment(seg, carry):
        for k, (events, _, _) in enumerate(SEGMENTS):
            if events:

                @pl.when(seg == k)
                def _():
                    for name, *where in events:
                        actions[name](*where)

        lax.fori_loop(start_of(seg, 1), start_of(seg + 1, 1), multiply, carry)
        first, end = start_of(seg, 2) // BACK_GROUP, start_of(seg + 1, 2) // BACK_GROUP
        return lax.fori_loop(first, end, give_back, carry)

    lax.fori_loop(0, NSEG, segment, 0)

    result = back_out[0]
    for slot in range(1, NSLOT):
        back_copy(slot, source[slot]).wait_recv()
        result = jnp.maximum(result, back[slot])
    swap_out[...] = result[1]
    swapping = pltpu.make_async_remote_copy(
        src_ref=swap_out,
        dst_ref=swap,
        send_sem=swap_sem.at[0],
        recv_sem=swap_sem.at[1],
        device_id=(1 - core, place),
        device_id_type=MESH,
    )
    swapping.start()

    for part in range(NPART):
        for slot in range(1, NSLOT):
            row_copy(part, slot).wait_send()
    for slot in sorted(PAIRED):
        pair_copy(slot).wait_send()
    id_pair_copy().wait_send()
    for slot in range(1, NSLOT):
        id_copy(slot).wait_send()
        back_copy(slot, source[slot]).wait_send()
    swapping.wait()
    o_ref[...] = jnp.maximum(result[0], swap[...])[:, :half]


def local(embeddings, cluster):
    half, width = embeddings.shape
    best = pl.pallas_call(
        kernel,
        out_shape=jax.ShapeDtypeStruct((1, half), jnp.float32),
        in_specs=[pl.BlockSpec(memory_space=pl.ANY)] * 2,
        out_specs=pl.BlockSpec(memory_space=pltpu.VMEM),
        scratch_shapes=[
            pltpu.VMEM((half, width), jnp.bfloat16),
            pltpu.VMEM((1, half), jnp.int32),
            pltpu.VMEM((NSLOT, half, width), jnp.bfloat16),
            pltpu.VMEM((NSLOT, half, width), jnp.bfloat16),
            pltpu.VMEM((2, NSLOT, 1, PAD), jnp.float32),
            pltpu.VMEM((1, PAD), jnp.float32),
            pltpu.VMEM((NSLOT, half, 128), jnp.float32),
            pltpu.VMEM((NSLOT, 1, 2 * half), jnp.float32),
            pltpu.VMEM((NSLOT, half, 128), jnp.float32),
            pltpu.VMEM((NSLOT, 8, 2 * half), jnp.float32),
            pltpu.VMEM((NSLOT, 2, 1, PAD), jnp.float32),
            pltpu.VMEM((NSLOT, 2, 1, PAD), jnp.float32),
            pltpu.VMEM((1, PAD), jnp.float32),
            pltpu.VMEM((1, PAD), jnp.float32),
            pltpu.SemaphoreType.DMA((NPART + 1,)),
            pltpu.SemaphoreType.DMA((NSLOT, NPART)),
            pltpu.SemaphoreType.DMA((NSLOT, NPART)),
            pltpu.SemaphoreType.DMA((NSLOT,)),
            pltpu.SemaphoreType.DMA((NSLOT,)),
            pltpu.SemaphoreType.DMA((NSLOT,)),
            pltpu.SemaphoreType.DMA((NSLOT,)),
            pltpu.SemaphoreType.DMA((NSLOT,)),
            pltpu.SemaphoreType.DMA((NSLOT,)),
            pltpu.SemaphoreType.DMA((2,)),
        ],
        compiler_params=pltpu.CompilerParams(
            collective_id=0, has_side_effects=True, vmem_limit_bytes=56 * 1024 * 1024
        ),
        cost_estimate=pl.CostEstimate(
            flops=4 * GROUP * len(LEFTS) * half * half * width, bytes_accessed=2 * half * width, transcendentals=half
        ),
    )(embeddings, cluster.reshape(1, half))
    return best.reshape(half)


def solution(mesh):
    return jax.shard_map(
        local,
        mesh=mesh,
        in_specs=(P(("gx", "gy"), None), P(("gx", "gy"))),
        out_specs=P(("gx", "gy")),
        check_vma=False,
    )
```

```python
import jax
import jax.numpy as jnp
from jax import lax
from jax.experimental import pallas as pl
from jax.experimental.pallas import tpu as pltpu
from jax.sharding import PartitionSpec as P

EPS = 1e-06
TURNS = (
    (0, 1, 2, 3, 4, 5),
    (0, 1, 2, 3, 5, 4),
    (0, 1, 3, 2, 4, 5),
    (0, 1, 3, 2, 5, 4),
    (1, 0, 2, 3, 4, 5),
    (1, 0, 2, 3, 5, 4),
    (1, 0, 3, 2, 4, 5),
    (1, 0, 3, 2, 5, 4),
)
TURN_OF = [0, 4, 4, 0, 2, 6, 6, 2, 2, 6, 6, 2, 0, 4, 4, 0, 1, 5, 5, 1, 3, 7, 7, 3, 3, 7, 7, 3, 1, 5, 5, 1, 1, 5, 5, 1, 3, 7, 7, 3, 3, 7, 7, 3, 1, 5, 5, 1, 0, 4, 4, 0, 2, 6, 6, 2, 2, 6, 6, 2, 0, 4, 4, 0]
HOLDERS = (0, 8, 2, 16, 1, 40, 6, 3, 7, 48, 44, 60)
SOURCES = (0, 4, 1, 32, 2, 20, 9, 3, 11, 48, 28, 60)
GREETED = (1, 2, 3, 4, 6, 7, 8, 9, 11, 16, 20, 28, 32, 40, 44, 48, 60)
PARTS = ((0, 64), (64, 64), (128, 64))
TREES = (
    {1: (0, 3), 2: (0, 1), 3: (0, 4), 4: (0, 0), 5: (1, 5), 6: (2, 2), 7: (4, 0), 8: (6, 1), 9: (3, 4), 10: (5, 3), 11: (10, 5)},
    {1: (0, 3), 2: (0, 1), 3: (0, 4), 4: (0, 0), 5: (1, 5), 6: (2, 2), 7: (2, 1), 8: (7, 2), 9: (3, 4), 10: (5, 3), 11: (10, 5)},
    {1: (0, 3), 2: (0, 1), 3: (0, 4), 4: (0, 0), 5: (1, 5), 6: (2, 2), 7: (4, 0), 8: (6, 1), 9: (3, 4), 10: (5, 3), 11: (10, 5)},
)
CHILDREN = (
    {0: (1, 2, 4, 3), 1: (5,), 2: (6,), 3: (9,), 4: (7,), 5: (10,), 6: (8,), 10: (11,)},
    {0: (1, 2, 3, 4), 1: (5,), 2: (7, 6), 3: (9,), 5: (10,), 7: (8,), 10: (11,)},
    {0: (1, 2, 4, 3), 1: (5,), 2: (6,), 3: (9,), 4: (7,), 5: (10,), 6: (8,), 10: (11,)},
)
GROUP = 2
ROOT_FIRST = 4
ROOT_ORDER = ((0, 1), (0, 2), (0, 3), (0, 4), (1, 1), (1, 2), (1, 3), (2, 4), (2, 1), (2, 2), (2, 3), (1, 4))
PAIRED = frozenset((0, 1, 3, 5, 9, 10, 11))
SEGMENTS = (
    (
        (('i',), ('f', 1, 0), ('f', 2, 0), ('f', 3, 0), ('f', 4, 0), ('j',), ('d', 0), ('s',), ('f', 1, 1), ('f', 2, 1), ('f', 3, 1), ('f', 4, 2), ('f', 5, 0), ('f', 6, 0), ('f', 1, 2), ('f', 2, 2), ('f', 3, 2), ('f', 7, 0)),
        ((1, 0, 0),),
        (),
    ),
    (
        (('f', 5, 1), ('f', 6, 1), ('d', 1)),
        ((2, 0, 1), (3, 0, 1)),
        (),
    ),
    (
        (('f', 4, 1), ('f', 7, 1), ('f', 9, 0), ('f', 10, 0), ('d', 3)),
        ((4, 1, 3),),
        (),
    ),
    (
        (('f', 5, 2), ('f', 6, 2)),
        ((6, 1, 3), (5, 3, 3)),
        (),
    ),
    (
        (('f', 7, 2), ('f', 8, 0), ('f', 9, 1), ('f', 10, 1), ('d', 5)),
        ((2, 3, 5),),
        (),
    ),
    (
        (('f', 8, 1), ('f', 11, 0)),
        ((7, 1, 0), (7, 3, 5)),
        (),
    ),
    (
        (('f', 8, 2), ('f', 9, 2), ('f', 10, 2)),
        ((8, 1, 3),),
        (),
    ),
    (
        (('f', 11, 1),),
        ((9, 0, 5),),
        (),
    ),
    (
        (('d', 10),),
        ((4, 10, 5), (6, 10, 5)),
        (),
    ),
    (
        (('d', 9),),
        ((8, 5, 9),),
        (),
    ),
    (
        (('f', 11, 2),),
        ((10, 0, 3), (11, 9, 9)),
        (),
    ),
    (
        (('d', 11),),
        ((2, 9, 11), (6, 9, 11), (7, 9, 11)),
        (1, 2, 3, 4, 5, 6, 7, 8, 0, 9, 10, 11),
    ),
)

MESH = pl.DeviceIdType.MESH
NSLOT = len(SOURCES)
NPART = len(PARTS)
NSEG = len(SEGMENTS)
LEFTS = [group[0] for _, groups, _ in SEGMENTS for group in groups]
RIGHTS = [[group[1 + u] for _, groups, _ in SEGMENTS for group in groups] for u in range(GROUP)]
BACKS = [slot for _, _, slots in SEGMENTS for slot in slots]
BACK_GROUP = 4
PAD = 256


def packed(digits, index):
    word = jnp.int32(0)
    for k in range(0, len(digits), 8):
        value = sum(d << (4 * j) for j, d in enumerate(digits[k : k + 8]))
        value = value - (1 << 32) if value >> 31 else value
        word = jnp.where(index // 8 == k // 8, jnp.int32(value), word)
    return lax.shift_right_logical(word, 4 * (index % 8)) & 15


def start_of(seg, column):
    first = jnp.int32(0)
    for k, segment in enumerate(SEGMENTS):
        if segment[column]:
            first = first + jnp.where(seg > k, len(segment[column]), 0)
    return first


def gray(code):
    return code ^ ((code >> 1) & 21)


def turned(turn, word):
    return sum(1 << TURNS[turn][k] for k in range(6) if word >> k & 1)


def kernel(
    x_hbm, c_hbm, o_ref, x_ref, c_ref, own, other, ids, ids_out, id_col, id_row, side, best, back, back_out, swap_out,
    swap, load_sem, row_send, row_recv, pair_send, pair_recv, id_send, id_recv, back_send, back_recv, swap_sem,
):
    core = lax.axis_index("gx")
    place = lax.axis_index("gy")
    half = x_ref.shape[0]

    loads = [
        pltpu.make_async_copy(
            x_hbm.at[pl.ds(begin, size)], x_ref.at[pl.ds(begin, size)], load_sem.at[part]
        )
        for part, (begin, size) in enumerate(PARTS)
    ]
    loads.append(pltpu.make_async_copy(c_hbm, c_ref, load_sem.at[NPART]))
    for load in loads:
        load.start()

    corner = gray(place)
    turn = packed(TURN_OF, corner)

    def chip(word):
        values = [turned(t, word) for t in range(len(TURNS))]
        there = jnp.int32(values[0])
        for value in sorted(set(values) - {values[0]}):
            hits = turn < 0
            for t, v in enumerate(values):
                if v == value:
                    hits = hits | (turn == t)
            there = jnp.where(hits, value, there)
        return gray(corner ^ there)

    chips = {word: chip(word) for word in GREETED}
    source = [chips.get(w) for w in SOURCES]
    holder = [chips.get(w) for w in HOLDERS]
    step_to = [chips[1 << k] for k in range(6)]

    barrier = pltpu.get_barrier_semaphore()
    for word in GREETED:
        pl.semaphore_signal(barrier, inc=1, device_id=(core, chips[word]), device_id_type=MESH)
    pl.semaphore_signal(barrier, inc=1, device_id=(1 - core, place), device_id_type=MESH)

    for part, (begin, size) in enumerate(PARTS):
        loads[part].wait()
        values = x_ref[begin : begin + size, :].astype(jnp.float32)
        total = jnp.sum(values * values, axis=1, keepdims=True)
        own[0, begin : begin + size, :] = (values * lax.rsqrt(total + EPS)).astype(jnp.bfloat16)
    loads[NPART].wait()
    cluster = c_ref[...].astype(jnp.float32)
    ids_out[...] = jnp.concatenate([cluster, jnp.full((1, PAD - half), -2.0, jnp.float32)], axis=1)
    ids[0, 0] = ids_out[...]
    back_out[...] = jnp.full(back_out.shape, -1.0, jnp.float32)

    pl.semaphore_wait(barrier, len(GREETED) + 1)

    def id_copy(slot):
        return pltpu.make_async_remote_copy(
            src_ref=ids_out,
            dst_ref=ids.at[0, slot],
            send_sem=id_send.at[slot],
            recv_sem=id_recv.at[slot],
            device_id=(core, holder[slot]),
            device_id_type=MESH,
        )

    def id_pair_copy():
        return pltpu.make_async_remote_copy(
            src_ref=ids.at[0],
            dst_ref=ids.at[1],
            send_sem=id_send.at[0],
            recv_sem=id_recv.at[0],
            device_id=(1 - core, place),
            device_id_type=MESH,
        )

    def back_copy(slot, where):
        return pltpu.make_async_remote_copy(
            src_ref=back_out.at[slot],
            dst_ref=back.at[slot],
            send_sem=back_send.at[slot],
            recv_sem=back_recv.at[slot],
            device_id=(core, where),
            device_id_type=MESH,
        )

    def row_copy(part, slot):
        begin, size = PARTS[part]
        parent, step = TREES[part][slot]
        return pltpu.make_async_remote_copy(
            src_ref=own.at[parent, pl.ds(begin, size)],
            dst_ref=own.at[slot, pl.ds(begin, size)],
            send_sem=row_send.at[slot, part],
            recv_sem=row_recv.at[slot, part],
            device_id=(core, step_to[step]),
            device_id_type=MESH,
        )

    def pair_copy(slot, part):
        begin, size = PARTS[part]
        return pltpu.make_async_remote_copy(
            src_ref=own.at[slot, pl.ds(begin, size)],
            dst_ref=other.at[slot, pl.ds(begin, size)],
            send_sem=pair_send.at[slot, part],
            recv_sem=pair_recv.at[slot, part],
            device_id=(1 - core, place),
            device_id_type=MESH,
        )

    for slot in range(1, NSLOT):
        id_copy(slot).start()
    for part, slot in ROOT_ORDER:
        row_copy(part, slot).start()
    for part in range(NPART):
        pair_copy(0, part).start()

    best[...] = jnp.full(best.shape, -1.0, jnp.float32)
    side[...] = jnp.full(side.shape, -1.0, jnp.float32)

    def forward(slot, part):
        row_copy(part, slot).wait_recv()
        for child in CHILDREN[part].get(slot, ()):
            row_copy(part, child).start()
        if slot in PAIRED:
            pair_copy(slot, part).start()

    def take_pair(slot):
        for part in range(NPART):
            pair_copy(slot, part).wait_recv()

    def send_ids():
        for slot in range(1, NSLOT):
            id_copy(slot).wait_recv()
        id_pair_copy().start()

    def take_ids():
        id_pair_copy().wait_recv()

        def turn_ids(slot, carry):
            id_col[slot] = jnp.broadcast_to(ids[0, slot], (128, PAD)).T[:half]
            id_row[slot] = jnp.concatenate([ids[0, slot, :, :half], ids[1, slot, :, :half]], axis=1)
            return carry

        lax.fori_loop(0, NSLOT, turn_ids, 0)

    def give_back(index, carry):
        slots = [packed(BACKS, BACK_GROUP * index + u) for u in range(BACK_GROUP)]
        for slot in slots:
            padded = jnp.concatenate([side[slot], jnp.full((PAD - half, 128), -1.0, jnp.float32)], axis=0)
            turned_side = jnp.max(padded.T.reshape(128 // 8, 8, PAD), axis=0)
            turned_side = jnp.max(turned_side, axis=0, keepdims=True)
            high = jnp.max(best[slot], axis=0, keepdims=True)
            back_out[slot, 0, :, :half] = jnp.maximum(high[:, :half], turned_side[:, :half])
            back_out[slot, 1, :, :half] = high[:, half:]
        for slot in slots:
            where = source[1]
            for k in range(2, NSLOT):
                where = jnp.where(slot == k, source[k], where)

            @pl.when(slot > 0)
            def _():
                back_copy(slot, where).start()

        return carry

    def products_of(p, qs, same):
        right = jnp.concatenate([part for q in qs for part in (own[q], other[q])], axis=0)
        left_id = id_col[p]
        row_best = side[p]
        for begin in range(0, 2 * half * len(qs), PAD):
            end = min(begin + PAD, 2 * half * len(qs))
            products = lax.dot_general(
                own[p], right[begin:end], (((1,), (1,)), ((), ())), preferred_element_type=jnp.float32
            )
            for k in range(begin, end, 128):
                q, first = qs[k // (2 * half)], k % (2 * half)
                lanes = slice(first, first + 128)
                allowed = left_id == id_row[q, :, lanes]
                if same:
                    row = lax.broadcasted_iota(jnp.int32, (half, 128), 0)
                    column = lax.broadcasted_iota(jnp.int32, (half, 128), 1) + first
                    allowed = allowed & (row != column)
                masked = jnp.where(allowed, products[:, k - begin : k - begin + 128], -1.0)
                row_best = jnp.maximum(row_best, masked)
                best[q, :, lanes] = jnp.maximum(
                    best[q, :, lanes], jnp.max(masked.reshape(half // 8, 8, 128), axis=0)
                )
        side[p] = row_best

    def multiply(index, carry):
        products_of(packed(LEFTS, index), [packed(rights, index) for rights in RIGHTS], False)
        return carry

    actions = {
        "f": forward,
        "d": take_pair,
        "i": send_ids,
        "j": take_ids,
        "s": lambda: products_of(0, [0], True),
    }

    def segment(seg, carry):
        for k, (events, _, _) in enumerate(SEGMENTS):
            if events:

                @pl.when(seg == k)
                def _():
                    for name, *where in events:
                        actions[name](*where)

        lax.fori_loop(start_of(seg, 1), start_of(seg + 1, 1), multiply, carry)
        first, end = start_of(seg, 2) // BACK_GROUP, start_of(seg + 1, 2) // BACK_GROUP
        return lax.fori_loop(first, end, give_back, carry)

    lax.fori_loop(0, NSEG, segment, 0)

    result = back_out[0]
    for slot in range(1, NSLOT):
        back_copy(slot, source[slot]).wait_recv()
        result = jnp.maximum(result, back[slot])
    swap_out[...] = result[1]
    swapping = pltpu.make_async_remote_copy(
        src_ref=swap_out,
        dst_ref=swap,
        send_sem=swap_sem.at[0],
        recv_sem=swap_sem.at[1],
        device_id=(1 - core, place),
        device_id_type=MESH,
    )
    swapping.start()

    for part in range(NPART):
        for slot in range(1, NSLOT):
            row_copy(part, slot).wait_send()
        for slot in sorted(PAIRED):
            pair_copy(slot, part).wait_send()
    id_pair_copy().wait_send()
    for slot in range(1, NSLOT):
        id_copy(slot).wait_send()
        back_copy(slot, source[slot]).wait_send()
    swapping.wait()
    o_ref[...] = jnp.maximum(result[0], swap[...])[:, :half]


def local(embeddings, cluster):
    half, width = embeddings.shape
    best = pl.pallas_call(
        kernel,
        out_shape=jax.ShapeDtypeStruct((1, half), jnp.float32),
        in_specs=[pl.BlockSpec(memory_space=pl.ANY)] * 2,
        out_specs=pl.BlockSpec(memory_space=pltpu.VMEM),
        scratch_shapes=[
            pltpu.VMEM((half, width), jnp.bfloat16),
            pltpu.VMEM((1, half), jnp.int32),
            pltpu.VMEM((NSLOT, half, width), jnp.bfloat16),
            pltpu.VMEM((NSLOT, half, width), jnp.bfloat16),
            pltpu.VMEM((2, NSLOT, 1, PAD), jnp.float32),
            pltpu.VMEM((1, PAD), jnp.float32),
            pltpu.VMEM((NSLOT, half, 128), jnp.float32),
            pltpu.VMEM((NSLOT, 1, 2 * half), jnp.float32),
            pltpu.VMEM((NSLOT, half, 128), jnp.float32),
            pltpu.VMEM((NSLOT, 8, 2 * half), jnp.float32),
            pltpu.VMEM((NSLOT, 2, 1, PAD), jnp.float32),
            pltpu.VMEM((NSLOT, 2, 1, PAD), jnp.float32),
            pltpu.VMEM((1, PAD), jnp.float32),
            pltpu.VMEM((1, PAD), jnp.float32),
            pltpu.SemaphoreType.DMA((NPART + 1,)),
            pltpu.SemaphoreType.DMA((NSLOT, NPART)),
            pltpu.SemaphoreType.DMA((NSLOT, NPART)),
            pltpu.SemaphoreType.DMA((NSLOT, NPART)),
            pltpu.SemaphoreType.DMA((NSLOT, NPART)),
            pltpu.SemaphoreType.DMA((NSLOT,)),
            pltpu.SemaphoreType.DMA((NSLOT,)),
            pltpu.SemaphoreType.DMA((NSLOT,)),
            pltpu.SemaphoreType.DMA((NSLOT,)),
            pltpu.SemaphoreType.DMA((2,)),
        ],
        compiler_params=pltpu.CompilerParams(
            collective_id=0, has_side_effects=True, vmem_limit_bytes=56 * 1024 * 1024
        ),
        cost_estimate=pl.CostEstimate(
            flops=4 * GROUP * len(LEFTS) * half * half * width, bytes_accessed=2 * half * width, transcendentals=half
        ),
    )(embeddings, cluster.reshape(1, half))
    return best.reshape(half)


def solution(mesh):
    return jax.shard_map(
        local,
        mesh=mesh,
        in_specs=(P(("gx", "gy"), None), P(("gx", "gy"))),
        out_specs=P(("gx", "gy")),
        check_vma=False,
    )
```

```python
import jax
import jax.numpy as jnp
from jax import lax
from jax.experimental import pallas as pl
from jax.experimental.pallas import tpu as pltpu
from jax.sharding import PartitionSpec as P

EPS = 1e-06
TURNS = (
    (0, 1, 2, 3, 4, 5),
    (0, 1, 2, 3, 5, 4),
    (0, 1, 3, 2, 4, 5),
    (0, 1, 3, 2, 5, 4),
    (1, 0, 2, 3, 4, 5),
    (1, 0, 2, 3, 5, 4),
    (1, 0, 3, 2, 4, 5),
    (1, 0, 3, 2, 5, 4),
)
TURN_OF = [0, 4, 4, 0, 2, 6, 6, 2, 2, 6, 6, 2, 0, 4, 4, 0, 1, 5, 5, 1, 3, 7, 7, 3, 3, 7, 7, 3, 1, 5, 5, 1, 1, 5, 5, 1, 3, 7, 7, 3, 3, 7, 7, 3, 1, 5, 5, 1, 0, 4, 4, 0, 2, 6, 6, 2, 2, 6, 6, 2, 0, 4, 4, 0]
SOURCES = (0, 4, 2, 1, 32, 20, 9, 3, 11, 48, 28, 60)
PARTS = ((0, 64), (64, 64), (128, 64))
TREES = (
    {1: (0, 3), 2: (0, 0), 3: (0, 1), 4: (0, 4), 5: (1, 5), 6: (3, 2), 7: (3, 1), 8: (7, 2), 9: (4, 4), 10: (5, 3), 11: (10, 5)},
    {1: (0, 3), 2: (0, 0), 3: (0, 1), 4: (0, 4), 5: (1, 5), 6: (3, 2), 7: (2, 0), 8: (6, 1), 9: (4, 4), 10: (5, 3), 11: (10, 5)},
    {1: (0, 3), 2: (0, 0), 3: (0, 1), 4: (0, 4), 5: (1, 5), 6: (3, 2), 7: (2, 0), 8: (6, 1), 9: (4, 4), 10: (5, 3), 11: (10, 5)},
)
CHILDREN = (
    {0: (1, 3, 4, 2), 1: (5,), 3: (7, 6), 4: (9,), 5: (10,), 7: (8,), 10: (11,)},
    {0: (1, 3, 2, 4), 1: (5,), 2: (7,), 3: (6,), 4: (9,), 5: (10,), 6: (8,), 10: (11,)},
    {0: (1, 3, 2, 4), 1: (5,), 2: (7,), 3: (6,), 4: (9,), 5: (10,), 6: (8,), 10: (11,)},
)
GROUP = 2
ROOT_ORDER = ((0, 1), (0, 3), (0, 4), (1, 2), (1, 1), (1, 3), (1, 4), (2, 2), (0, 2), (2, 1), (2, 3), (2, 4))
PAIRED = frozenset((0, 1, 2, 4, 5, 6, 7, 9))
SEGMENTS = (
    (
        (('d', 0), ('s',), ('f', 1, 0), ('f', 2, 1), ('f', 3, 0), ('f', 4, 0), ('f', 1, 1), ('f', 2, 2), ('f', 3, 1), ('f', 4, 1), ('f', 5, 0), ('f', 6, 0), ('f', 1, 2), ('f', 2, 0), ('f', 3, 2), ('f', 4, 2)),
        ((1, 0, 0),),
        (),
    ),
    (
        (('f', 5, 1), ('f', 6, 1), ('d', 1)),
        ((2, 0, 1),),
        (),
    ),
    (
        (('d', 2),),
        ((3, 1, 2), (4, 0, 1)),
        (),
    ),
    (
        (('f', 7, 0), ('f', 7, 1), ('f', 9, 0), ('f', 10, 0)),
        ((4, 2, 2),),
        (),
    ),
    (
        (('f', 5, 2), ('f', 6, 2), ('d', 4)),
        ((5, 2, 4), (6, 1, 2)),
        (),
    ),
    (
        (('f', 7, 2), ('f', 8, 1), ('f', 9, 1), ('f', 10, 1), ('d', 5)),
        ((3, 4, 5),),
        (),
    ),
    (
        (('f', 8, 0), ('f', 11, 0)),
        ((6, 5, 4), (7, 4, 5)),
        (),
    ),
    (
        (('f', 8, 2), ('f', 9, 2), ('f', 10, 2)),
        ((8, 1, 4), (9, 0, 5)),
        (),
    ),
    (
        (('f', 11, 1), ('d', 9)),
        ((8, 5, 9),),
        (),
    ),
    (
        (('d', 7),),
        ((9, 7, 2), (10, 0, 4)),
        (),
    ),
    (
        (('d', 6),),
        ((10, 2, 6),),
        (),
    ),
    (
        (('f', 11, 2),),
        ((11, 2, 7), (11, 9, 6), (9, 6, 6)),
        (1, 2, 3, 4, 5, 6, 7, 8, 0, 9, 10, 11),
    ),
)

MESH = pl.DeviceIdType.MESH
NSLOT = len(SOURCES)
NPART = len(PARTS)
NSEG = len(SEGMENTS)
LEFTS = [group[0] for _, groups, _ in SEGMENTS for group in groups]
RIGHTS = [[group[1 + u] for _, groups, _ in SEGMENTS for group in groups] for u in range(GROUP)]
BACKS = [slot for _, _, slots in SEGMENTS for slot in slots]
BACK_GROUP = 4
PAD = 256


def packed(digits, index):
    word = jnp.int32(0)
    for k in range(0, len(digits), 8):
        value = sum(d << (4 * j) for j, d in enumerate(digits[k : k + 8]))
        value = value - (1 << 32) if value >> 31 else value
        word = jnp.where(index // 8 == k // 8, jnp.int32(value), word)
    return lax.shift_right_logical(word, 4 * (index % 8)) & 15


def start_of(seg, column):
    first = jnp.int32(0)
    for k, segment in enumerate(SEGMENTS):
        if segment[column]:
            first = first + jnp.where(seg > k, len(segment[column]), 0)
    return first


def gray(code):
    return code ^ ((code >> 1) & 21)


def turned(turn, word):
    return sum(1 << TURNS[turn][k] for k in range(6) if word >> k & 1)


def kernel(
    x_hbm, c_hbm, o_ref, x_ref, c_ref, own, other, ids, side, best, back, back_out, swap_out,
    swap, load_sem, row_send, row_recv, pair_send, pair_recv, id_send, id_recv, back_send, back_recv, swap_sem,
):
    core = lax.axis_index("gx")
    place = lax.axis_index("gy")
    half = x_ref.shape[0]

    loads = [
        pltpu.make_async_copy(
            x_hbm.at[pl.ds(begin, size)], x_ref.at[pl.ds(begin, size)], load_sem.at[part]
        )
        for part, (begin, size) in enumerate(PARTS)
    ]
    loads.append(pltpu.make_async_copy(c_hbm, c_ref, load_sem.at[NPART]))
    for load in loads:
        load.start()

    corner = gray(place)
    turn = packed(TURN_OF, corner)

    def chip(word):
        values = [turned(t, word) for t in range(len(TURNS))]
        there = jnp.int32(values[0])
        for value in sorted(set(values) - {values[0]}):
            hits = turn < 0
            for t, v in enumerate(values):
                if v == value:
                    hits = hits | (turn == t)
            there = jnp.where(hits, value, there)
        return gray(corner ^ there)

    step_to = [chip(1 << k) for k in range(6)]

    barrier = pltpu.get_barrier_semaphore()
    for where in step_to:
        pl.semaphore_signal(barrier, inc=1, device_id=(core, where), device_id_type=MESH)
    pl.semaphore_signal(barrier, inc=1, device_id=(1 - core, place), device_id_type=MESH)

    source = [chip(w) for w in SOURCES]

    for part, (begin, size) in enumerate(PARTS):
        loads[part].wait()
        values = x_ref[begin : begin + size, :].astype(jnp.float32)
        total = jnp.sum(values * values, axis=1, keepdims=True)
        own[0, begin : begin + size, :] = (values * lax.rsqrt(total + EPS)).astype(jnp.bfloat16)
    loads[NPART].wait()
    cluster = c_ref[...].astype(jnp.float32)
    ids[0, 0] = jnp.concatenate([cluster, jnp.full((1, PAD - half), -2.0, jnp.float32)], axis=1)
    back_out[...] = jnp.full(back_out.shape, -1.0, jnp.float32)

    pl.semaphore_wait(barrier, 7)

    def id_copy(slot):
        parent, step = TREES[0][slot]
        return pltpu.make_async_remote_copy(
            src_ref=ids.at[0, parent],
            dst_ref=ids.at[0, slot],
            send_sem=id_send.at[0, slot],
            recv_sem=id_recv.at[0, slot],
            device_id=(core, step_to[step]),
            device_id_type=MESH,
        )

    def id_pair_copy(slot):
        return pltpu.make_async_remote_copy(
            src_ref=ids.at[0, slot],
            dst_ref=ids.at[1, slot],
            send_sem=id_send.at[1, slot],
            recv_sem=id_recv.at[1, slot],
            device_id=(1 - core, place),
            device_id_type=MESH,
        )

    def back_copy(slot, where):
        return pltpu.make_async_remote_copy(
            src_ref=back_out.at[slot],
            dst_ref=back.at[slot],
            send_sem=back_send.at[slot],
            recv_sem=back_recv.at[slot],
            device_id=(core, where),
            device_id_type=MESH,
        )

    def row_copy(part, slot):
        begin, size = PARTS[part]
        parent, step = TREES[part][slot]
        return pltpu.make_async_remote_copy(
            src_ref=own.at[parent, pl.ds(begin, size)],
            dst_ref=own.at[slot, pl.ds(begin, size)],
            send_sem=row_send.at[slot, part],
            recv_sem=row_recv.at[slot, part],
            device_id=(core, step_to[step]),
            device_id_type=MESH,
        )

    def pair_copy(slot, part):
        begin, size = PARTS[part]
        return pltpu.make_async_remote_copy(
            src_ref=own.at[slot, pl.ds(begin, size)],
            dst_ref=other.at[slot, pl.ds(begin, size)],
            send_sem=pair_send.at[slot, part],
            recv_sem=pair_recv.at[slot, part],
            device_id=(1 - core, place),
            device_id_type=MESH,
        )

    for slot in CHILDREN[0][0]:
        id_copy(slot).start()
    for part, slot in ROOT_ORDER:
        row_copy(part, slot).start()
    id_pair_copy(0).start()
    for part in range(NPART):
        pair_copy(0, part).start()

    best[...] = jnp.full(best.shape, -1.0, jnp.float32)
    side[...] = jnp.full(side.shape, -1.0, jnp.float32)

    def forward(slot, part):
        row_copy(part, slot).wait_recv()
        for child in CHILDREN[part].get(slot, ()):
            row_copy(part, child).start()
        if slot in PAIRED:
            pair_copy(slot, part).start()
        if part == 0:
            id_copy(slot).wait_recv()
            for child in CHILDREN[part].get(slot, ()):
                id_copy(child).start()
            if slot in PAIRED:
                id_pair_copy(slot).start()

    def take_pair(slot):
        id_pair_copy(slot).wait_recv()
        for part in range(NPART):
            pair_copy(slot, part).wait_recv()

    def give_back(index, carry):
        slots = [packed(BACKS, BACK_GROUP * index + u) for u in range(BACK_GROUP)]
        for slot in slots:
            padded = jnp.concatenate([side[slot], jnp.full((PAD - half, 128), -1.0, jnp.float32)], axis=0)
            turned_side = jnp.max(padded.T.reshape(128 // 8, 8, PAD), axis=0)
            turned_side = jnp.max(turned_side, axis=0, keepdims=True)
            high = jnp.max(best[slot], axis=0, keepdims=True)
            back_out[slot, 0, :, :half] = jnp.maximum(high[:, :half], turned_side[:, :half])
            back_out[slot, 1, :, :half] = high[:, half:]
        for slot in slots:
            where = source[1]
            for k in range(2, NSLOT):
                where = jnp.where(slot == k, source[k], where)

            @pl.when(slot > 0)
            def _():
                back_copy(slot, where).start()

        return carry

    def products_of(p, qs, same):
        right = jnp.concatenate([part for q in qs for part in (own[q], other[q])], axis=0)
        left_id = jnp.broadcast_to(ids[0, p], (128, PAD)).T[:half]
        right_ids = [jnp.concatenate([ids[0, q, :, :half], ids[1, q, :, :half]], axis=1) for q in qs]
        row_best = side[p]
        for begin in range(0, 2 * half * len(qs), PAD):
            end = min(begin + PAD, 2 * half * len(qs))
            products = lax.dot_general(
                own[p], right[begin:end], (((1,), (1,)), ((), ())), preferred_element_type=jnp.float32
            )
            for k in range(begin, end, 128):
                u, first = k // (2 * half), k % (2 * half)
                q, lanes = qs[u], slice(first, first + 128)
                allowed = left_id == right_ids[u][:, lanes]
                if same:
                    row = lax.broadcasted_iota(jnp.int32, (half, 128), 0)
                    column = lax.broadcasted_iota(jnp.int32, (half, 128), 1) + first
                    allowed = allowed & (row != column)
                masked = jnp.where(allowed, products[:, k - begin : k - begin + 128], -1.0)
                row_best = jnp.maximum(row_best, masked)
                best[q, :, lanes] = jnp.maximum(
                    best[q, :, lanes], jnp.max(masked.reshape(half // 8, 8, 128), axis=0)
                )
        side[p] = row_best

    def multiply(index, carry):
        products_of(packed(LEFTS, index), [packed(rights, index) for rights in RIGHTS], False)
        return carry

    actions = {
        "f": forward,
        "d": take_pair,
        "s": lambda: products_of(0, [0], True),
    }

    def segment(seg, carry):
        for k, (events, _, _) in enumerate(SEGMENTS):
            if events:

                @pl.when(seg == k)
                def _():
                    for name, *where in events:
                        actions[name](*where)

        lax.fori_loop(start_of(seg, 1), start_of(seg + 1, 1), multiply, carry)
        first, end = start_of(seg, 2) // BACK_GROUP, start_of(seg + 1, 2) // BACK_GROUP
        return lax.fori_loop(first, end, give_back, carry)

    lax.fori_loop(0, NSEG, segment, 0)

    result = back_out[0]
    for slot in range(1, NSLOT):
        back_copy(slot, source[slot]).wait_recv()
        result = jnp.maximum(result, back[slot])
    swap_out[...] = result[1]
    swapping = pltpu.make_async_remote_copy(
        src_ref=swap_out,
        dst_ref=swap,
        send_sem=swap_sem.at[0],
        recv_sem=swap_sem.at[1],
        device_id=(1 - core, place),
        device_id_type=MESH,
    )
    swapping.start()

    for part in range(NPART):
        for slot in range(1, NSLOT):
            row_copy(part, slot).wait_send()
        for slot in sorted(PAIRED):
            pair_copy(slot, part).wait_send()
    for slot in sorted(PAIRED):
        id_pair_copy(slot).wait_send()
    for slot in range(1, NSLOT):
        id_copy(slot).wait_send()
        back_copy(slot, source[slot]).wait_send()
    swapping.wait()
    o_ref[...] = jnp.maximum(result[0], swap[...])[:, :half]


def local(embeddings, cluster):
    half, width = embeddings.shape
    best = pl.pallas_call(
        kernel,
        out_shape=jax.ShapeDtypeStruct((1, half), jnp.float32),
        in_specs=[pl.BlockSpec(memory_space=pl.ANY)] * 2,
        out_specs=pl.BlockSpec(memory_space=pltpu.VMEM),
        scratch_shapes=[
            pltpu.VMEM((half, width), jnp.bfloat16),
            pltpu.VMEM((1, half), jnp.int32),
            pltpu.VMEM((NSLOT, half, width), jnp.bfloat16),
            pltpu.VMEM((NSLOT, half, width), jnp.bfloat16),
            pltpu.VMEM((2, NSLOT, 1, PAD), jnp.float32),
            pltpu.VMEM((NSLOT, half, 128), jnp.float32),
            pltpu.VMEM((NSLOT, 8, 2 * half), jnp.float32),
            pltpu.VMEM((NSLOT, 2, 1, PAD), jnp.float32),
            pltpu.VMEM((NSLOT, 2, 1, PAD), jnp.float32),
            pltpu.VMEM((1, PAD), jnp.float32),
            pltpu.VMEM((1, PAD), jnp.float32),
            pltpu.SemaphoreType.DMA((NPART + 1,)),
            pltpu.SemaphoreType.DMA((NSLOT, NPART)),
            pltpu.SemaphoreType.DMA((NSLOT, NPART)),
            pltpu.SemaphoreType.DMA((NSLOT, NPART)),
            pltpu.SemaphoreType.DMA((NSLOT, NPART)),
            pltpu.SemaphoreType.DMA((2, NSLOT)),
            pltpu.SemaphoreType.DMA((2, NSLOT)),
            pltpu.SemaphoreType.DMA((NSLOT,)),
            pltpu.SemaphoreType.DMA((NSLOT,)),
            pltpu.SemaphoreType.DMA((2,)),
        ],
        compiler_params=pltpu.CompilerParams(
            collective_id=0, has_side_effects=True, vmem_limit_bytes=56 * 1024 * 1024
        ),
        cost_estimate=pl.CostEstimate(
            flops=4 * GROUP * len(LEFTS) * half * half * width, bytes_accessed=2 * half * width, transcendentals=half
        ),
    )(embeddings, cluster.reshape(1, half))
    return best.reshape(half)


def solution(mesh):
    return jax.shard_map(
        local,
        mesh=mesh,
        in_specs=(P(("gx", "gy"), None), P(("gx", "gy"))),
        out_specs=P(("gx", "gy")),
        check_vma=False,
    )
```

```python
import jax
import jax.numpy as jnp
from jax import lax
from jax.experimental import pallas as pl
from jax.experimental.pallas import tpu as pltpu
from jax.sharding import PartitionSpec as P

EPS = 1e-06
TURNS = (
    (0, 1, 2, 3, 4, 5),
    (0, 1, 2, 3, 5, 4),
    (0, 1, 3, 2, 4, 5),
    (0, 1, 3, 2, 5, 4),
    (1, 0, 2, 3, 4, 5),
    (1, 0, 2, 3, 5, 4),
    (1, 0, 3, 2, 4, 5),
    (1, 0, 3, 2, 5, 4),
)
TURN_OF = [0, 4, 4, 0, 2, 6, 6, 2, 2, 6, 6, 2, 0, 4, 4, 0, 1, 5, 5, 1, 3, 7, 7, 3, 3, 7, 7, 3, 1, 5, 5, 1, 1, 5, 5, 1, 3, 7, 7, 3, 3, 7, 7, 3, 1, 5, 5, 1, 0, 4, 4, 0, 2, 6, 6, 2, 2, 6, 6, 2, 0, 4, 4, 0]
SOURCES = (0, 4, 2, 1, 32, 20, 9, 3, 11, 48, 28, 60)
PARTS = ((0, 64), (64, 64), (128, 64))
TREES = (
    {1: (0, 3), 2: (0, 0), 3: (0, 1), 4: (0, 4), 5: (1, 5), 6: (3, 2), 7: (3, 1), 8: (7, 2), 9: (4, 4), 10: (5, 3), 11: (10, 5)},
    {1: (0, 3), 2: (0, 0), 3: (0, 1), 4: (0, 4), 5: (1, 5), 6: (3, 2), 7: (2, 0), 8: (6, 1), 9: (4, 4), 10: (5, 3), 11: (10, 5)},
    {1: (0, 3), 2: (0, 0), 3: (0, 1), 4: (0, 4), 5: (1, 5), 6: (3, 2), 7: (2, 0), 8: (6, 1), 9: (4, 4), 10: (5, 3), 11: (10, 5)},
)
CHILDREN = (
    {0: (1, 3, 4, 2), 1: (5,), 3: (7, 6), 4: (9,), 5: (10,), 7: (8,), 10: (11,)},
    {0: (1, 3, 2, 4), 1: (5,), 2: (7,), 3: (6,), 4: (9,), 5: (10,), 6: (8,), 10: (11,)},
    {0: (1, 3, 2, 4), 1: (5,), 2: (7,), 3: (6,), 4: (9,), 5: (10,), 6: (8,), 10: (11,)},
)
GROUP = 2
ROOT_ORDER = ((0, 1), (0, 3), (0, 4), (1, 2), (1, 1), (1, 3), (1, 4), (2, 2), (0, 2), (2, 1), (2, 3), (2, 4))
PAIRED = frozenset((0, 1, 2, 4, 5, 6, 7, 9))
SEGMENTS = (
    (
        (('d', 0), ('s',), ('f', 1, 0), ('f', 2, 1), ('f', 3, 0), ('f', 4, 0), ('f', 1, 1), ('f', 2, 2), ('f', 3, 1), ('f', 4, 1), ('f', 5, 0), ('f', 6, 0), ('f', 1, 2), ('f', 2, 0), ('f', 3, 2), ('f', 4, 2)),
        ((1, 0, 0),),
        (),
    ),
    (
        (('f', 5, 1), ('f', 6, 1), ('d', 1)),
        ((2, 0, 1),),
        (),
    ),
    (
        (('d', 2),),
        ((3, 1, 2), (4, 0, 1)),
        (),
    ),
    (
        (('f', 7, 0), ('f', 7, 1), ('f', 9, 0), ('f', 10, 0)),
        ((4, 2, 2),),
        (),
    ),
    (
        (('f', 5, 2), ('f', 6, 2), ('d', 4)),
        ((5, 2, 4), (6, 1, 2)),
        (),
    ),
    (
        (('f', 7, 2), ('f', 8, 1), ('f', 9, 1), ('f', 10, 1), ('d', 5)),
        ((3, 4, 5),),
        (),
    ),
    (
        (('f', 8, 0), ('f', 11, 0)),
        ((6, 5, 4), (7, 4, 5)),
        (),
    ),
    (
        (('f', 8, 2), ('f', 9, 2), ('f', 10, 2)),
        ((8, 1, 4), (9, 0, 5)),
        (),
    ),
    (
        (('f', 11, 1), ('d', 9)),
        ((8, 5, 9),),
        (),
    ),
    (
        (('d', 7),),
        ((9, 7, 2), (10, 0, 4)),
        (),
    ),
    (
        (('d', 6),),
        ((10, 2, 6),),
        (),
    ),
    (
        (('f', 11, 2),),
        ((11, 2, 7), (11, 9, 6), (9, 6, 6)),
        (1, 2, 3, 4, 5, 6, 7, 8, 0, 9, 10, 11),
    ),
)

MESH = pl.DeviceIdType.MESH
NSLOT = len(SOURCES)
NPART = len(PARTS)
NSEG = len(SEGMENTS)
LEFTS = [group[0] for _, groups, _ in SEGMENTS for group in groups]
RIGHTS = [[group[1 + u] for _, groups, _ in SEGMENTS for group in groups] for u in range(GROUP)]
BACKS = [slot for _, _, slots in SEGMENTS for slot in slots]
BACK_GROUP = 4
PAD = 256


def packed(digits, index):
    word = jnp.int32(0)
    for k in range(0, len(digits), 8):
        value = sum(d << (4 * j) for j, d in enumerate(digits[k : k + 8]))
        value = value - (1 << 32) if value >> 31 else value
        word = jnp.where(index // 8 == k // 8, jnp.int32(value), word)
    return lax.shift_right_logical(word, 4 * (index % 8)) & 15


def start_of(seg, column):
    first = jnp.int32(0)
    for k, segment in enumerate(SEGMENTS):
        if segment[column]:
            first = first + jnp.where(seg > k, len(segment[column]), 0)
    return first


def gray(code):
    return code ^ ((code >> 1) & 21)


def turned(turn, word):
    return sum(1 << TURNS[turn][k] for k in range(6) if word >> k & 1)


def kernel(
    x_hbm, c_hbm, o_ref, x_ref, c_ref, own, other, ids, side, best, back, back_out,
    load_sem, row_send, row_recv, pair_send, pair_recv, id_send, id_recv, back_send, back_recv,
):
    core = lax.axis_index("gx")
    place = lax.axis_index("gy")
    half = x_ref.shape[0]

    loads = [
        pltpu.make_async_copy(
            x_hbm.at[pl.ds(begin, size)], x_ref.at[pl.ds(begin, size)], load_sem.at[part]
        )
        for part, (begin, size) in enumerate(PARTS)
    ]
    loads.append(pltpu.make_async_copy(c_hbm, c_ref, load_sem.at[NPART]))
    for load in loads:
        load.start()

    corner = gray(place)
    turn = packed(TURN_OF, corner)

    def chip(word):
        values = [turned(t, word) for t in range(len(TURNS))]
        there = jnp.int32(values[0])
        for value in sorted(set(values) - {values[0]}):
            hits = turn < 0
            for t, v in enumerate(values):
                if v == value:
                    hits = hits | (turn == t)
            there = jnp.where(hits, value, there)
        return gray(corner ^ there)

    step_to = [chip(1 << k) for k in range(6)]

    barrier = pltpu.get_barrier_semaphore()
    for where in step_to:
        pl.semaphore_signal(barrier, inc=1, device_id=(core, where), device_id_type=MESH)
    pl.semaphore_signal(barrier, inc=1, device_id=(1 - core, place), device_id_type=MESH)

    source = [place] + [chip(w) for w in SOURCES[1:]]

    loads[NPART].wait()
    cluster = c_ref[...].astype(jnp.float32)
    ids[0, 0] = jnp.concatenate([cluster, jnp.full((1, PAD - half), -2.0, jnp.float32)], axis=1)

    def normalize(part):
        begin, size = PARTS[part]
        loads[part].wait()
        values = x_ref[begin : begin + size, :].astype(jnp.float32)
        total = jnp.sum(values * values, axis=1, keepdims=True)
        own[0, begin : begin + size, :] = (values * lax.rsqrt(total + EPS)).astype(jnp.bfloat16)

    def id_copy(slot):
        parent, step = TREES[0][slot]
        return pltpu.make_async_remote_copy(
            src_ref=ids.at[0, parent],
            dst_ref=ids.at[0, slot],
            send_sem=id_send.at[0, slot],
            recv_sem=id_recv.at[0, slot],
            device_id=(core, step_to[step]),
            device_id_type=MESH,
        )

    def id_pair_copy(slot):
        return pltpu.make_async_remote_copy(
            src_ref=ids.at[0, slot],
            dst_ref=ids.at[1, slot],
            send_sem=id_send.at[1, slot],
            recv_sem=id_recv.at[1, slot],
            device_id=(1 - core, place),
            device_id_type=MESH,
        )

    def back_copy(slot, which, where):
        return pltpu.make_async_remote_copy(
            src_ref=back_out.at[slot, which],
            dst_ref=back.at[slot, which],
            send_sem=back_send.at[slot, which],
            recv_sem=back_recv.at[slot, which],
            device_id=(1 - core if which else core, where),
            device_id_type=MESH,
        )

    def row_copy(part, slot):
        begin, size = PARTS[part]
        parent, step = TREES[part][slot]
        return pltpu.make_async_remote_copy(
            src_ref=own.at[parent, pl.ds(begin, size)],
            dst_ref=own.at[slot, pl.ds(begin, size)],
            send_sem=row_send.at[slot, part],
            recv_sem=row_recv.at[slot, part],
            device_id=(core, step_to[step]),
            device_id_type=MESH,
        )

    def pair_copy(slot, part):
        begin, size = PARTS[part]
        return pltpu.make_async_remote_copy(
            src_ref=own.at[slot, pl.ds(begin, size)],
            dst_ref=other.at[slot, pl.ds(begin, size)],
            send_sem=pair_send.at[slot, part],
            recv_sem=pair_recv.at[slot, part],
            device_id=(1 - core, place),
            device_id_type=MESH,
        )

    normalized = 0
    for part, slot in ROOT_ORDER:
        if part >= normalized:
            normalize(part)
            if part == 0:
                pl.semaphore_wait(barrier, 7)
            normalized = part + 1
        row_copy(part, slot).start()
        if part == 0:
            id_copy(slot).start()
    id_pair_copy(0).start()
    for part in range(NPART):
        pair_copy(0, part).start()

    best[...] = jnp.full(best.shape, -1.0, jnp.float32)
    side[...] = jnp.full(side.shape, -1.0, jnp.float32)

    def forward(slot, part):
        row_copy(part, slot).wait_recv()
        for child in CHILDREN[part].get(slot, ()):
            row_copy(part, child).start()
        if slot in PAIRED:
            pair_copy(slot, part).start()
        if part == 0:
            id_copy(slot).wait_recv()
            for child in CHILDREN[part].get(slot, ()):
                id_copy(child).start()
            if slot in PAIRED:
                id_pair_copy(slot).start()

    def take_pair(slot):
        id_pair_copy(slot).wait_recv()
        for part in range(NPART):
            pair_copy(slot, part).wait_recv()

    def give_back(index, carry):
        slots = [packed(BACKS, BACK_GROUP * index + u) for u in range(BACK_GROUP)]
        for slot in slots:
            padded = jnp.concatenate([side[slot], jnp.full((PAD - half, 128), -1.0, jnp.float32)], axis=0)
            turned_side = jnp.max(padded.T.reshape(128 // 8, 8, PAD), axis=0)
            turned_side = jnp.max(turned_side, axis=0, keepdims=True)
            high = jnp.max(best[slot], axis=0, keepdims=True)
            back_out[slot, 0, :, :half] = jnp.maximum(high[:, :half], turned_side[:, :half])
            back_out[slot, 1, :, :half] = high[:, half:]
        for slot in slots:
            where = source[0]
            whole = slot == 0
            for k in range(1, NSLOT):
                where = jnp.where(slot == k, source[k], where)
                if k in PAIRED:
                    whole = whole | (slot == k)

            @pl.when(slot > 0)
            def _():
                back_copy(slot, 0, where).start()

            @pl.when(whole)
            def _():
                back_copy(slot, 1, where).start()

        return carry

    def products_of(p, qs, same):
        right = jnp.concatenate([part for q in qs for part in (own[q], other[q])], axis=0)
        left_id = jnp.broadcast_to(ids[0, p], (128, PAD)).T[:half]
        right_ids = [jnp.concatenate([ids[0, q, :, :half], ids[1, q, :, :half]], axis=1) for q in qs]
        row_best = side[p]
        for begin in range(0, 2 * half * len(qs), PAD):
            end = min(begin + PAD, 2 * half * len(qs))
            products = lax.dot_general(
                own[p], right[begin:end], (((1,), (1,)), ((), ())), preferred_element_type=jnp.float32
            )
            for k in range(begin, end, 128):
                u, first = k // (2 * half), k % (2 * half)
                q, lanes = qs[u], slice(first, first + 128)
                allowed = left_id == right_ids[u][:, lanes]
                if same:
                    row = lax.broadcasted_iota(jnp.int32, (half, 128), 0)
                    column = lax.broadcasted_iota(jnp.int32, (half, 128), 1) + first
                    allowed = allowed & (row != column)
                masked = jnp.where(allowed, products[:, k - begin : k - begin + 128], -1.0)
                row_best = jnp.maximum(row_best, masked)
                best[q, :, lanes] = jnp.maximum(
                    best[q, :, lanes], jnp.max(masked.reshape(half // 8, 8, 128), axis=0)
                )
        side[p] = row_best

    def multiply(index, carry):
        products_of(packed(LEFTS, index), [packed(rights, index) for rights in RIGHTS], False)
        return carry

    actions = {
        "f": forward,
        "d": take_pair,
        "s": lambda: products_of(0, [0], True),
    }

    def segment(seg, carry):
        for k, (events, _, _) in enumerate(SEGMENTS):
            if events:

                @pl.when(seg == k)
                def _():
                    for name, *where in events:
                        actions[name](*where)

        lax.fori_loop(start_of(seg, 1), start_of(seg + 1, 1), multiply, carry)
        first, end = start_of(seg, 2) // BACK_GROUP, start_of(seg + 1, 2) // BACK_GROUP
        return lax.fori_loop(first, end, give_back, carry)

    lax.fori_loop(0, NSEG, segment, 0)

    returned = [(slot, 0) for slot in range(1, NSLOT)] + [(slot, 1) for slot in sorted(PAIRED)]
    result = back_out[0, 0]
    for slot, which in returned:
        back_copy(slot, which, source[slot]).wait_recv()
        result = jnp.maximum(result, back[slot, which])
    o_ref[...] = result[:, :half]

    for part in range(NPART):
        for slot in range(1, NSLOT):
            row_copy(part, slot).wait_send()
        for slot in sorted(PAIRED):
            pair_copy(slot, part).wait_send()
    for slot in sorted(PAIRED):
        id_pair_copy(slot).wait_send()
    for slot in range(1, NSLOT):
        id_copy(slot).wait_send()
    for slot, which in returned:
        back_copy(slot, which, source[slot]).wait_send()


def local(embeddings, cluster):
    half, width = embeddings.shape
    best = pl.pallas_call(
        kernel,
        out_shape=jax.ShapeDtypeStruct((1, half), jnp.float32),
        in_specs=[pl.BlockSpec(memory_space=pl.ANY)] * 2,
        out_specs=pl.BlockSpec(memory_space=pltpu.VMEM),
        scratch_shapes=[
            pltpu.VMEM((half, width), jnp.bfloat16),
            pltpu.VMEM((1, half), jnp.int32),
            pltpu.VMEM((NSLOT, half, width), jnp.bfloat16),
            pltpu.VMEM((NSLOT, half, width), jnp.bfloat16),
            pltpu.VMEM((2, NSLOT, 1, PAD), jnp.float32),
            pltpu.VMEM((NSLOT, half, 128), jnp.float32),
            pltpu.VMEM((NSLOT, 8, 2 * half), jnp.float32),
            pltpu.VMEM((NSLOT, 2, 1, PAD), jnp.float32),
            pltpu.VMEM((NSLOT, 2, 1, PAD), jnp.float32),
            pltpu.SemaphoreType.DMA((NPART + 1,)),
            pltpu.SemaphoreType.DMA((NSLOT, NPART)),
            pltpu.SemaphoreType.DMA((NSLOT, NPART)),
            pltpu.SemaphoreType.DMA((NSLOT, NPART)),
            pltpu.SemaphoreType.DMA((NSLOT, NPART)),
            pltpu.SemaphoreType.DMA((2, NSLOT)),
            pltpu.SemaphoreType.DMA((2, NSLOT)),
            pltpu.SemaphoreType.DMA((NSLOT, 2)),
            pltpu.SemaphoreType.DMA((NSLOT, 2)),
        ],
        compiler_params=pltpu.CompilerParams(
            collective_id=0, has_side_effects=True, vmem_limit_bytes=56 * 1024 * 1024
        ),
        cost_estimate=pl.CostEstimate(
            flops=4 * GROUP * len(LEFTS) * half * half * width, bytes_accessed=2 * half * width, transcendentals=half
        ),
    )(embeddings, cluster.reshape(1, half))
    return best.reshape(half)


def solution(mesh):
    return jax.shard_map(
        local,
        mesh=mesh,
        in_specs=(P(("gx", "gy"), None), P(("gx", "gy"))),
        out_specs=P(("gx", "gy")),
        check_vma=False,
    )
```

```python
import jax
import jax.numpy as jnp
from jax import lax
from jax.experimental import pallas as pl
from jax.experimental.pallas import tpu as pltpu
from jax.sharding import PartitionSpec as P

EPS = 1e-06
TURNS = (
    (0, 1, 2, 3, 4, 5),
    (0, 1, 2, 3, 5, 4),
    (0, 1, 3, 2, 4, 5),
    (0, 1, 3, 2, 5, 4),
    (1, 0, 2, 3, 4, 5),
    (1, 0, 2, 3, 5, 4),
    (1, 0, 3, 2, 4, 5),
    (1, 0, 3, 2, 5, 4),
)
TURN_OF = [0, 4, 4, 0, 2, 6, 6, 2, 2, 6, 6, 2, 0, 4, 4, 0, 1, 5, 5, 1, 3, 7, 7, 3, 3, 7, 7, 3, 1, 5, 5, 1, 1, 5, 5, 1, 3, 7, 7, 3, 3, 7, 7, 3, 1, 5, 5, 1, 0, 4, 4, 0, 2, 6, 6, 2, 2, 6, 6, 2, 0, 4, 4, 0]
SOURCES = (0, 4, 8, 2, 9, 32, 52, 48, 20, 3, 11, 25)
PARTS = ((0, 64), (64, 64), (128, 64))
TREES = (
    {1: (0, 3), 2: (0, 2), 3: (0, 0), 4: (2, 1), 5: (0, 4), 6: (7, 3), 7: (5, 4), 8: (6, 4), 9: (3, 0), 10: (9, 2), 11: (4, 5)},
    {1: (0, 3), 2: (0, 2), 3: (0, 0), 4: (2, 1), 5: (0, 4), 6: (7, 3), 7: (5, 4), 8: (1, 5), 9: (3, 0), 10: (4, 1), 11: (4, 5)},
    {1: (0, 3), 2: (0, 2), 3: (0, 0), 4: (2, 1), 5: (0, 4), 6: (8, 5), 7: (6, 2), 8: (1, 5), 9: (3, 0), 10: (4, 1), 11: (4, 5)},
)
CHILDREN = (
    {0: (5, 3, 2, 1), 2: (4,), 3: (9,), 4: (11,), 5: (7,), 6: (8,), 7: (6,), 9: (10,)},
    {0: (2, 5, 1, 3), 1: (8,), 2: (4,), 3: (9,), 4: (10, 11), 5: (7,), 7: (6,)},
    {0: (1, 2, 3, 5), 1: (8,), 2: (4,), 3: (9,), 4: (10, 11), 6: (7,), 8: (6,)},
)
GROUP = 4
ROOT_ORDER = ((0, 2), (0, 3), (0, 5), (2, 1), (1, 1), (1, 2), (1, 3), (1, 5), (0, 1), (2, 2), (2, 3), (2, 5))
PAIRED = frozenset((0, 1, 2, 3, 4, 9, 10, 11))
SEGMENTS = (
    (
        (('f', 1, 2), ('f', 2, 0), ('f', 3, 0), ('f', 5, 0), ('d', 0), ('s',), ('f', 1, 1), ('f', 2, 1), ('f', 3, 1), ('f', 5, 1), ('f', 4, 0), ('f', 8, 2), ('f', 1, 0), ('f', 2, 2), ('f', 7, 0), ('f', 9, 0), ('f', 4, 1), ('f', 8, 1), ('f', 3, 2), ('f', 7, 1), ('f', 4, 2), ('f', 6, 0), ('f', 6, 2), ('f', 10, 0), ('d', 3)),
        ((3, 1, 4, 0, 2),),
        (),
    ),
    (
        (('f', 5, 2), ('f', 9, 1), ('d', 1)),
        ((1, 4, 5, 0, 2),),
        (),
    ),
    (
        (('f', 6, 1), ('f', 10, 1), ('f', 11, 0), ('f', 7, 2), ('f', 8, 0), ('f', 9, 2), ('d', 2)),
        ((2, 6, 7, 5, 8),),
        (),
    ),
    (
        (('f', 10, 2), ('f', 11, 1)),
        ((3, 8, 7, 5, 6),),
        (),
    ),
    (
        (('d', 9),),
        ((9, 7, 8, 5, 0),),
        (),
    ),
    (
        (('f', 11, 2),),
        ((1, 8, 10, 11, 6),),
        (),
    ),
    (
        (('d', 10),),
        ((10, 8, 7, 5, 6),),
        (),
    ),
    (
        (('d', 4),),
        ((4, 7, 5, 8, 6),),
        (),
    ),
    (
        (('d', 11),),
        ((11, 9, 2, 7, 7),),
        (0, 1, 2, 3, 4, 5, 6, 7, 8, 9, 10, 11),
    ),
)

MESH = pl.DeviceIdType.MESH
NSLOT = len(SOURCES)
NPART = len(PARTS)
NSEG = len(SEGMENTS)
LEFTS = [group[0] for _, groups, _ in SEGMENTS for group in groups]
RIGHTS = [[group[1 + u] for _, groups, _ in SEGMENTS for group in groups] for u in range(GROUP)]
BACKS = [slot for _, _, slots in SEGMENTS for slot in slots]
BACK_GROUP = 4
PAD = 256


def packed(digits, index):
    word = jnp.int32(0)
    for k in range(0, len(digits), 8):
        value = sum(d << (4 * j) for j, d in enumerate(digits[k : k + 8]))
        value = value - (1 << 32) if value >> 31 else value
        word = jnp.where(index // 8 == k // 8, jnp.int32(value), word)
    return lax.shift_right_logical(word, 4 * (index % 8)) & 15


def start_of(seg, column):
    first = jnp.int32(0)
    for k, segment in enumerate(SEGMENTS):
        if segment[column]:
            first = first + jnp.where(seg > k, len(segment[column]), 0)
    return first


def gray(code):
    return code ^ ((code >> 1) & 21)


def turned(turn, word):
    return sum(1 << TURNS[turn][k] for k in range(6) if word >> k & 1)


def kernel(
    x_hbm, c_hbm, o_ref, x_ref, c_ref, own, other, ids, side, best, back, back_out,
    load_sem, row_send, row_recv, pair_send, pair_recv, id_send, id_recv, back_send, back_recv,
):
    core = lax.axis_index("gx")
    place = lax.axis_index("gy")
    half = x_ref.shape[0]

    loads = [
        pltpu.make_async_copy(
            x_hbm.at[pl.ds(begin, size)], x_ref.at[pl.ds(begin, size)], load_sem.at[part]
        )
        for part, (begin, size) in enumerate(PARTS)
    ]
    loads.append(pltpu.make_async_copy(c_hbm, c_ref, load_sem.at[NPART]))
    for load in loads:
        load.start()

    corner = gray(place)
    turn = packed(TURN_OF, corner)

    def chip(word):
        values = [turned(t, word) for t in range(len(TURNS))]
        there = jnp.int32(values[0])
        for value in sorted(set(values) - {values[0]}):
            hits = turn < 0
            for t, v in enumerate(values):
                if v == value:
                    hits = hits | (turn == t)
            there = jnp.where(hits, value, there)
        return gray(corner ^ there)

    step_to = [chip(1 << k) for k in range(6)]

    barrier = pltpu.get_barrier_semaphore()
    for where in step_to:
        pl.semaphore_signal(barrier, inc=1, device_id=(core, where), device_id_type=MESH)
    pl.semaphore_signal(barrier, inc=1, device_id=(1 - core, place), device_id_type=MESH)

    source = [place] + [chip(w) for w in SOURCES[1:]]

    loads[NPART].wait()
    cluster = c_ref[...].astype(jnp.float32)
    ids[0, 0] = jnp.concatenate([cluster, jnp.full((1, PAD - half), -2.0, jnp.float32)], axis=1)

    def normalize(part):
        begin, size = PARTS[part]
        loads[part].wait()
        values = x_ref[begin : begin + size, :].astype(jnp.float32)
        total = jnp.sum(values * values, axis=1, keepdims=True)
        own[0, begin : begin + size, :] = (values * lax.rsqrt(total + EPS)).astype(jnp.bfloat16)

    def id_copy(slot):
        parent, step = TREES[0][slot]
        return pltpu.make_async_remote_copy(
            src_ref=ids.at[0, parent],
            dst_ref=ids.at[0, slot],
            send_sem=id_send.at[0, slot],
            recv_sem=id_recv.at[0, slot],
            device_id=(core, step_to[step]),
            device_id_type=MESH,
        )

    def id_pair_copy(slot):
        return pltpu.make_async_remote_copy(
            src_ref=ids.at[0, slot],
            dst_ref=ids.at[1, slot],
            send_sem=id_send.at[1, slot],
            recv_sem=id_recv.at[1, slot],
            device_id=(1 - core, place),
            device_id_type=MESH,
        )

    def back_copy(slot, which, where):
        return pltpu.make_async_remote_copy(
            src_ref=back_out.at[slot, which],
            dst_ref=back.at[slot, which],
            send_sem=back_send.at[slot, which],
            recv_sem=back_recv.at[slot, which],
            device_id=(1 - core if which else core, where),
            device_id_type=MESH,
        )

    def row_copy(part, slot):
        begin, size = PARTS[part]
        parent, step = TREES[part][slot]
        return pltpu.make_async_remote_copy(
            src_ref=own.at[parent, pl.ds(begin, size)],
            dst_ref=own.at[slot, pl.ds(begin, size)],
            send_sem=row_send.at[slot, part],
            recv_sem=row_recv.at[slot, part],
            device_id=(core, step_to[step]),
            device_id_type=MESH,
        )

    def pair_copy(slot, part):
        begin, size = PARTS[part]
        return pltpu.make_async_remote_copy(
            src_ref=own.at[slot, pl.ds(begin, size)],
            dst_ref=other.at[slot, pl.ds(begin, size)],
            send_sem=pair_send.at[slot, part],
            recv_sem=pair_recv.at[slot, part],
            device_id=(1 - core, place),
            device_id_type=MESH,
        )

    normalized = 0
    for part, slot in ROOT_ORDER:
        while normalized <= part:
            normalize(normalized)
            if normalized == 0:
                pl.semaphore_wait(barrier, 7)
            normalized += 1
        row_copy(part, slot).start()
        if part == 0:
            id_copy(slot).start()
    id_pair_copy(0).start()
    for part in range(NPART):
        pair_copy(0, part).start()

    best[...] = jnp.full(best.shape, -1.0, jnp.float32)
    side[...] = jnp.full(side.shape, -1.0, jnp.float32)

    def forward(slot, part):
        row_copy(part, slot).wait_recv()
        for child in CHILDREN[part].get(slot, ()):
            row_copy(part, child).start()
        if slot in PAIRED:
            pair_copy(slot, part).start()
        if part == 0:
            id_copy(slot).wait_recv()
            for child in CHILDREN[part].get(slot, ()):
                id_copy(child).start()
            if slot in PAIRED:
                id_pair_copy(slot).start()

    def take_pair(slot):
        id_pair_copy(slot).wait_recv()
        for part in range(NPART):
            pair_copy(slot, part).wait_recv()

    def give_back(index, carry):
        slots = [packed(BACKS, BACK_GROUP * index + u) for u in range(BACK_GROUP)]
        for slot in slots:
            turned_side = jnp.max(side[slot].T.reshape(128 // 8, 8, 2 * half), axis=0)
            turned_side = jnp.max(turned_side, axis=0, keepdims=True)
            high = jnp.max(best[slot], axis=0, keepdims=True)
            back_out[slot, 0, :, :half] = jnp.maximum(high[:, :half], turned_side[:, :half])
            back_out[slot, 1, :, :half] = turned_side[:, half:]
        for slot in slots:
            where = source[0]
            whole = slot == 0
            for k in range(1, NSLOT):
                where = jnp.where(slot == k, source[k], where)
                if k in PAIRED:
                    whole = whole | (slot == k)

            @pl.when(slot > 0)
            def _():
                back_copy(slot, 0, where).start()

            @pl.when(whole)
            def _():
                back_copy(slot, 1, where).start()

        return carry

    def products_of(p, qs, same):
        left = jnp.concatenate([own[p], other[p]], axis=0)
        right = jnp.concatenate([own[q] for q in qs], axis=0)
        left_id = jnp.concatenate(
            [jnp.broadcast_to(ids[which, p], (128, PAD)).T[:half] for which in range(2)], axis=0
        )
        right_id = jnp.concatenate([ids[0, q, :, :half] for q in qs], axis=1)
        row_best = side[p]
        column_best = []
        for begin in range(0, half * len(qs), PAD):
            end = min(begin + PAD, half * len(qs))
            products = lax.dot_general(
                left, right[begin:end], (((1,), (1,)), ((), ())), preferred_element_type=jnp.float32
            )
            for k in range(begin, end, 128):
                allowed = left_id == right_id[:, k : k + 128]
                if same:
                    row = lax.broadcasted_iota(jnp.int32, (2 * half, 128), 0)
                    column = lax.broadcasted_iota(jnp.int32, (2 * half, 128), 1) + k
                    column = jnp.where(column >= half, column - half, column)
                    allowed = allowed & (row != column)
                masked = jnp.where(allowed, products[:, k - begin : k - begin + 128], -1.0)
                row_best = jnp.maximum(row_best, masked)
                column_best.append(jnp.max(masked.reshape(half // 4, 8, 128), axis=0))
        side[p] = row_best
        columns = jnp.concatenate(column_best, axis=1)
        for u, q in enumerate(qs):
            best[q, :, :half] = jnp.maximum(best[q, :, :half], columns[:, u * half : (u + 1) * half])

    def multiply(index, carry):
        products_of(packed(LEFTS, index), [packed(rights, index) for rights in RIGHTS], False)
        return carry

    actions = {
        "f": forward,
        "d": take_pair,
        "s": lambda: products_of(0, [0, 0], True),
    }

    def segment(seg, carry):
        for k, (events, _, _) in enumerate(SEGMENTS):
            if events:

                @pl.when(seg == k)
                def _():
                    for name, *where in events:
                        actions[name](*where)

        lax.fori_loop(start_of(seg, 1), start_of(seg + 1, 1), multiply, carry)
        first, end = start_of(seg, 2) // BACK_GROUP, start_of(seg + 1, 2) // BACK_GROUP
        return lax.fori_loop(first, end, give_back, carry)

    lax.fori_loop(0, NSEG, segment, 0)

    returned = [(slot, 0) for slot in range(1, NSLOT)] + [(slot, 1) for slot in sorted(PAIRED)]
    result = back_out[0, 0]
    for slot, which in returned:
        back_copy(slot, which, source[slot]).wait_recv()
        result = jnp.maximum(result, back[slot, which])
    o_ref[...] = result[:, :half]

    for part in range(NPART):
        for slot in range(1, NSLOT):
            row_copy(part, slot).wait_send()
        for slot in sorted(PAIRED):
            pair_copy(slot, part).wait_send()
    for slot in sorted(PAIRED):
        id_pair_copy(slot).wait_send()
    for slot in range(1, NSLOT):
        id_copy(slot).wait_send()
    for slot, which in returned:
        back_copy(slot, which, source[slot]).wait_send()


def local(embeddings, cluster):
    half, width = embeddings.shape
    best = pl.pallas_call(
        kernel,
        out_shape=jax.ShapeDtypeStruct((1, half), jnp.float32),
        in_specs=[pl.BlockSpec(memory_space=pl.ANY)] * 2,
        out_specs=pl.BlockSpec(memory_space=pltpu.VMEM),
        scratch_shapes=[
            pltpu.VMEM((half, width), jnp.bfloat16),
            pltpu.VMEM((1, half), jnp.int32),
            pltpu.VMEM((NSLOT, half, width), jnp.bfloat16),
            pltpu.VMEM((NSLOT, half, width), jnp.bfloat16),
            pltpu.VMEM((2, NSLOT, 1, PAD), jnp.float32),
            pltpu.VMEM((NSLOT, 2 * half, 128), jnp.float32),
            pltpu.VMEM((NSLOT, 8, PAD), jnp.float32),
            pltpu.VMEM((NSLOT, 2, 1, PAD), jnp.float32),
            pltpu.VMEM((NSLOT, 2, 1, PAD), jnp.float32),
            pltpu.SemaphoreType.DMA((NPART + 1,)),
            pltpu.SemaphoreType.DMA((NSLOT, NPART)),
            pltpu.SemaphoreType.DMA((NSLOT, NPART)),
            pltpu.SemaphoreType.DMA((NSLOT, NPART)),
            pltpu.SemaphoreType.DMA((NSLOT, NPART)),
            pltpu.SemaphoreType.DMA((2, NSLOT)),
            pltpu.SemaphoreType.DMA((2, NSLOT)),
            pltpu.SemaphoreType.DMA((NSLOT, 2)),
            pltpu.SemaphoreType.DMA((NSLOT, 2)),
        ],
        compiler_params=pltpu.CompilerParams(
            collective_id=0, has_side_effects=True, vmem_limit_bytes=56 * 1024 * 1024
        ),
        cost_estimate=pl.CostEstimate(
            flops=4 * GROUP * len(LEFTS) * half * half * width, bytes_accessed=2 * half * width, transcendentals=half
        ),
    )(embeddings, cluster.reshape(1, half))
    return best.reshape(half)


def solution(mesh):
    return jax.shard_map(
        local,
        mesh=mesh,
        in_specs=(P(("gx", "gy"), None), P(("gx", "gy"))),
        out_specs=P(("gx", "gy")),
        check_vma=False,
    )
```

```python
import jax
import jax.numpy as jnp
from jax import lax
from jax.experimental import pallas as pl
from jax.experimental.pallas import tpu as pltpu
from jax.sharding import PartitionSpec as P

EPS = 1e-06
TURNS = (
    (0, 1, 2, 3, 4, 5),
    (0, 1, 2, 3, 5, 4),
    (0, 1, 3, 2, 4, 5),
    (0, 1, 3, 2, 5, 4),
    (1, 0, 2, 3, 4, 5),
    (1, 0, 2, 3, 5, 4),
    (1, 0, 3, 2, 4, 5),
    (1, 0, 3, 2, 5, 4),
)
TURN_OF = [0, 4, 4, 0, 2, 6, 6, 2, 2, 6, 6, 2, 0, 4, 4, 0, 1, 5, 5, 1, 3, 7, 7, 3, 3, 7, 7, 3, 1, 5, 5, 1, 1, 5, 5, 1, 3, 7, 7, 3, 3, 7, 7, 3, 1, 5, 5, 1, 0, 4, 4, 0, 2, 6, 6, 2, 2, 6, 6, 2, 0, 4, 4, 0]
SOURCES = (0, 1, 34, 8, 5, 24, 2, 32, 50, 28, 21, 13)
PARTS = ((0, 32), (32, 32), (64, 64), (128, 64))
TREES = (
    {1: (0, 1), 2: (6, 4), 3: (0, 2), 4: (1, 3), 5: (3, 5), 6: (0, 0), 7: (2, 1), 8: (2, 4), 9: (5, 2), 10: (4, 5), 11: (4, 3)},
    {1: (0, 1), 2: (7, 0), 3: (0, 2), 4: (1, 3), 5: (3, 5), 6: (0, 0), 7: (0, 4), 8: (2, 4), 9: (5, 2), 10: (4, 5), 11: (4, 3)},
    {1: (0, 1), 2: (7, 0), 3: (0, 2), 4: (1, 3), 5: (3, 5), 6: (0, 0), 7: (0, 4), 8: (2, 4), 9: (5, 2), 10: (4, 5), 11: (4, 3)},
    {1: (0, 1), 2: (6, 4), 3: (0, 2), 4: (1, 3), 5: (3, 5), 6: (0, 0), 7: (2, 1), 8: (2, 4), 9: (5, 2), 10: (4, 5), 11: (4, 3)},
)
CHILDREN = (
    {0: (1, 6, 3), 1: (4,), 2: (8, 7), 3: (5,), 4: (10, 11), 5: (9,), 6: (2,)},
    {0: (1, 3, 7, 6), 1: (4,), 2: (8,), 3: (5,), 4: (10, 11), 5: (9,), 7: (2,)},
    {0: (1, 3, 7, 6), 1: (4,), 2: (8,), 3: (5,), 4: (10, 11), 5: (9,), 7: (2,)},
    {0: (1, 6, 3), 1: (4,), 2: (8, 7), 3: (5,), 4: (10, 11), 5: (9,), 6: (2,)},
)
GROUP = 2
ROOT_ORDER = ((0, 1), (0, 3), (0, 6), (1, 7))
PAIRED = frozenset((0, 1, 2, 3, 5, 6, 7, 8))
SEGMENTS = (
    (
        (('r', 1, 1), ('r', 1, 3), ('r', 3, 6), ('r', 2, 7), ('r', 2, 1), ('r', 2, 3), ('d', 0), ('s',), ('f', 1, 0), ('f', 3, 0), ('f', 6, 0), ('f', 7, 1), ('f', 1, 1), ('f', 3, 1), ('r', 3, 1), ('r', 3, 3), ('f', 4, 0), ('f', 5, 0), ('f', 6, 3), ('f', 7, 2), ('f', 4, 1), ('f', 5, 1), ('f', 1, 2), ('f', 2, 0), ('f', 2, 1), ('f', 3, 2), ('r', 1, 6), ('f', 10, 0), ('f', 11, 0), ('r', 2, 6), ('f', 1, 3), ('f', 2, 2), ('f', 2, 3), ('f', 3, 3)),
        ((1, 0, 0),),
        (),
    ),
    (
        (('f', 4, 2), ('f', 5, 2), ('d', 1)),
        ((2, 0, 1),),
        (),
    ),
    (
        (('f', 6, 1), ('f', 7, 0), ('f', 8, 0), ('f', 9, 0)),
        ((3, 0, 1),),
        (),
    ),
    (
        (('d', 2),),
        ((3, 2, 2),),
        (),
    ),
    (
        (('f', 8, 1), ('f', 9, 1), ('f', 4, 3), ('f', 5, 3), ('d', 3)),
        ((4, 3, 2),),
        (),
    ),
    (
        (('f', 6, 2), ('f', 7, 3)),
        ((5, 3, 0), (5, 2, 1)),
        (),
    ),
    (
        (('f', 10, 1), ('f', 11, 1), ('f', 8, 2), ('f', 9, 2), ('d', 7), ('d', 5)),
        ((4, 7, 5), (6, 3, 1)),
        (),
    ),
    (
        (('d', 6),),
        ((7, 5, 6),),
        (),
    ),
    (
        (('f', 10, 2), ('f', 11, 2), ('f', 8, 3), ('f', 9, 3)),
        ((8, 5, 0), (8, 1, 6), (9, 0, 2)),
        (),
    ),
    (
        (('d', 8),),
        ((4, 8, 6), (9, 6, 7)),
        (),
    ),
    (
        (('f', 10, 3), ('f', 11, 3)),
        ((10, 7, 1), (11, 1, 2), (11, 6, 8), (10, 8, 8)),
        (1, 2, 3, 4, 5, 6, 7, 8, 0, 9, 10, 11),
    ),
)

MESH = pl.DeviceIdType.MESH
NSLOT = len(SOURCES)
NPART = len(PARTS)
NSEG = len(SEGMENTS)
LEFTS = [group[0] for _, groups, _ in SEGMENTS for group in groups]
RIGHTS = [[group[1 + u] for _, groups, _ in SEGMENTS for group in groups] for u in range(GROUP)]
BACKS = [slot for _, _, slots in SEGMENTS for slot in slots]
BACK_GROUP = 4
PAD = 256


def packed(digits, index):
    word = jnp.int32(0)
    for k in range(0, len(digits), 8):
        value = sum(d << (4 * j) for j, d in enumerate(digits[k : k + 8]))
        value = value - (1 << 32) if value >> 31 else value
        word = jnp.where(index // 8 == k // 8, jnp.int32(value), word)
    return lax.shift_right_logical(word, 4 * (index % 8)) & 15


def start_of(seg, column):
    first = jnp.int32(0)
    for k, segment in enumerate(SEGMENTS):
        if segment[column]:
            first = first + jnp.where(seg > k, len(segment[column]), 0)
    return first


def gray(code):
    return code ^ ((code >> 1) & 21)


def turned(turn, word):
    return sum(1 << TURNS[turn][k] for k in range(6) if word >> k & 1)


def kernel(
    x_hbm, c_hbm, o_ref, x_ref, c_ref, own, other, ids, side, best, back, back_out,
    load_sem, row_send, row_recv, pair_send, pair_recv, id_send, id_recv, back_send, back_recv,
):
    core = lax.axis_index("gx")
    place = lax.axis_index("gy")
    half = x_ref.shape[0]

    loads = [
        pltpu.make_async_copy(
            x_hbm.at[pl.ds(begin, size)], x_ref.at[pl.ds(begin, size)], load_sem.at[part]
        )
        for part, (begin, size) in enumerate(PARTS)
    ]
    loads.append(pltpu.make_async_copy(c_hbm, c_ref, load_sem.at[NPART]))
    for load in loads:
        load.start()

    corner = gray(place)
    turn = packed(TURN_OF, corner)

    def chip(word):
        values = [turned(t, word) for t in range(len(TURNS))]
        there = jnp.int32(values[0])
        for value in sorted(set(values) - {values[0]}):
            hits = turn < 0
            for t, v in enumerate(values):
                if v == value:
                    hits = hits | (turn == t)
            there = jnp.where(hits, value, there)
        return gray(corner ^ there)

    step_to = [chip(1 << k) for k in range(6)]

    barrier = pltpu.get_barrier_semaphore()
    for where in step_to:
        pl.semaphore_signal(barrier, inc=1, device_id=(core, where), device_id_type=MESH)
    pl.semaphore_signal(barrier, inc=1, device_id=(1 - core, place), device_id_type=MESH)

    source = [place] + [chip(w) for w in SOURCES[1:]]

    loads[NPART].wait()
    cluster = c_ref[...].astype(jnp.float32)
    ids[0, 0] = jnp.concatenate([cluster, jnp.full((1, PAD - half), -2.0, jnp.float32)], axis=1)

    def normalize(part):
        begin, size = PARTS[part]
        loads[part].wait()
        values = x_ref[begin : begin + size, :].astype(jnp.float32)
        total = jnp.sum(values * values, axis=1, keepdims=True)
        own[0, begin : begin + size, :] = (values * lax.rsqrt(total + EPS)).astype(jnp.bfloat16)

    def id_copy(slot):
        parent, step = TREES[0][slot]
        return pltpu.make_async_remote_copy(
            src_ref=ids.at[0, parent],
            dst_ref=ids.at[0, slot],
            send_sem=id_send.at[0, slot],
            recv_sem=id_recv.at[0, slot],
            device_id=(core, step_to[step]),
            device_id_type=MESH,
        )

    def id_pair_copy(slot):
        return pltpu.make_async_remote_copy(
            src_ref=ids.at[0, slot],
            dst_ref=ids.at[1, slot],
            send_sem=id_send.at[1, slot],
            recv_sem=id_recv.at[1, slot],
            device_id=(1 - core, place),
            device_id_type=MESH,
        )

    def back_copy(slot, which, where):
        return pltpu.make_async_remote_copy(
            src_ref=back_out.at[slot, which],
            dst_ref=back.at[slot, which],
            send_sem=back_send.at[slot, which],
            recv_sem=back_recv.at[slot, which],
            device_id=(1 - core if which else core, where),
            device_id_type=MESH,
        )

    def row_copy(part, slot):
        begin, size = PARTS[part]
        parent, step = TREES[part][slot]
        return pltpu.make_async_remote_copy(
            src_ref=own.at[parent, pl.ds(begin, size)],
            dst_ref=own.at[slot, pl.ds(begin, size)],
            send_sem=row_send.at[slot, part],
            recv_sem=row_recv.at[slot, part],
            device_id=(core, step_to[step]),
            device_id_type=MESH,
        )

    def pair_copy(slot, part):
        begin, size = PARTS[part]
        return pltpu.make_async_remote_copy(
            src_ref=own.at[slot, pl.ds(begin, size)],
            dst_ref=other.at[slot, pl.ds(begin, size)],
            send_sem=pair_send.at[slot, part],
            recv_sem=pair_recv.at[slot, part],
            device_id=(1 - core, place),
            device_id_type=MESH,
        )

    normalized = 0
    for part, slot in ROOT_ORDER:
        while normalized <= part:
            normalize(normalized)
            if normalized == 0:
                pl.semaphore_wait(barrier, 7)
            normalized += 1
        row_copy(part, slot).start()
        if part == 0:
            id_copy(slot).start()
    for part in range(normalized, NPART):
        normalize(part)
    id_pair_copy(0).start()
    for part in range(NPART):
        pair_copy(0, part).start()

    best[...] = jnp.full(best.shape, -1.0, jnp.float32)
    side[...] = jnp.full(side.shape, -1.0, jnp.float32)

    def forward(slot, part):
        row_copy(part, slot).wait_recv()
        for child in CHILDREN[part].get(slot, ()):
            row_copy(part, child).start()
        if slot in PAIRED:
            pair_copy(slot, part).start()
        if part == 0:
            id_copy(slot).wait_recv()
            for child in CHILDREN[part].get(slot, ()):
                id_copy(child).start()
            if slot in PAIRED:
                id_pair_copy(slot).start()

    def leave(part, slot):
        row_copy(part, slot).start()
        if part == 0:
            id_copy(slot).start()

    def take_pair(slot):
        id_pair_copy(slot).wait_recv()
        for part in range(NPART):
            pair_copy(slot, part).wait_recv()

    def give_back(index, carry):
        slots = [packed(BACKS, BACK_GROUP * index + u) for u in range(BACK_GROUP)]
        for slot in slots:
            padded = jnp.concatenate([side[slot], jnp.full((PAD - half, 128), -1.0, jnp.float32)], axis=0)
            turned_side = jnp.max(padded.T.reshape(128 // 8, 8, PAD), axis=0)
            turned_side = jnp.max(turned_side, axis=0, keepdims=True)
            high = jnp.max(best[slot], axis=0, keepdims=True)
            back_out[slot, 0, :, :half] = jnp.maximum(high[:, :half], turned_side[:, :half])
            back_out[slot, 1, :, :half] = high[:, half:]
        for slot in slots:
            where = source[0]
            whole = slot == 0
            for k in range(1, NSLOT):
                where = jnp.where(slot == k, source[k], where)
                if k in PAIRED:
                    whole = whole | (slot == k)

            @pl.when(slot > 0)
            def _():
                back_copy(slot, 0, where).start()

            @pl.when(whole)
            def _():
                back_copy(slot, 1, where).start()

        return carry

    def products_of(p, qs, same):
        right = jnp.concatenate([part for q in qs for part in (own[q], other[q])], axis=0)
        left_id = jnp.broadcast_to(ids[0, p], (128, PAD)).T[:half]
        right_ids = [jnp.concatenate([ids[0, q, :, :half], ids[1, q, :, :half]], axis=1) for q in qs]
        row_best = side[p]
        for begin in range(0, 2 * half * len(qs), PAD):
            end = min(begin + PAD, 2 * half * len(qs))
            products = lax.dot_general(
                own[p], right[begin:end], (((1,), (1,)), ((), ())), preferred_element_type=jnp.float32
            )
            for k in range(begin, end, 128):
                u, first = k // (2 * half), k % (2 * half)
                q, lanes = qs[u], slice(first, first + 128)
                allowed = left_id == right_ids[u][:, lanes]
                if same:
                    row = lax.broadcasted_iota(jnp.int32, (half, 128), 0)
                    column = lax.broadcasted_iota(jnp.int32, (half, 128), 1) + first
                    allowed = allowed & (row != column)
                masked = jnp.where(allowed, products[:, k - begin : k - begin + 128], -1.0)
                row_best = jnp.maximum(row_best, masked)
                best[q, :, lanes] = jnp.maximum(
                    best[q, :, lanes], jnp.max(masked.reshape(half // 8, 8, 128), axis=0)
                )
        side[p] = row_best

    def multiply(index, carry):
        products_of(packed(LEFTS, index), [packed(rights, index) for rights in RIGHTS], False)
        return carry

    actions = {
        "r": leave,
        "f": forward,
        "d": take_pair,
        "s": lambda: products_of(0, [0], True),
    }

    def segment(seg, carry):
        for k, (events, _, _) in enumerate(SEGMENTS):
            if events:

                @pl.when(seg == k)
                def _():
                    for name, *where in events:
                        actions[name](*where)

        lax.fori_loop(start_of(seg, 1), start_of(seg + 1, 1), multiply, carry)
        first, end = start_of(seg, 2) // BACK_GROUP, start_of(seg + 1, 2) // BACK_GROUP
        return lax.fori_loop(first, end, give_back, carry)

    lax.fori_loop(0, NSEG, segment, 0)

    for part in range(NPART):
        for slot in range(1, NSLOT):
            row_copy(part, slot).wait_send()
        for slot in sorted(PAIRED):
            pair_copy(slot, part).wait_send()
    for slot in sorted(PAIRED):
        id_pair_copy(slot).wait_send()
    for slot in range(1, NSLOT):
        id_copy(slot).wait_send()

    returned = [(slot, 0) for slot in range(1, NSLOT)] + [(slot, 1) for slot in sorted(PAIRED)]
    result = back_out[0, 0]
    for slot, which in returned:
        back_copy(slot, which, source[slot]).wait_recv()
        result = jnp.maximum(result, back[slot, which])
    o_ref[...] = result[:, :half]

    for slot, which in returned:
        back_copy(slot, which, source[slot]).wait_send()


def local(embeddings, cluster):
    half, width = embeddings.shape
    best = pl.pallas_call(
        kernel,
        out_shape=jax.ShapeDtypeStruct((1, half), jnp.float32),
        in_specs=[pl.BlockSpec(memory_space=pl.ANY)] * 2,
        out_specs=pl.BlockSpec(memory_space=pltpu.VMEM),
        scratch_shapes=[
            pltpu.VMEM((half, width), jnp.bfloat16),
            pltpu.VMEM((1, half), jnp.int32),
            pltpu.VMEM((NSLOT, half, width), jnp.bfloat16),
            pltpu.VMEM((NSLOT, half, width), jnp.bfloat16),
            pltpu.VMEM((2, NSLOT, 1, PAD), jnp.float32),
            pltpu.VMEM((NSLOT, half, 128), jnp.float32),
            pltpu.VMEM((NSLOT, 8, 2 * half), jnp.float32),
            pltpu.VMEM((NSLOT, 2, 1, PAD), jnp.float32),
            pltpu.VMEM((NSLOT, 2, 1, PAD), jnp.float32),
            pltpu.SemaphoreType.DMA((NPART + 1,)),
            pltpu.SemaphoreType.DMA((NSLOT, NPART)),
            pltpu.SemaphoreType.DMA((NSLOT, NPART)),
            pltpu.SemaphoreType.DMA((NSLOT, NPART)),
            pltpu.SemaphoreType.DMA((NSLOT, NPART)),
            pltpu.SemaphoreType.DMA((2, NSLOT)),
            pltpu.SemaphoreType.DMA((2, NSLOT)),
            pltpu.SemaphoreType.DMA((NSLOT, 2)),
            pltpu.SemaphoreType.DMA((NSLOT, 2)),
        ],
        compiler_params=pltpu.CompilerParams(
            collective_id=0, has_side_effects=True, vmem_limit_bytes=56 * 1024 * 1024
        ),
        cost_estimate=pl.CostEstimate(
            flops=4 * GROUP * len(LEFTS) * half * half * width, bytes_accessed=2 * half * width, transcendentals=half
        ),
    )(embeddings, cluster.reshape(1, half))
    return best.reshape(half)


def solution(mesh):
    return jax.shard_map(
        local,
        mesh=mesh,
        in_specs=(P(("gx", "gy"), None), P(("gx", "gy"))),
        out_specs=P(("gx", "gy")),
        check_vma=False,
    )
```

```python
import jax
import jax.numpy as jnp
from jax import lax
from jax.experimental import pallas as pl
from jax.experimental.pallas import tpu as pltpu
from jax.sharding import PartitionSpec as P

EPS = 1e-06
TURNS = (
    (0, 1, 2, 3, 4, 5),
    (0, 1, 2, 3, 5, 4),
    (0, 1, 3, 2, 4, 5),
    (0, 1, 3, 2, 5, 4),
    (1, 0, 2, 3, 4, 5),
    (1, 0, 2, 3, 5, 4),
    (1, 0, 3, 2, 4, 5),
    (1, 0, 3, 2, 5, 4),
)
TURN_OF = [0, 4, 4, 0, 2, 6, 6, 2, 2, 6, 6, 2, 0, 4, 4, 0, 1, 5, 5, 1, 3, 7, 7, 3, 3, 7, 7, 3, 1, 5, 5, 1, 1, 5, 5, 1, 3, 7, 7, 3, 3, 7, 7, 3, 1, 5, 5, 1, 0, 4, 4, 0, 2, 6, 6, 2, 2, 6, 6, 2, 0, 4, 4, 0]
SOURCES = (0, 4, 2, 1, 32, 20, 9, 3, 11, 48, 28, 60)
PARTS = ((0, 64), (64, 64), (128, 64))
TREES = (
    {1: (0, 3), 2: (0, 0), 3: (0, 1), 4: (0, 4), 5: (1, 5), 6: (3, 2), 7: (3, 1), 8: (7, 2), 9: (4, 4), 10: (5, 3), 11: (10, 5)},
    {1: (0, 3), 2: (0, 0), 3: (0, 1), 4: (0, 4), 5: (1, 5), 6: (3, 2), 7: (2, 0), 8: (6, 1), 9: (4, 4), 10: (5, 3), 11: (10, 5)},
    {1: (0, 3), 2: (0, 0), 3: (0, 1), 4: (0, 4), 5: (1, 5), 6: (3, 2), 7: (2, 0), 8: (6, 1), 9: (4, 4), 10: (5, 3), 11: (10, 5)},
)
CHILDREN = (
    {0: (1, 3, 4, 2), 1: (5,), 3: (7, 6), 4: (9,), 5: (10,), 7: (8,), 10: (11,)},
    {0: (1, 3, 2, 4), 1: (5,), 2: (7,), 3: (6,), 4: (9,), 5: (10,), 6: (8,), 10: (11,)},
    {0: (1, 3, 2, 4), 1: (5,), 2: (7,), 3: (6,), 4: (9,), 5: (10,), 6: (8,), 10: (11,)},
)
GROUP = 2
ROOT_ORDER = ((0, 1), (0, 3), (0, 4), (1, 2), (1, 1), (1, 3), (1, 4), (2, 2), (0, 2), (2, 1), (2, 3), (2, 4))
PAIRED = frozenset((0, 1, 2, 4, 5, 6, 7, 9))
SEGMENTS = (
    (
        (('d', 0), ('s',), ('f', 1, 0), ('f', 2, 1), ('f', 3, 0), ('f', 4, 0), ('f', 1, 1), ('f', 2, 2), ('f', 3, 1), ('f', 4, 1), ('f', 5, 0), ('f', 6, 0), ('f', 1, 2), ('f', 2, 0), ('f', 3, 2), ('f', 4, 2)),
        ((1, 0, 0),),
        (),
    ),
    (
        (('f', 5, 1), ('f', 6, 1), ('d', 1)),
        ((2, 0, 1),),
        (),
    ),
    (
        (('d', 2),),
        ((3, 1, 2), (4, 0, 1)),
        (),
    ),
    (
        (('f', 7, 0), ('f', 7, 1), ('f', 9, 0), ('f', 10, 0)),
        ((4, 2, 2),),
        (),
    ),
    (
        (('f', 5, 2), ('f', 6, 2), ('d', 4)),
        ((5, 2, 4), (6, 1, 2)),
        (),
    ),
    (
        (('f', 7, 2), ('f', 8, 1), ('f', 9, 1), ('f', 10, 1), ('d', 5)),
        ((3, 4, 5),),
        (),
    ),
    (
        (('f', 8, 0), ('f', 11, 0)),
        ((6, 5, 4), (7, 4, 5)),
        (),
    ),
    (
        (('f', 8, 2), ('f', 9, 2), ('f', 10, 2)),
        ((8, 1, 4), (9, 0, 5)),
        (),
    ),
    (
        (('f', 11, 1), ('d', 9)),
        ((8, 5, 9),),
        (),
    ),
    (
        (('d', 7),),
        ((9, 7, 2), (10, 0, 4)),
        (),
    ),
    (
        (('d', 6),),
        ((10, 2, 6),),
        (),
    ),
    (
        (('f', 11, 2),),
        ((11, 2, 7), (11, 9, 6), (9, 6, 6)),
        (1, 2, 3, 4, 5, 6, 7, 8, 0, 9, 10, 11),
    ),
)

MESH = pl.DeviceIdType.MESH
NSLOT = len(SOURCES)
NPART = len(PARTS)
NSEG = len(SEGMENTS)
LEFTS = [group[0] for _, groups, _ in SEGMENTS for group in groups]
RIGHTS = [[group[1 + u] for _, groups, _ in SEGMENTS for group in groups] for u in range(GROUP)]
BACKS = [slot for _, _, slots in SEGMENTS for slot in slots]
BACK_GROUP = 4
PAD = 256


def packed(digits, index):
    word = jnp.int32(0)
    for k in range(0, len(digits), 8):
        value = sum(d << (4 * j) for j, d in enumerate(digits[k : k + 8]))
        value = value - (1 << 32) if value >> 31 else value
        word = jnp.where(index // 8 == k // 8, jnp.int32(value), word)
    return lax.shift_right_logical(word, 4 * (index % 8)) & 15


def start_of(seg, column):
    first = jnp.int32(0)
    for k, segment in enumerate(SEGMENTS):
        if segment[column]:
            first = first + jnp.where(seg > k, len(segment[column]), 0)
    return first


def gray(code):
    return code ^ ((code >> 1) & 21)


def turned(turn, word):
    return sum(1 << TURNS[turn][k] for k in range(6) if word >> k & 1)


def kernel(
    x_hbm, c_hbm, o_ref, x_ref, c_ref, own, other, ids, side, best, back, back_out,
    load_sem, row_send, row_recv, pair_send, pair_recv, id_send, id_recv, back_send, back_recv,
):
    core = lax.axis_index("gx")
    place = lax.axis_index("gy")
    half = x_ref.shape[0]

    loads = [
        pltpu.make_async_copy(
            x_hbm.at[pl.ds(begin, size)], x_ref.at[pl.ds(begin, size)], load_sem.at[part]
        )
        for part, (begin, size) in enumerate(PARTS)
    ]
    loads.append(pltpu.make_async_copy(c_hbm, c_ref, load_sem.at[NPART]))
    for load in loads:
        load.start()

    corner = gray(place)
    turn = packed(TURN_OF, corner)

    def chip(word):
        values = [turned(t, word) for t in range(len(TURNS))]
        there = jnp.int32(values[0])
        for value in sorted(set(values) - {values[0]}):
            hits = turn < 0
            for t, v in enumerate(values):
                if v == value:
                    hits = hits | (turn == t)
            there = jnp.where(hits, value, there)
        return gray(corner ^ there)

    step_to = [chip(1 << k) for k in range(6)]

    barrier = pltpu.get_barrier_semaphore()
    for where in step_to:
        pl.semaphore_signal(barrier, inc=1, device_id=(core, where), device_id_type=MESH)
    pl.semaphore_signal(barrier, inc=1, device_id=(1 - core, place), device_id_type=MESH)

    source = [place] + [chip(w) for w in SOURCES[1:]]

    loads[NPART].wait()
    cluster = c_ref[...].astype(jnp.float32)
    ids[0, 0] = jnp.concatenate([cluster, jnp.full((1, PAD - half), -2.0, jnp.float32)], axis=1)

    def normalize(part):
        begin, size = PARTS[part]
        loads[part].wait()
        values = x_ref[begin : begin + size, :].astype(jnp.float32)
        total = jnp.sum(values * values, axis=1, keepdims=True)
        own[0, begin : begin + size, :] = (values * lax.rsqrt(total + EPS)).astype(jnp.bfloat16)

    def id_copy(slot):
        parent, step = TREES[0][slot]
        return pltpu.make_async_remote_copy(
            src_ref=ids.at[0, parent],
            dst_ref=ids.at[0, slot],
            send_sem=id_send.at[0, slot],
            recv_sem=id_recv.at[0, slot],
            device_id=(core, step_to[step]),
            device_id_type=MESH,
        )

    def id_pair_copy(slot):
        return pltpu.make_async_remote_copy(
            src_ref=ids.at[0, slot],
            dst_ref=ids.at[1, slot],
            send_sem=id_send.at[1, slot],
            recv_sem=id_recv.at[1, slot],
            device_id=(1 - core, place),
            device_id_type=MESH,
        )

    def back_copy(slot, which, where):
        return pltpu.make_async_remote_copy(
            src_ref=back_out.at[slot, which],
            dst_ref=back.at[slot, which],
            send_sem=back_send.at[slot, which],
            recv_sem=back_recv.at[slot, which],
            device_id=(1 - core if which else core, where),
            device_id_type=MESH,
        )

    def row_copy(part, slot):
        begin, size = PARTS[part]
        parent, step = TREES[part][slot]
        return pltpu.make_async_remote_copy(
            src_ref=own.at[parent, pl.ds(begin, size)],
            dst_ref=own.at[slot, pl.ds(begin, size)],
            send_sem=row_send.at[slot, part],
            recv_sem=row_recv.at[slot, part],
            device_id=(core, step_to[step]),
            device_id_type=MESH,
        )

    def pair_copy(slot, part):
        begin, size = PARTS[part]
        return pltpu.make_async_remote_copy(
            src_ref=own.at[slot, pl.ds(begin, size)],
            dst_ref=other.at[slot, pl.ds(begin, size)],
            send_sem=pair_send.at[slot, part],
            recv_sem=pair_recv.at[slot, part],
            device_id=(1 - core, place),
            device_id_type=MESH,
        )

    normalized = 0
    for part, slot in ROOT_ORDER:
        while normalized <= part:
            normalize(normalized)
            if normalized == 0:
                pl.semaphore_wait(barrier, 7)
            normalized += 1
        row_copy(part, slot).start()
        if part == 0:
            id_copy(slot).start()
    for part in range(normalized, NPART):
        normalize(part)
    id_pair_copy(0).start()
    for part in range(NPART):
        pair_copy(0, part).start()

    best[...] = jnp.full(best.shape, -1.0, jnp.float32)
    side[...] = jnp.full(side.shape, -1.0, jnp.float32)

    def forward(slot, part):
        row_copy(part, slot).wait_recv()
        for child in CHILDREN[part].get(slot, ()):
            row_copy(part, child).start()
        if slot in PAIRED:
            pair_copy(slot, part).start()
        if part == 0:
            id_copy(slot).wait_recv()
            for child in CHILDREN[part].get(slot, ()):
                id_copy(child).start()
            if slot in PAIRED:
                id_pair_copy(slot).start()

    def leave(part, slot):
        row_copy(part, slot).start()
        if part == 0:
            id_copy(slot).start()

    def take_pair(slot):
        id_pair_copy(slot).wait_recv()
        for part in range(NPART):
            pair_copy(slot, part).wait_recv()

    def give_back(index, carry):
        slots = [packed(BACKS, BACK_GROUP * index + u) for u in range(BACK_GROUP)]
        for slot in slots:
            padded = jnp.concatenate([side[slot], jnp.full((PAD - half, 128), -1.0, jnp.float32)], axis=0)
            turned_side = jnp.max(padded.T.reshape(128 // 8, 8, PAD), axis=0)
            turned_side = jnp.max(turned_side, axis=0, keepdims=True)
            high = jnp.max(best[slot], axis=0, keepdims=True)
            back_out[slot, 0, :, :half] = jnp.maximum(high[:, :half], turned_side[:, :half])
            back_out[slot, 1, :, :half] = high[:, half:]
        for slot in slots:
            where = source[0]
            whole = slot == 0
            for k in range(1, NSLOT):
                where = jnp.where(slot == k, source[k], where)
                if k in PAIRED:
                    whole = whole | (slot == k)

            @pl.when(slot > 0)
            def _():
                back_copy(slot, 0, where).start()

            @pl.when(whole)
            def _():
                back_copy(slot, 1, where).start()

        return carry

    def products_of(p, qs, same):
        right = jnp.concatenate([part for q in qs for part in (own[q], other[q])], axis=0)
        left_id = jnp.broadcast_to(ids[0, p], (128, PAD)).T[:half]
        right_ids = [jnp.concatenate([ids[0, q, :, :half], ids[1, q, :, :half]], axis=1) for q in qs]
        row_best = side[p]
        for begin in range(0, 2 * half * len(qs), PAD):
            end = min(begin + PAD, 2 * half * len(qs))
            products = lax.dot_general(
                own[p], right[begin:end], (((1,), (1,)), ((), ())), preferred_element_type=jnp.float32
            )
            for k in range(begin, end, 128):
                u, first = k // (2 * half), k % (2 * half)
                q, lanes = qs[u], slice(first, first + 128)
                allowed = left_id == right_ids[u][:, lanes]
                if same:
                    row = lax.broadcasted_iota(jnp.int32, (half, 128), 0)
                    column = lax.broadcasted_iota(jnp.int32, (half, 128), 1) + first
                    allowed = allowed & (row != column)
                masked = jnp.where(allowed, products[:, k - begin : k - begin + 128], -1.0)
                row_best = jnp.maximum(row_best, masked)
                best[q, :, lanes] = jnp.maximum(
                    best[q, :, lanes], jnp.max(masked.reshape(half // 8, 8, 128), axis=0)
                )
        side[p] = row_best

    def multiply(index, carry):
        products_of(packed(LEFTS, index), [packed(rights, index) for rights in RIGHTS], False)
        return carry

    actions = {
        "r": leave,
        "f": forward,
        "d": take_pair,
        "s": lambda: products_of(0, [0], True),
    }

    def segment(seg, carry):
        for k, (events, _, _) in enumerate(SEGMENTS):
            if events:

                @pl.when(seg == k)
                def _():
                    for name, *where in events:
                        actions[name](*where)

        lax.fori_loop(start_of(seg, 1), start_of(seg + 1, 1), multiply, carry)
        first, end = start_of(seg, 2) // BACK_GROUP, start_of(seg + 1, 2) // BACK_GROUP
        return lax.fori_loop(first, end, give_back, carry)

    lax.fori_loop(0, NSEG, segment, 0)

    for part in range(NPART):
        for slot in range(1, NSLOT):
            row_copy(part, slot).wait_send()
        for slot in sorted(PAIRED):
            pair_copy(slot, part).wait_send()
    for slot in sorted(PAIRED):
        id_pair_copy(slot).wait_send()
    for slot in range(1, NSLOT):
        id_copy(slot).wait_send()

    returned = [(slot, 0) for slot in range(1, NSLOT)] + [(slot, 1) for slot in sorted(PAIRED)]
    result = back_out[0, 0]
    for slot, which in returned:
        back_copy(slot, which, source[slot]).wait_recv()
        result = jnp.maximum(result, back[slot, which])
    o_ref[...] = result[:, :half]

    for slot, which in returned:
        back_copy(slot, which, source[slot]).wait_send()


def local(embeddings, cluster):
    half, width = embeddings.shape
    best = pl.pallas_call(
        kernel,
        out_shape=jax.ShapeDtypeStruct((1, half), jnp.float32),
        in_specs=[pl.BlockSpec(memory_space=pl.ANY)] * 2,
        out_specs=pl.BlockSpec(memory_space=pltpu.VMEM),
        scratch_shapes=[
            pltpu.VMEM((half, width), jnp.bfloat16),
            pltpu.VMEM((1, half), jnp.int32),
            pltpu.VMEM((NSLOT, half, width), jnp.bfloat16),
            pltpu.VMEM((NSLOT, half, width), jnp.bfloat16),
            pltpu.VMEM((2, NSLOT, 1, PAD), jnp.float32),
            pltpu.VMEM((NSLOT, half, 128), jnp.float32),
            pltpu.VMEM((NSLOT, 8, 2 * half), jnp.float32),
            pltpu.VMEM((NSLOT, 2, 1, PAD), jnp.float32),
            pltpu.VMEM((NSLOT, 2, 1, PAD), jnp.float32),
            pltpu.SemaphoreType.DMA((NPART + 1,)),
            pltpu.SemaphoreType.DMA((NSLOT, NPART)),
            pltpu.SemaphoreType.DMA((NSLOT, NPART)),
            pltpu.SemaphoreType.DMA((NSLOT, NPART)),
            pltpu.SemaphoreType.DMA((NSLOT, NPART)),
            pltpu.SemaphoreType.DMA((2, NSLOT)),
            pltpu.SemaphoreType.DMA((2, NSLOT)),
            pltpu.SemaphoreType.DMA((NSLOT, 2)),
            pltpu.SemaphoreType.DMA((NSLOT, 2)),
        ],
        compiler_params=pltpu.CompilerParams(
            collective_id=0, has_side_effects=True, vmem_limit_bytes=56 * 1024 * 1024
        ),
        cost_estimate=pl.CostEstimate(
            flops=4 * GROUP * len(LEFTS) * half * half * width, bytes_accessed=2 * half * width, transcendentals=half
        ),
    )(embeddings, cluster.reshape(1, half))
    return jnp.maximum(best.reshape(half), -1.0)


def solution(mesh):
    return jax.shard_map(
        local,
        mesh=mesh,
        in_specs=(P(("gx", "gy"), None), P(("gx", "gy"))),
        out_specs=P(("gx", "gy")),
        check_vma=False,
    )
```

```python
import jax
import jax.numpy as jnp
from jax import lax
from jax.experimental import pallas as pl
from jax.experimental.pallas import tpu as pltpu
from jax.sharding import PartitionSpec as P

EPS = 1e-06
TURNS = (
    (0, 1, 2, 3, 4, 5),
    (0, 1, 2, 3, 5, 4),
    (0, 1, 3, 2, 4, 5),
    (0, 1, 3, 2, 5, 4),
    (1, 0, 2, 3, 4, 5),
    (1, 0, 2, 3, 5, 4),
    (1, 0, 3, 2, 4, 5),
    (1, 0, 3, 2, 5, 4),
)
TURN_OF = [0, 4, 4, 0, 2, 6, 6, 2, 2, 6, 6, 2, 0, 4, 4, 0, 1, 5, 5, 1, 3, 7, 7, 3, 3, 7, 7, 3, 1, 5, 5, 1, 1, 5, 5, 1, 3, 7, 7, 3, 3, 7, 7, 3, 1, 5, 5, 1, 0, 4, 4, 0, 2, 6, 6, 2, 2, 6, 6, 2, 0, 4, 4, 0]
SOURCES = (0, 4, 2, 1, 32, 20, 9, 3, 11, 48, 28, 60)
PARTS = ((0, 64), (64, 64), (128, 64))
TREES = (
    {1: (0, 3), 2: (0, 0), 3: (0, 1), 4: (0, 4), 5: (1, 5), 6: (3, 2), 7: (3, 1), 8: (7, 2), 9: (4, 4), 10: (5, 3), 11: (10, 5)},
    {1: (0, 3), 2: (0, 0), 3: (0, 1), 4: (0, 4), 5: (1, 5), 6: (3, 2), 7: (2, 0), 8: (6, 1), 9: (4, 4), 10: (5, 3), 11: (10, 5)},
    {1: (0, 3), 2: (0, 0), 3: (0, 1), 4: (0, 4), 5: (1, 5), 6: (3, 2), 7: (2, 0), 8: (6, 1), 9: (4, 4), 10: (5, 3), 11: (10, 5)},
)
CHILDREN = (
    {0: (1, 3, 4, 2), 1: (5,), 3: (7, 6), 4: (9,), 5: (10,), 7: (8,), 10: (11,)},
    {0: (1, 3, 2, 4), 1: (5,), 2: (7,), 3: (6,), 4: (9,), 5: (10,), 6: (8,), 10: (11,)},
    {0: (1, 3, 2, 4), 1: (5,), 2: (7,), 3: (6,), 4: (9,), 5: (10,), 6: (8,), 10: (11,)},
)
GROUP = 2
ROOT_ORDER = ((0, 1), (0, 3), (0, 4), (1, 2), (1, 1), (1, 3), (1, 4), (2, 2), (0, 2), (2, 1), (2, 3), (2, 4))
PAIRED = frozenset((0, 1, 2, 3, 4, 5, 6, 7, 9))
SEGMENTS = (
    (
        (('d', 0), ('s',), ('f', 1, 0), ('f', 2, 1), ('f', 3, 0), ('f', 4, 0), ('f', 1, 1), ('f', 2, 2), ('f', 3, 1), ('f', 4, 1), ('f', 5, 0), ('f', 6, 0), ('f', 1, 2), ('f', 2, 0), ('f', 3, 2), ('f', 4, 2)),
        ((1, 0, 0),),
        (),
    ),
    (
        (('f', 5, 1), ('f', 6, 1), ('d', 1)),
        ((2, 0, 1),),
        (),
    ),
    (
        (('d', 2),),
        ((3, 1, 2),),
        (),
    ),
    (
        (('d', 3),),
        ((4, 3, 0),),
        (),
    ),
    (
        (('f', 7, 0), ('f', 7, 1), ('f', 9, 0), ('f', 10, 0)),
        ((4, 1, 2),),
        (),
    ),
    (
        (('f', 5, 2), ('f', 6, 2), ('d', 4)),
        ((5, 3, 4), (6, 1, 4), (5, 2, 2)),
        (),
    ),
    (
        (('f', 7, 2), ('f', 8, 1), ('f', 9, 1), ('f', 10, 1), ('d', 5)),
        ((6, 2, 5), (7, 4, 5)),
        (),
    ),
    (
        (('f', 8, 0), ('f', 11, 0), ('f', 8, 2), ('f', 9, 2), ('f', 10, 2)),
        ((8, 1, 4), (9, 0, 5)),
        (),
    ),
    (
        (('f', 11, 1), ('d', 9)),
        ((8, 5, 9),),
        (),
    ),
    (
        (('d', 7),),
        ((9, 7, 2), (10, 0, 4)),
        (),
    ),
    (
        (('d', 6),),
        ((10, 2, 6), (9, 6, 6)),
        (8, 10, 5, 1),
    ),
    (
        (('f', 11, 2),),
        ((11, 2, 6), (11, 7, 9)),
        (11, 6, 7, 9, 2, 3, 4, 0),
    ),
)

MESH = pl.DeviceIdType.MESH
NSLOT = len(SOURCES)
NPART = len(PARTS)
NSEG = len(SEGMENTS)
LEFTS = [group[0] for _, groups, _ in SEGMENTS for group in groups]
RIGHTS = [[group[1 + u] for _, groups, _ in SEGMENTS for group in groups] for u in range(GROUP)]
BACKS = [slot for _, _, slots in SEGMENTS for slot in slots]
BACK_GROUP = 4
PAD = 256


def packed(digits, index):
    word = jnp.int32(0)
    for k in range(0, len(digits), 8):
        value = sum(d << (4 * j) for j, d in enumerate(digits[k : k + 8]))
        value = value - (1 << 32) if value >> 31 else value
        word = jnp.where(index // 8 == k // 8, jnp.int32(value), word)
    return lax.shift_right_logical(word, 4 * (index % 8)) & 15


def start_of(seg, column):
    first = jnp.int32(0)
    for k, segment in enumerate(SEGMENTS):
        if segment[column]:
            first = first + jnp.where(seg > k, len(segment[column]), 0)
    return first


def gray(code):
    return code ^ ((code >> 1) & 21)


def turned(turn, word):
    return sum(1 << TURNS[turn][k] for k in range(6) if word >> k & 1)


def kernel(
    x_hbm, c_hbm, o_ref, x_ref, c_ref, own, other, ids, side, best, back, back_out,
    load_sem, row_send, row_recv, pair_send, pair_recv, id_send, id_recv, back_send, back_recv,
):
    core = lax.axis_index("gx")
    place = lax.axis_index("gy")
    half = x_ref.shape[0]

    loads = [
        pltpu.make_async_copy(
            x_hbm.at[pl.ds(begin, size)], x_ref.at[pl.ds(begin, size)], load_sem.at[part]
        )
        for part, (begin, size) in enumerate(PARTS)
    ]
    loads.append(pltpu.make_async_copy(c_hbm, c_ref, load_sem.at[NPART]))
    for load in loads:
        load.start()

    corner = gray(place)
    turn = packed(TURN_OF, corner)

    def chip(word):
        values = [turned(t, word) for t in range(len(TURNS))]
        there = jnp.int32(values[0])
        for value in sorted(set(values) - {values[0]}):
            hits = turn < 0
            for t, v in enumerate(values):
                if v == value:
                    hits = hits | (turn == t)
            there = jnp.where(hits, value, there)
        return gray(corner ^ there)

    step_to = [chip(1 << k) for k in range(6)]

    barrier = pltpu.get_barrier_semaphore()
    for where in step_to:
        pl.semaphore_signal(barrier, inc=1, device_id=(core, where), device_id_type=MESH)
    pl.semaphore_signal(barrier, inc=1, device_id=(1 - core, place), device_id_type=MESH)

    source = [place] + [chip(w) for w in SOURCES[1:]]

    loads[NPART].wait()
    cluster = c_ref[...].astype(jnp.float32)
    ids[0, 0] = jnp.concatenate([cluster, jnp.full((1, PAD - half), -2.0, jnp.float32)], axis=1)

    def normalize(part):
        begin, size = PARTS[part]
        loads[part].wait()
        values = x_ref[begin : begin + size, :].astype(jnp.float32)
        total = jnp.sum(values * values, axis=1, keepdims=True)
        own[0, begin : begin + size, :] = (values * lax.rsqrt(total + EPS)).astype(jnp.bfloat16)

    def id_copy(slot):
        parent, step = TREES[0][slot]
        return pltpu.make_async_remote_copy(
            src_ref=ids.at[0, parent],
            dst_ref=ids.at[0, slot],
            send_sem=id_send.at[0, slot],
            recv_sem=id_recv.at[0, slot],
            device_id=(core, step_to[step]),
            device_id_type=MESH,
        )

    def id_pair_copy(slot):
        return pltpu.make_async_remote_copy(
            src_ref=ids.at[0, slot],
            dst_ref=ids.at[1, slot],
            send_sem=id_send.at[1, slot],
            recv_sem=id_recv.at[1, slot],
            device_id=(1 - core, place),
            device_id_type=MESH,
        )

    def back_copy(slot, which, where):
        return pltpu.make_async_remote_copy(
            src_ref=back_out.at[slot, which],
            dst_ref=back.at[slot, which],
            send_sem=back_send.at[slot, which],
            recv_sem=back_recv.at[slot, which],
            device_id=(1 - core if which else core, where),
            device_id_type=MESH,
        )

    def row_copy(part, slot):
        begin, size = PARTS[part]
        parent, step = TREES[part][slot]
        return pltpu.make_async_remote_copy(
            src_ref=own.at[parent, pl.ds(begin, size)],
            dst_ref=own.at[slot, pl.ds(begin, size)],
            send_sem=row_send.at[slot, part],
            recv_sem=row_recv.at[slot, part],
            device_id=(core, step_to[step]),
            device_id_type=MESH,
        )

    def pair_copy(slot, part):
        begin, size = PARTS[part]
        return pltpu.make_async_remote_copy(
            src_ref=own.at[slot, pl.ds(begin, size)],
            dst_ref=other.at[slot, pl.ds(begin, size)],
            send_sem=pair_send.at[slot, part],
            recv_sem=pair_recv.at[slot, part],
            device_id=(1 - core, place),
            device_id_type=MESH,
        )

    normalized = 0
    for part, slot in ROOT_ORDER:
        while normalized <= part:
            normalize(normalized)
            if normalized == 0:
                pl.semaphore_wait(barrier, 7)
            normalized += 1
        row_copy(part, slot).start()
        if part == 0:
            id_copy(slot).start()
    for part in range(normalized, NPART):
        normalize(part)
    id_pair_copy(0).start()
    for part in range(NPART):
        pair_copy(0, part).start()

    best[...] = jnp.full(best.shape, -1.0, jnp.float32)
    side[...] = jnp.full(side.shape, -1.0, jnp.float32)

    def forward(slot, part):
        row_copy(part, slot).wait_recv()
        for child in CHILDREN[part].get(slot, ()):
            row_copy(part, child).start()
        if slot in PAIRED:
            pair_copy(slot, part).start()
        if part == 0:
            id_copy(slot).wait_recv()
            for child in CHILDREN[part].get(slot, ()):
                id_copy(child).start()
            if slot in PAIRED:
                id_pair_copy(slot).start()

    def leave(part, slot):
        row_copy(part, slot).start()
        if part == 0:
            id_copy(slot).start()

    def take_pair(slot):
        id_pair_copy(slot).wait_recv()
        for part in range(NPART):
            pair_copy(slot, part).wait_recv()

    def give_back(index, carry):
        slots = [packed(BACKS, BACK_GROUP * index + u) for u in range(BACK_GROUP)]
        for slot in slots:
            padded = jnp.concatenate([side[slot], jnp.full((PAD - half, 128), -1.0, jnp.float32)], axis=0)
            turned_side = jnp.max(padded.T.reshape(128 // 8, 8, PAD), axis=0)
            turned_side = jnp.max(turned_side, axis=0, keepdims=True)
            high = jnp.max(best[slot], axis=0, keepdims=True)
            back_out[slot, 0, :, :half] = jnp.maximum(high[:, :half], turned_side[:, :half])
            back_out[slot, 1, :, :half] = high[:, half:]
        for slot in slots:
            where = source[0]
            whole = slot == 0
            for k in range(1, NSLOT):
                where = jnp.where(slot == k, source[k], where)
                if k in PAIRED:
                    whole = whole | (slot == k)

            @pl.when(slot > 0)
            def _():
                back_copy(slot, 0, where).start()

            @pl.when(whole)
            def _():
                back_copy(slot, 1, where).start()

        return carry

    def products_of(p, qs, same):
        right = jnp.concatenate([part for q in qs for part in (own[q], other[q])], axis=0)
        left_id = jnp.broadcast_to(ids[0, p], (128, PAD)).T[:half]
        right_ids = [jnp.concatenate([ids[0, q, :, :half], ids[1, q, :, :half]], axis=1) for q in qs]
        row_best = side[p]
        for begin in range(0, 2 * half * len(qs), PAD):
            end = min(begin + PAD, 2 * half * len(qs))
            products = lax.dot_general(
                own[p], right[begin:end], (((1,), (1,)), ((), ())), preferred_element_type=jnp.float32
            )
            for k in range(begin, end, 128):
                u, first = k // (2 * half), k % (2 * half)
                q, lanes = qs[u], slice(first, first + 128)
                allowed = left_id == right_ids[u][:, lanes]
                if same:
                    row = lax.broadcasted_iota(jnp.int32, (half, 128), 0)
                    column = lax.broadcasted_iota(jnp.int32, (half, 128), 1) + first
                    allowed = allowed & (row != column)
                masked = jnp.where(allowed, products[:, k - begin : k - begin + 128], -1.0)
                row_best = jnp.maximum(row_best, masked)
                best[q, :, lanes] = jnp.maximum(
                    best[q, :, lanes], jnp.max(masked.reshape(half // 8, 8, 128), axis=0)
                )
        side[p] = row_best

    def multiply(index, carry):
        products_of(packed(LEFTS, index), [packed(rights, index) for rights in RIGHTS], False)
        return carry

    actions = {
        "r": leave,
        "f": forward,
        "d": take_pair,
        "s": lambda: products_of(0, [0], True),
    }

    def segment(seg, carry):
        for k, (events, _, _) in enumerate(SEGMENTS):
            if events:

                @pl.when(seg == k)
                def _():
                    for name, *where in events:
                        actions[name](*where)

        lax.fori_loop(start_of(seg, 1), start_of(seg + 1, 1), multiply, carry)
        first, end = start_of(seg, 2) // BACK_GROUP, start_of(seg + 1, 2) // BACK_GROUP
        return lax.fori_loop(first, end, give_back, carry)

    lax.fori_loop(0, NSEG, segment, 0)

    for part in range(NPART):
        for slot in range(1, NSLOT):
            row_copy(part, slot).wait_send()
        for slot in sorted(PAIRED):
            pair_copy(slot, part).wait_send()
    for slot in sorted(PAIRED):
        id_pair_copy(slot).wait_send()
    for slot in range(1, NSLOT):
        id_copy(slot).wait_send()

    returned = [(slot, 0) for slot in range(1, NSLOT)] + [(slot, 1) for slot in sorted(PAIRED)]
    result = back_out[0, 0]
    for slot, which in returned:
        back_copy(slot, which, source[slot]).wait_recv()
        result = jnp.maximum(result, back[slot, which])
    o_ref[...] = result[:, :half]

    for slot, which in returned:
        back_copy(slot, which, source[slot]).wait_send()


def local(embeddings, cluster):
    half, width = embeddings.shape
    best = pl.pallas_call(
        kernel,
        out_shape=jax.ShapeDtypeStruct((1, half), jnp.float32),
        in_specs=[pl.BlockSpec(memory_space=pl.ANY)] * 2,
        out_specs=pl.BlockSpec(memory_space=pltpu.VMEM),
        scratch_shapes=[
            pltpu.VMEM((half, width), jnp.bfloat16),
            pltpu.VMEM((1, half), jnp.int32),
            pltpu.VMEM((NSLOT, half, width), jnp.bfloat16),
            pltpu.VMEM((NSLOT, half, width), jnp.bfloat16),
            pltpu.VMEM((2, NSLOT, 1, PAD), jnp.float32),
            pltpu.VMEM((NSLOT, half, 128), jnp.float32),
            pltpu.VMEM((NSLOT, 8, 2 * half), jnp.float32),
            pltpu.VMEM((NSLOT, 2, 1, PAD), jnp.float32),
            pltpu.VMEM((NSLOT, 2, 1, PAD), jnp.float32),
            pltpu.SemaphoreType.DMA((NPART + 1,)),
            pltpu.SemaphoreType.DMA((NSLOT, NPART)),
            pltpu.SemaphoreType.DMA((NSLOT, NPART)),
            pltpu.SemaphoreType.DMA((NSLOT, NPART)),
            pltpu.SemaphoreType.DMA((NSLOT, NPART)),
            pltpu.SemaphoreType.DMA((2, NSLOT)),
            pltpu.SemaphoreType.DMA((2, NSLOT)),
            pltpu.SemaphoreType.DMA((NSLOT, 2)),
            pltpu.SemaphoreType.DMA((NSLOT, 2)),
        ],
        compiler_params=pltpu.CompilerParams(
            collective_id=0, has_side_effects=True, vmem_limit_bytes=56 * 1024 * 1024
        ),
        cost_estimate=pl.CostEstimate(
            flops=4 * GROUP * len(LEFTS) * half * half * width, bytes_accessed=2 * half * width, transcendentals=half
        ),
    )(embeddings, cluster.reshape(1, half))
    return jnp.maximum(best.reshape(half), -1.0)


def solution(mesh):
    return jax.shard_map(
        local,
        mesh=mesh,
        in_specs=(P(("gx", "gy"), None), P(("gx", "gy"))),
        out_specs=P(("gx", "gy")),
        check_vma=False,
    )
```

```python
import jax
import jax.numpy as jnp
from jax import lax
from jax.experimental import pallas as pl
from jax.experimental.pallas import tpu as pltpu
from jax.sharding import PartitionSpec as P

EPS = 1e-06
TURNS = (
    (0, 1, 2, 3, 4, 5),
    (0, 1, 2, 3, 5, 4),
    (0, 1, 3, 2, 4, 5),
    (0, 1, 3, 2, 5, 4),
    (1, 0, 2, 3, 4, 5),
    (1, 0, 2, 3, 5, 4),
    (1, 0, 3, 2, 4, 5),
    (1, 0, 3, 2, 5, 4),
)
TURN_OF = [0, 4, 4, 0, 2, 6, 6, 2, 2, 6, 6, 2, 0, 4, 4, 0, 1, 5, 5, 1, 3, 7, 7, 3, 3, 7, 7, 3, 1, 5, 5, 1, 1, 5, 5, 1, 3, 7, 7, 3, 3, 7, 7, 3, 1, 5, 5, 1, 0, 4, 4, 0, 2, 6, 6, 2, 2, 6, 6, 2, 0, 4, 4, 0]
SOURCES = (0, 4, 2, 1, 32, 20, 9, 3, 11, 48, 28, 60)
PARTS = ((0, 64), (64, 64), (128, 64))
TREES = (
    {1: (0, 3), 2: (0, 0), 3: (0, 1), 4: (0, 4), 5: (1, 5), 6: (3, 2), 7: (3, 1), 8: (7, 2), 9: (4, 4), 10: (5, 3), 11: (10, 5)},
    {1: (0, 3), 2: (0, 0), 3: (0, 1), 4: (0, 4), 5: (1, 5), 6: (3, 2), 7: (2, 0), 8: (6, 1), 9: (4, 4), 10: (5, 3), 11: (10, 5)},
    {1: (0, 3), 2: (0, 0), 3: (0, 1), 4: (0, 4), 5: (1, 5), 6: (3, 2), 7: (2, 0), 8: (6, 1), 9: (4, 4), 10: (5, 3), 11: (10, 5)},
)
CHILDREN = (
    {0: (1, 3, 4, 2), 1: (5,), 3: (7, 6), 4: (9,), 5: (10,), 7: (8,), 10: (11,)},
    {0: (1, 3, 2, 4), 1: (5,), 2: (7,), 3: (6,), 4: (9,), 5: (10,), 6: (8,), 10: (11,)},
    {0: (1, 3, 2, 4), 1: (5,), 2: (7,), 3: (6,), 4: (9,), 5: (10,), 6: (8,), 10: (11,)},
)
GROUP = 2
ROOT_ORDER = ((0, 1), (0, 3), (0, 4), (1, 2), (1, 1), (1, 3), (1, 4), (2, 2), (0, 2), (2, 1), (2, 3), (2, 4))
PAIRED = frozenset((0, 1, 2, 3, 4, 5, 6, 7, 9))
SEGMENTS = (
    (
        (('d', 0), ('s',), ('f', 1, 0), ('f', 2, 1), ('f', 3, 0), ('f', 4, 0), ('f', 1, 1), ('f', 2, 2), ('f', 3, 1), ('f', 4, 1), ('f', 5, 0), ('f', 6, 0), ('f', 1, 2), ('f', 2, 0), ('f', 3, 2), ('f', 4, 2)),
        ((1, 0, 0),),
        (),
    ),
    (
        (('f', 5, 1), ('f', 6, 1), ('d', 1)),
        ((2, 0, 1),),
        (),
    ),
    (
        (('d', 2),),
        ((3, 1, 2),),
        (),
    ),
    (
        (('d', 3),),
        ((4, 3, 0),),
        (),
    ),
    (
        (('f', 7, 0), ('f', 7, 1), ('f', 9, 0), ('f', 10, 0)),
        ((4, 1, 2),),
        (),
    ),
    (
        (('f', 5, 2), ('f', 6, 2), ('d', 4)),
        ((5, 3, 4), (6, 1, 4), (5, 2, 2)),
        (),
    ),
    (
        (('f', 7, 2), ('f', 8, 1), ('f', 9, 1), ('f', 10, 1), ('d', 5)),
        ((6, 2, 5), (7, 4, 5)),
        (),
    ),
    (
        (('f', 8, 0), ('f', 11, 0), ('f', 8, 2), ('f', 9, 2), ('f', 10, 2)),
        ((8, 1, 4), (9, 0, 5)),
        (),
    ),
    (
        (('f', 11, 1), ('d', 9)),
        ((8, 5, 9),),
        (),
    ),
    (
        (('d', 7),),
        ((9, 7, 2), (10, 0, 4)),
        (),
    ),
    (
        (('d', 6),),
        ((10, 2, 6), (9, 6, 6)),
        (8, 10, 5, 1),
    ),
    (
        (('f', 11, 2),),
        ((11, 2, 6), (11, 7, 9)),
        (11, 6, 7, 9, 2, 3, 4, 0),
    ),
)

MESH = pl.DeviceIdType.MESH
NSLOT = len(SOURCES)
NPART = len(PARTS)
NSEG = len(SEGMENTS)
LEFTS = [group[0] for _, groups, _ in SEGMENTS for group in groups]
RIGHTS = [[group[1 + u] for _, groups, _ in SEGMENTS for group in groups] for u in range(GROUP)]
BACKS = [slot for _, _, slots in SEGMENTS for slot in slots]
BACK_GROUP = 2
PAD = 256


def packed(digits, index):
    word = jnp.int32(0)
    for k in range(0, len(digits), 8):
        value = sum(d << (4 * j) for j, d in enumerate(digits[k : k + 8]))
        value = value - (1 << 32) if value >> 31 else value
        word = jnp.where(index // 8 == k // 8, jnp.int32(value), word)
    return lax.shift_right_logical(word, 4 * (index % 8)) & 15


def start_of(seg, column):
    first = jnp.int32(0)
    for k, segment in enumerate(SEGMENTS):
        if segment[column]:
            first = first + jnp.where(seg > k, len(segment[column]), 0)
    return first


def gray(code):
    return code ^ ((code >> 1) & 21)


def turned(turn, word):
    return sum(1 << TURNS[turn][k] for k in range(6) if word >> k & 1)


def kernel(
    x_hbm, c_hbm, o_ref, x_ref, c_ref, own, other, ids, side, best, back, back_out,
    load_sem, row_send, row_recv, pair_send, pair_recv, id_send, id_recv, back_send, back_recv,
):
    core = lax.axis_index("gx")
    place = lax.axis_index("gy")
    half = x_ref.shape[0]

    loads = [
        pltpu.make_async_copy(
            x_hbm.at[pl.ds(begin, size)], x_ref.at[pl.ds(begin, size)], load_sem.at[part]
        )
        for part, (begin, size) in enumerate(PARTS)
    ]
    loads.append(pltpu.make_async_copy(c_hbm, c_ref, load_sem.at[NPART]))
    for load in loads:
        load.start()

    corner = gray(place)
    turn = packed(TURN_OF, corner)

    def chip(word):
        values = [turned(t, word) for t in range(len(TURNS))]
        there = jnp.int32(values[0])
        for value in sorted(set(values) - {values[0]}):
            hits = turn < 0
            for t, v in enumerate(values):
                if v == value:
                    hits = hits | (turn == t)
            there = jnp.where(hits, value, there)
        return gray(corner ^ there)

    step_to = [chip(1 << k) for k in range(6)]

    barrier = pltpu.get_barrier_semaphore()
    for where in step_to:
        pl.semaphore_signal(barrier, inc=1, device_id=(core, where), device_id_type=MESH)
    pl.semaphore_signal(barrier, inc=1, device_id=(1 - core, place), device_id_type=MESH)

    source = [place] + [chip(w) for w in SOURCES[1:]]

    loads[NPART].wait()
    cluster = c_ref[...].astype(jnp.float32)
    ids[0, 0] = jnp.concatenate([cluster, jnp.full((1, PAD - half), -2.0, jnp.float32)], axis=1)

    def normalize(part):
        begin, size = PARTS[part]
        loads[part].wait()
        values = x_ref[begin : begin + size, :].astype(jnp.float32)
        total = jnp.sum(values * values, axis=1, keepdims=True)
        own[0, begin : begin + size, :] = (values * lax.rsqrt(total + EPS)).astype(jnp.bfloat16)

    def id_copy(slot):
        parent, step = TREES[0][slot]
        return pltpu.make_async_remote_copy(
            src_ref=ids.at[0, parent],
            dst_ref=ids.at[0, slot],
            send_sem=id_send.at[0, slot],
            recv_sem=id_recv.at[0, slot],
            device_id=(core, step_to[step]),
            device_id_type=MESH,
        )

    def id_pair_copy(slot):
        return pltpu.make_async_remote_copy(
            src_ref=ids.at[0, slot],
            dst_ref=ids.at[1, slot],
            send_sem=id_send.at[1, slot],
            recv_sem=id_recv.at[1, slot],
            device_id=(1 - core, place),
            device_id_type=MESH,
        )

    def back_copy(slot, which, where):
        return pltpu.make_async_remote_copy(
            src_ref=back_out.at[slot, which],
            dst_ref=back.at[slot, which],
            send_sem=back_send.at[slot, which],
            recv_sem=back_recv.at[slot, which],
            device_id=(1 - core if which else core, where),
            device_id_type=MESH,
        )

    def row_copy(part, slot):
        begin, size = PARTS[part]
        parent, step = TREES[part][slot]
        return pltpu.make_async_remote_copy(
            src_ref=own.at[parent, pl.ds(begin, size)],
            dst_ref=own.at[slot, pl.ds(begin, size)],
            send_sem=row_send.at[slot, part],
            recv_sem=row_recv.at[slot, part],
            device_id=(core, step_to[step]),
            device_id_type=MESH,
        )

    def pair_copy(slot, part):
        begin, size = PARTS[part]
        return pltpu.make_async_remote_copy(
            src_ref=own.at[slot, pl.ds(begin, size)],
            dst_ref=other.at[slot, pl.ds(begin, size)],
            send_sem=pair_send.at[slot, part],
            recv_sem=pair_recv.at[slot, part],
            device_id=(1 - core, place),
            device_id_type=MESH,
        )

    normalized = 0
    for part, slot in ROOT_ORDER:
        while normalized <= part:
            normalize(normalized)
            if normalized == 0:
                pl.semaphore_wait(barrier, 7)
            normalized += 1
        row_copy(part, slot).start()
        if part == 0:
            id_copy(slot).start()
    for part in range(normalized, NPART):
        normalize(part)
    id_pair_copy(0).start()
    for part in range(NPART):
        pair_copy(0, part).start()

    best[...] = jnp.full(best.shape, -1.0, jnp.float32)
    side[...] = jnp.full(side.shape, -1.0, jnp.float32)

    def forward(slot, part):
        row_copy(part, slot).wait_recv()
        for child in CHILDREN[part].get(slot, ()):
            row_copy(part, child).start()
        if slot in PAIRED:
            pair_copy(slot, part).start()
        if part == 0:
            id_copy(slot).wait_recv()
            for child in CHILDREN[part].get(slot, ()):
                id_copy(child).start()
            if slot in PAIRED:
                id_pair_copy(slot).start()

    def leave(part, slot):
        row_copy(part, slot).start()
        if part == 0:
            id_copy(slot).start()

    def take_pair(slot):
        id_pair_copy(slot).wait_recv()
        for part in range(NPART):
            pair_copy(slot, part).wait_recv()

    def give_back(index, carry):
        slots = [packed(BACKS, BACK_GROUP * index + u) for u in range(BACK_GROUP)]
        for slot in slots:
            padded = jnp.concatenate([side[slot], jnp.full((PAD - half, 128), -1.0, jnp.float32)], axis=0)
            turned_side = jnp.max(padded.T.reshape(128 // 8, 8, PAD), axis=0)
            turned_side = jnp.max(turned_side, axis=0, keepdims=True)
            high = jnp.max(best[slot], axis=0, keepdims=True)
            back_out[slot, 0, :, :half] = jnp.maximum(high[:, :half], turned_side[:, :half])
            back_out[slot, 1, :, :half] = high[:, half:]
        for slot in slots:
            where = source[0]
            whole = slot == 0
            for k in range(1, NSLOT):
                where = jnp.where(slot == k, source[k], where)
                if k in PAIRED:
                    whole = whole | (slot == k)

            @pl.when(slot > 0)
            def _():
                back_copy(slot, 0, where).start()

            @pl.when(whole)
            def _():
                back_copy(slot, 1, where).start()

        return carry

    def products_of(p, qs, same):
        right = jnp.concatenate([part for q in qs for part in (own[q], other[q])], axis=0)
        left_id = jnp.broadcast_to(ids[0, p], (128, PAD)).T[:half]
        right_ids = [jnp.concatenate([ids[0, q, :, :half], ids[1, q, :, :half]], axis=1) for q in qs]
        row_best = side[p]
        for begin in range(0, 2 * half * len(qs), PAD):
            end = min(begin + PAD, 2 * half * len(qs))
            products = lax.dot_general(
                own[p], right[begin:end], (((1,), (1,)), ((), ())), preferred_element_type=jnp.float32
            )
            for k in range(begin, end, 128):
                u, first = k // (2 * half), k % (2 * half)
                q, lanes = qs[u], slice(first, first + 128)
                allowed = left_id == right_ids[u][:, lanes]
                if same:
                    row = lax.broadcasted_iota(jnp.int32, (half, 128), 0)
                    column = lax.broadcasted_iota(jnp.int32, (half, 128), 1) + first
                    allowed = allowed & (row != column)
                masked = jnp.where(allowed, products[:, k - begin : k - begin + 128], -1.0)
                row_best = jnp.maximum(row_best, masked)
                best[q, :, lanes] = jnp.maximum(
                    best[q, :, lanes], jnp.max(masked.reshape(half // 8, 8, 128), axis=0)
                )
        side[p] = row_best

    def multiply(index, carry):
        products_of(packed(LEFTS, index), [packed(rights, index) for rights in RIGHTS], False)
        return carry

    actions = {
        "r": leave,
        "f": forward,
        "d": take_pair,
        "s": lambda: products_of(0, [0], True),
    }

    def segment(seg, carry):
        for k, (events, _, _) in enumerate(SEGMENTS):
            if events:

                @pl.when(seg == k)
                def _():
                    for name, *where in events:
                        actions[name](*where)

        lax.fori_loop(start_of(seg, 1), start_of(seg + 1, 1), multiply, carry)
        first, end = start_of(seg, 2) // BACK_GROUP, start_of(seg + 1, 2) // BACK_GROUP
        return lax.fori_loop(first, end, give_back, carry)

    lax.fori_loop(0, NSEG, segment, 0)

    for part in range(NPART):
        for slot in range(1, NSLOT):
            row_copy(part, slot).wait_send()
        for slot in sorted(PAIRED):
            pair_copy(slot, part).wait_send()
    for slot in sorted(PAIRED):
        id_pair_copy(slot).wait_send()
    for slot in range(1, NSLOT):
        id_copy(slot).wait_send()

    returned = [(slot, 0) for slot in range(1, NSLOT)] + [(slot, 1) for slot in sorted(PAIRED)]
    result = back_out[0, 0]
    for slot, which in returned:
        back_copy(slot, which, source[slot]).wait_recv()
        result = jnp.maximum(result, back[slot, which])
    o_ref[...] = result[:, :half]

    for slot, which in returned:
        back_copy(slot, which, source[slot]).wait_send()


def local(embeddings, cluster):
    half, width = embeddings.shape
    best = pl.pallas_call(
        kernel,
        out_shape=jax.ShapeDtypeStruct((1, half), jnp.float32),
        in_specs=[pl.BlockSpec(memory_space=pl.ANY)] * 2,
        out_specs=pl.BlockSpec(memory_space=pltpu.VMEM),
        scratch_shapes=[
            pltpu.VMEM((half, width), jnp.bfloat16),
            pltpu.VMEM((1, half), jnp.int32),
            pltpu.VMEM((NSLOT, half, width), jnp.bfloat16),
            pltpu.VMEM((NSLOT, half, width), jnp.bfloat16),
            pltpu.VMEM((2, NSLOT, 1, PAD), jnp.float32),
            pltpu.VMEM((NSLOT, half, 128), jnp.float32),
            pltpu.VMEM((NSLOT, 8, 2 * half), jnp.float32),
            pltpu.VMEM((NSLOT, 2, 1, PAD), jnp.float32),
            pltpu.VMEM((NSLOT, 2, 1, PAD), jnp.float32),
            pltpu.SemaphoreType.DMA((NPART + 1,)),
            pltpu.SemaphoreType.DMA((NSLOT, NPART)),
            pltpu.SemaphoreType.DMA((NSLOT, NPART)),
            pltpu.SemaphoreType.DMA((NSLOT, NPART)),
            pltpu.SemaphoreType.DMA((NSLOT, NPART)),
            pltpu.SemaphoreType.DMA((2, NSLOT)),
            pltpu.SemaphoreType.DMA((2, NSLOT)),
            pltpu.SemaphoreType.DMA((NSLOT, 2)),
            pltpu.SemaphoreType.DMA((NSLOT, 2)),
        ],
        compiler_params=pltpu.CompilerParams(
            collective_id=0, has_side_effects=True, vmem_limit_bytes=56 * 1024 * 1024
        ),
        cost_estimate=pl.CostEstimate(
            flops=4 * GROUP * len(LEFTS) * half * half * width, bytes_accessed=2 * half * width, transcendentals=half
        ),
    )(embeddings, cluster.reshape(1, half))
    return jnp.maximum(best.reshape(half), -1.0)


def solution(mesh):
    return jax.shard_map(
        local,
        mesh=mesh,
        in_specs=(P(("gx", "gy"), None), P(("gx", "gy"))),
        out_specs=P(("gx", "gy")),
        check_vma=False,
    )
```

```python
import jax
import jax.numpy as jnp
from jax import lax
from jax.experimental import pallas as pl
from jax.experimental.pallas import tpu as pltpu
from jax.sharding import PartitionSpec as P

EPS = 1e-06
TURNS = (
    (0, 1, 2, 3, 4, 5),
    (0, 1, 2, 3, 5, 4),
    (0, 1, 3, 2, 4, 5),
    (0, 1, 3, 2, 5, 4),
    (1, 0, 2, 3, 4, 5),
    (1, 0, 2, 3, 5, 4),
    (1, 0, 3, 2, 4, 5),
    (1, 0, 3, 2, 5, 4),
)
TURN_OF = [0, 4, 4, 0, 2, 6, 6, 2, 2, 6, 6, 2, 0, 4, 4, 0, 1, 5, 5, 1, 3, 7, 7, 3, 3, 7, 7, 3, 1, 5, 5, 1, 1, 5, 5, 1, 3, 7, 7, 3, 3, 7, 7, 3, 1, 5, 5, 1, 0, 4, 4, 0, 2, 6, 6, 2, 2, 6, 6, 2, 0, 4, 4, 0]
SOURCES = (0, 4, 2, 1, 32, 20, 9, 3, 11, 48, 28, 60)
PARTS = ((0, 64), (64, 64), (128, 64))
TREES = (
    {1: (0, 3), 2: (0, 0), 3: (0, 1), 4: (0, 4), 5: (1, 5), 6: (3, 2), 7: (3, 1), 8: (7, 2), 9: (4, 4), 10: (5, 3), 11: (10, 5)},
    {1: (0, 3), 2: (0, 0), 3: (0, 1), 4: (0, 4), 5: (1, 5), 6: (3, 2), 7: (2, 0), 8: (6, 1), 9: (4, 4), 10: (5, 3), 11: (10, 5)},
    {1: (0, 3), 2: (0, 0), 3: (0, 1), 4: (0, 4), 5: (1, 5), 6: (3, 2), 7: (2, 0), 8: (6, 1), 9: (4, 4), 10: (5, 3), 11: (10, 5)},
)
CHILDREN = (
    {0: (1, 3, 4, 2), 1: (5,), 3: (7, 6), 4: (9,), 5: (10,), 7: (8,), 10: (11,)},
    {0: (1, 3, 2, 4), 1: (5,), 2: (7,), 3: (6,), 4: (9,), 5: (10,), 6: (8,), 10: (11,)},
    {0: (1, 3, 2, 4), 1: (5,), 2: (7,), 3: (6,), 4: (9,), 5: (10,), 6: (8,), 10: (11,)},
)
GROUP = 2
ROOT_ORDER = ((0, 1), (0, 3), (0, 4), (1, 2), (1, 1), (1, 3), (1, 4), (2, 2), (0, 2), (2, 1), (2, 3), (2, 4))
PAIRED = frozenset((0, 1, 2, 3, 4, 5, 6, 7, 9))
SEGMENTS = (
    (
        (('d', 0), ('s',), ('f', 1, 0), ('f', 2, 1), ('f', 3, 0), ('f', 4, 0), ('f', 1, 1), ('f', 2, 2), ('f', 3, 1), ('f', 4, 1), ('f', 5, 0), ('f', 6, 0), ('f', 1, 2), ('f', 2, 0), ('f', 3, 2), ('f', 4, 2)),
        ((1, 0, 0),),
        (),
    ),
    (
        (('f', 5, 1), ('f', 6, 1), ('d', 1)),
        ((2, 0, 1),),
        (),
    ),
    (
        (('d', 2),),
        ((3, 1, 2),),
        (),
    ),
    (
        (('d', 3),),
        ((4, 3, 0),),
        (),
    ),
    (
        (('f', 7, 0), ('f', 7, 1), ('f', 9, 0), ('f', 10, 0)),
        ((4, 1, 2),),
        (),
    ),
    (
        (('f', 5, 2), ('f', 6, 2), ('d', 4)),
        ((5, 3, 4), (6, 1, 4), (5, 2, 2)),
        (),
    ),
    (
        (('f', 7, 2), ('f', 8, 1), ('f', 9, 1), ('f', 10, 1), ('d', 5)),
        ((6, 2, 5), (7, 4, 5)),
        (),
    ),
    (
        (('f', 8, 0), ('f', 11, 0), ('f', 8, 2), ('f', 9, 2), ('f', 10, 2)),
        ((8, 1, 4), (9, 0, 5)),
        (),
    ),
    (
        (('f', 11, 1), ('d', 9)),
        ((8, 5, 9),),
        (),
    ),
    (
        (('d', 7),),
        ((9, 7, 2), (10, 0, 4)),
        (),
    ),
    (
        (('d', 6),),
        ((10, 2, 6), (9, 6, 6)),
        (8, 10, 5, 1),
    ),
    (
        (('f', 11, 2),),
        ((11, 2, 6), (11, 7, 9)),
        (11, 6, 7, 9, 2, 3, 4, 0),
    ),
)

MESH = pl.DeviceIdType.MESH
NSLOT = len(SOURCES)
NPART = len(PARTS)
NSEG = len(SEGMENTS)
LEFTS = [group[0] for _, groups, _ in SEGMENTS for group in groups]
RIGHTS = [[group[1 + u] for _, groups, _ in SEGMENTS for group in groups] for u in range(GROUP)]
BACKS = [slot for _, _, slots in SEGMENTS for slot in slots]
BACK_GROUP = 1
PAD = 256


def packed(digits, index):
    word = jnp.int32(0)
    for k in range(0, len(digits), 8):
        value = sum(d << (4 * j) for j, d in enumerate(digits[k : k + 8]))
        value = value - (1 << 32) if value >> 31 else value
        word = jnp.where(index // 8 == k // 8, jnp.int32(value), word)
    return lax.shift_right_logical(word, 4 * (index % 8)) & 15


def start_of(seg, column):
    first = jnp.int32(0)
    for k, segment in enumerate(SEGMENTS):
        if segment[column]:
            first = first + jnp.where(seg > k, len(segment[column]), 0)
    return first


def gray(code):
    return code ^ ((code >> 1) & 21)


def turned(turn, word):
    return sum(1 << TURNS[turn][k] for k in range(6) if word >> k & 1)


def kernel(
    x_hbm, c_hbm, o_ref, x_ref, c_ref, own, other, ids, side, best, back, back_out,
    load_sem, row_send, row_recv, pair_send, pair_recv, id_send, id_recv, back_send, back_recv,
):
    core = lax.axis_index("gx")
    place = lax.axis_index("gy")
    half = x_ref.shape[0]

    loads = [
        pltpu.make_async_copy(
            x_hbm.at[pl.ds(begin, size)], x_ref.at[pl.ds(begin, size)], load_sem.at[part]
        )
        for part, (begin, size) in enumerate(PARTS)
    ]
    loads.append(pltpu.make_async_copy(c_hbm, c_ref, load_sem.at[NPART]))
    for load in loads:
        load.start()

    corner = gray(place)
    turn = packed(TURN_OF, corner)

    def chip(word):
        values = [turned(t, word) for t in range(len(TURNS))]
        there = jnp.int32(values[0])
        for value in sorted(set(values) - {values[0]}):
            hits = turn < 0
            for t, v in enumerate(values):
                if v == value:
                    hits = hits | (turn == t)
            there = jnp.where(hits, value, there)
        return gray(corner ^ there)

    step_to = [chip(1 << k) for k in range(6)]

    barrier = pltpu.get_barrier_semaphore()
    for where in step_to:
        pl.semaphore_signal(barrier, inc=1, device_id=(core, where), device_id_type=MESH)
    pl.semaphore_signal(barrier, inc=1, device_id=(1 - core, place), device_id_type=MESH)

    source = [place] + [chip(w) for w in SOURCES[1:]]

    loads[NPART].wait()
    cluster = c_ref[...].astype(jnp.float32)
    ids[0, 0] = jnp.concatenate([cluster, jnp.full((1, PAD - half), -2.0, jnp.float32)], axis=1)

    def normalize(part):
        begin, size = PARTS[part]
        loads[part].wait()
        values = x_ref[begin : begin + size, :].astype(jnp.float32)
        total = jnp.sum(values * values, axis=1, keepdims=True)
        own[0, begin : begin + size, :] = (values * lax.rsqrt(total + EPS)).astype(jnp.bfloat16)

    def id_copy(slot):
        parent, step = TREES[0][slot]
        return pltpu.make_async_remote_copy(
            src_ref=ids.at[0, parent],
            dst_ref=ids.at[0, slot],
            send_sem=id_send.at[0, slot],
            recv_sem=id_recv.at[0, slot],
            device_id=(core, step_to[step]),
            device_id_type=MESH,
        )

    def id_pair_copy(slot):
        return pltpu.make_async_remote_copy(
            src_ref=ids.at[0, slot],
            dst_ref=ids.at[1, slot],
            send_sem=id_send.at[1, slot],
            recv_sem=id_recv.at[1, slot],
            device_id=(1 - core, place),
            device_id_type=MESH,
        )

    def back_copy(slot, which, where):
        return pltpu.make_async_remote_copy(
            src_ref=back_out.at[slot, which],
            dst_ref=back.at[slot, which],
            send_sem=back_send.at[slot, which],
            recv_sem=back_recv.at[slot, which],
            device_id=(1 - core if which else core, where),
            device_id_type=MESH,
        )

    def row_copy(part, slot):
        begin, size = PARTS[part]
        parent, step = TREES[part][slot]
        return pltpu.make_async_remote_copy(
            src_ref=own.at[parent, pl.ds(begin, size)],
            dst_ref=own.at[slot, pl.ds(begin, size)],
            send_sem=row_send.at[slot, part],
            recv_sem=row_recv.at[slot, part],
            device_id=(core, step_to[step]),
            device_id_type=MESH,
        )

    def pair_copy(slot, part):
        begin, size = PARTS[part]
        return pltpu.make_async_remote_copy(
            src_ref=own.at[slot, pl.ds(begin, size)],
            dst_ref=other.at[slot, pl.ds(begin, size)],
            send_sem=pair_send.at[slot, part],
            recv_sem=pair_recv.at[slot, part],
            device_id=(1 - core, place),
            device_id_type=MESH,
        )

    normalized = 0
    for part, slot in ROOT_ORDER:
        while normalized <= part:
            normalize(normalized)
            if normalized == 0:
                pl.semaphore_wait(barrier, 7)
            normalized += 1
        row_copy(part, slot).start()
        if part == 0:
            id_copy(slot).start()
    for part in range(normalized, NPART):
        normalize(part)
    id_pair_copy(0).start()
    for part in range(NPART):
        pair_copy(0, part).start()

    best[...] = jnp.full(best.shape, -1.0, jnp.float32)
    side[...] = jnp.full(side.shape, -1.0, jnp.float32)

    def forward(slot, part):
        row_copy(part, slot).wait_recv()
        for child in CHILDREN[part].get(slot, ()):
            row_copy(part, child).start()
        if slot in PAIRED:
            pair_copy(slot, part).start()
        if part == 0:
            id_copy(slot).wait_recv()
            for child in CHILDREN[part].get(slot, ()):
                id_copy(child).start()
            if slot in PAIRED:
                id_pair_copy(slot).start()

    def leave(part, slot):
        row_copy(part, slot).start()
        if part == 0:
            id_copy(slot).start()

    def take_pair(slot):
        id_pair_copy(slot).wait_recv()
        for part in range(NPART):
            pair_copy(slot, part).wait_recv()

    def give_back(index, carry):
        slots = [packed(BACKS, BACK_GROUP * index + u) for u in range(BACK_GROUP)]
        for slot in slots:
            padded = jnp.concatenate([side[slot], jnp.full((PAD - half, 128), -1.0, jnp.float32)], axis=0)
            turned_side = jnp.max(padded.T.reshape(128 // 8, 8, PAD), axis=0)
            turned_side = jnp.max(turned_side, axis=0, keepdims=True)
            high = jnp.max(best[slot], axis=0, keepdims=True)
            back_out[slot, 0, :, :half] = jnp.maximum(high[:, :half], turned_side[:, :half])
            back_out[slot, 1, :, :half] = high[:, half:]
        for slot in slots:
            where = source[0]
            whole = slot == 0
            for k in range(1, NSLOT):
                where = jnp.where(slot == k, source[k], where)
                if k in PAIRED:
                    whole = whole | (slot == k)

            @pl.when(slot > 0)
            def _():
                back_copy(slot, 0, where).start()

            @pl.when(whole)
            def _():
                back_copy(slot, 1, where).start()

        return carry

    def products_of(p, qs, same):
        right = jnp.concatenate([part for q in qs for part in (own[q], other[q])], axis=0)
        left_id = jnp.broadcast_to(ids[0, p], (128, PAD)).T[:half]
        right_ids = [jnp.concatenate([ids[0, q, :, :half], ids[1, q, :, :half]], axis=1) for q in qs]
        row_best = side[p]
        for begin in range(0, 2 * half * len(qs), PAD):
            end = min(begin + PAD, 2 * half * len(qs))
            products = lax.dot_general(
                own[p], right[begin:end], (((1,), (1,)), ((), ())), preferred_element_type=jnp.float32
            )
            for k in range(begin, end, 128):
                u, first = k // (2 * half), k % (2 * half)
                q, lanes = qs[u], slice(first, first + 128)
                allowed = left_id == right_ids[u][:, lanes]
                if same:
                    row = lax.broadcasted_iota(jnp.int32, (half, 128), 0)
                    column = lax.broadcasted_iota(jnp.int32, (half, 128), 1) + first
                    allowed = allowed & (row != column)
                masked = jnp.where(allowed, products[:, k - begin : k - begin + 128], -1.0)
                row_best = jnp.maximum(row_best, masked)
                best[q, :, lanes] = jnp.maximum(
                    best[q, :, lanes], jnp.max(masked.reshape(half // 8, 8, 128), axis=0)
                )
        side[p] = row_best

    def multiply(index, carry):
        products_of(packed(LEFTS, index), [packed(rights, index) for rights in RIGHTS], False)
        return carry

    actions = {
        "r": leave,
        "f": forward,
        "d": take_pair,
        "s": lambda: products_of(0, [0], True),
    }

    def segment(seg, carry):
        for k, (events, _, _) in enumerate(SEGMENTS):
            if events:

                @pl.when(seg == k)
                def _():
                    for name, *where in events:
                        actions[name](*where)

        lax.fori_loop(start_of(seg, 1), start_of(seg + 1, 1), multiply, carry)
        first, end = start_of(seg, 2) // BACK_GROUP, start_of(seg + 1, 2) // BACK_GROUP
        return lax.fori_loop(first, end, give_back, carry)

    lax.fori_loop(0, NSEG, segment, 0)

    for part in range(NPART):
        for slot in range(1, NSLOT):
            row_copy(part, slot).wait_send()
        for slot in sorted(PAIRED):
            pair_copy(slot, part).wait_send()
    for slot in sorted(PAIRED):
        id_pair_copy(slot).wait_send()
    for slot in range(1, NSLOT):
        id_copy(slot).wait_send()

    returned = [(slot, 0) for slot in range(1, NSLOT)] + [(slot, 1) for slot in sorted(PAIRED)]
    result = back_out[0, 0]
    for slot, which in returned:
        back_copy(slot, which, source[slot]).wait_recv()
        result = jnp.maximum(result, back[slot, which])
    o_ref[...] = result[:, :half]

    for slot, which in returned:
        back_copy(slot, which, source[slot]).wait_send()


def local(embeddings, cluster):
    half, width = embeddings.shape
    best = pl.pallas_call(
        kernel,
        out_shape=jax.ShapeDtypeStruct((1, half), jnp.float32),
        in_specs=[pl.BlockSpec(memory_space=pl.ANY)] * 2,
        out_specs=pl.BlockSpec(memory_space=pltpu.VMEM),
        scratch_shapes=[
            pltpu.VMEM((half, width), jnp.bfloat16),
            pltpu.VMEM((1, half), jnp.int32),
            pltpu.VMEM((NSLOT, half, width), jnp.bfloat16),
            pltpu.VMEM((NSLOT, half, width), jnp.bfloat16),
            pltpu.VMEM((2, NSLOT, 1, PAD), jnp.float32),
            pltpu.VMEM((NSLOT, half, 128), jnp.float32),
            pltpu.VMEM((NSLOT, 8, 2 * half), jnp.float32),
            pltpu.VMEM((NSLOT, 2, 1, PAD), jnp.float32),
            pltpu.VMEM((NSLOT, 2, 1, PAD), jnp.float32),
            pltpu.SemaphoreType.DMA((NPART + 1,)),
            pltpu.SemaphoreType.DMA((NSLOT, NPART)),
            pltpu.SemaphoreType.DMA((NSLOT, NPART)),
            pltpu.SemaphoreType.DMA((NSLOT, NPART)),
            pltpu.SemaphoreType.DMA((NSLOT, NPART)),
            pltpu.SemaphoreType.DMA((2, NSLOT)),
            pltpu.SemaphoreType.DMA((2, NSLOT)),
            pltpu.SemaphoreType.DMA((NSLOT, 2)),
            pltpu.SemaphoreType.DMA((NSLOT, 2)),
        ],
        compiler_params=pltpu.CompilerParams(
            collective_id=0, has_side_effects=True, vmem_limit_bytes=56 * 1024 * 1024
        ),
        cost_estimate=pl.CostEstimate(
            flops=4 * GROUP * len(LEFTS) * half * half * width, bytes_accessed=2 * half * width, transcendentals=half
        ),
    )(embeddings, cluster.reshape(1, half))
    return jnp.maximum(best.reshape(half), -1.0)


def solution(mesh):
    return jax.shard_map(
        local,
        mesh=mesh,
        in_specs=(P(("gx", "gy"), None), P(("gx", "gy"))),
        out_specs=P(("gx", "gy")),
        check_vma=False,
    )
```
